128 devices in a mesh: dom: 8 (over z, core), blk: 16 (over x, y).
Axes of the slice: x: 4, y: 4, z: 4, core: 2. Of those that a mesh axis runs over, the one named last changes fastest.
Arguments:
- node_owner: int32 [131072, 1], P(('dom', 'blk')), may hold values from 0 to 127; in each aligned block of 1024 rows (0 to 1023, 1024 to 2047, ...) at most 16 rows name the same one
- node_qrow: int32 [131072], P(('dom', 'blk')), may hold values from 0 to 1023
- node_rem: int32 [131072], P(('dom', 'blk')), may hold values from 0 to 1023
- quotient: bfloat16 [131072, 256], P(('dom', 'blk')), may hold values from -5 to 5
- remainder: bfloat16 [1024, 256], replicated, may hold values from -5 to 5
- edge_src: int32 [1024, 6144], P(('dom', 'blk')), may hold values from 0 to 16895, as said below
- edge_dst: int32 [1024, 6144], P(('dom', 'blk')), may hold values from 0 to 127
- block_count: int32 [1024], P(('dom', 'blk')), may hold values from 1024 to 6144, as said below
- w_self: bfloat16 [256, 256], replicated, may hold values from -0.375 to 0.375
- w_neigh: bfloat16 [256, 256], replicated, may hold values from -0.375 to 0.375
- bias: float32 [256], replicated, may hold values from -3 to 3
- cotangent: bfloat16 [131072, 256], P(('dom', 'blk')), may hold values from -6 to 6
Outputs:
- out: bfloat16 [131072, 256], P(('dom', 'blk'))
- d_quotient: float32 [131072, 256], P(('dom', 'blk'))
- d_remainder: float32 [1024, 256], replicated
- d_w_self: float32 [256, 256], replicated
- d_w_neigh: float32 [256, 256], replicated
- d_bias: float32 [256], replicated
The draws below stay inside these ranges and needn't reach their ends.
Inputs may be any that keep to these rules, and one draw needn't show every extreme that they name: `node_owner`: among the nodes of one device no device is named more than 16 times, and exactly 16 times in some devices' nodes. `edge_src`: indexes the source rows of the block's device as the steps state. `block_count`: some block has all 6144 slots live.
All inputs are finite; a program needn't handle non-finite values.
Results may differ from the reference program's by a relative error of at most 0.008.
Values may be sent and summed in bfloat16 or wider, within the bound.
A program may use at most 128 MiB of HBM per device.

```python
import math
import jax
import jax.numpy as jnp
import numpy as np
from jax import lax

D = 256
REM = 1024
QROWS_DEV = 1024
ROWS_BLK = 128
NB = 8
HALO = 256
EMAX = 6144
NODES_DEV = 1024
NODES = 131072
PART_NODES = 16384
BLOCKS = 1024
CAP = 16
N_DOM = 8
N_BLK = 16
DEVICES = 128


def draw_edge_src(key, part):
    key_inner, key_outer, key_pick = jax.random.split(key, 3)
    inner = jax.random.randint(key_inner, (BLOCKS, EMAX), 0, PART_NODES)
    outer = PART_NODES + jax.random.randint(key_outer, (BLOCKS, EMAX), 0, 2 * HALO)
    picker = jax.random.randint(key_pick, (BLOCKS, EMAX), 0, 8)
    return jnp.where(picker == 0, outer, inner).astype(jnp.int32)


def draw_edge_dst(key, part):
    key_first, key_second = jax.random.split(jax.random.fold_in(key, 7))
    first = jax.random.randint(key_first, (BLOCKS, EMAX), 0, ROWS_BLK)
    second = jax.random.randint(key_second, (BLOCKS, EMAX), 0, ROWS_BLK)
    return jnp.minimum(first, second).astype(jnp.int32)


def draw_block_count(key, part):
    key_heavy, key_large, key_small, key_spot = jax.random.split(jax.random.fold_in(key, 11), 4)
    heavy = jax.random.randint(key_heavy, (BLOCKS,), 0, 8) == 0
    large = jax.random.randint(key_large, (BLOCKS,), 2 * EMAX // 3, EMAX + 1)
    small = jax.random.randint(key_small, (BLOCKS,), EMAX // 6, EMAX // 2 + 1)
    counts = jnp.where(heavy, large, small)
    spot = jax.random.randint(key_spot, (), 0, BLOCKS)
    return counts.at[spot].set(EMAX).astype(jnp.int32)


def touch_ends(entries, own_key, smallest, largest):
    extent = entries.shape
    place = [jax.random.randint(jax.random.fold_in(own_key, axis), (), 0, extent[axis]) for axis in range(len(extent))]
    entries = entries.at[tuple(place)].set(smallest)
    longest = extent.index(max(extent))
    place[longest] = (place[longest] + 1) % extent[longest]
    return entries.at[tuple(place)].set(largest)


def level_of(key, shape, pieces, smallest, high):
    def one(position, shards_of):
        heights = jax.random.uniform(jax.random.fold_in(jax.random.fold_in(key, 6), position), (shards_of,), jnp.float32, smallest / len(pieces), high / len(pieces))
        return jnp.repeat(jnp.exp(heights), shape[position] // shards_of).reshape((-1,) + (1,) * (len(shape) - position - 1))

    factor_of = one(*pieces[0])
    for cut in pieces[1:]:
        factor_of = factor_of * one(*cut)
    return factor_of


def rank_bounds(count, lean):
    loads = [(1 << 20) // math.isqrt(grade ** lean) + 1 for grade in range(1, count + 1)]
    spread = 1 + sum(loads) // (1 << 30)
    return np.cumsum(np.array([max(1, weight // spread) for weight in loads]))


def skewed_ids(key, extent, number_of, lean):
    grid = rank_bounds(number_of, lean)
    pick = jax.random.randint(jax.random.fold_in(key, 1), extent, 0, int(grid[number_of - 1]))
    standing = jnp.searchsorted(jnp.asarray(grid, jnp.int32), pick, side="right")
    return jax.random.permutation(jax.random.fold_in(key, 2), number_of)[standing].astype(jnp.int32)


def deal_out(key, own, number, rows, amount, top, most, skew):
    sequence = jax.random.permutation(key, amount)
    crowded, common = shares(amount, rows * top, most, skew, True), shares(amount, rows * top, most, skew, False)
    places = jnp.arange(amount)

    def named(sizes, rotation):
        used = int((sizes > 0).sum())
        fixed = max(1, used // 4)
        shifted = fixed + (places - fixed + rotation * (used - fixed)) % max(1, amount - fixed)
        return jnp.zeros((amount,), jnp.int32).at[sequence[jnp.where(places < fixed, places, shifted)]].set(jnp.asarray(sizes, jnp.int32))

    sizes = jnp.where(number % 4 == 0, named(crowded, number // 4), named(common, number - number // 4 - 1))
    mixed = jax.random.permutation(jax.random.fold_in(own, 3), amount)
    giver, sink = mixed[0:amount // 2 * 2:2], mixed[1:amount // 2 * 2:2]
    margin = jnp.minimum(sizes[giver] - 1, most - sizes[sink]) // 2
    margin = jnp.where((giver == sequence[0]) | (sink == sequence[0]) | (sizes[sink] == 0), 0, jnp.maximum(margin, 0))
    shifted = jax.random.randint(jax.random.fold_in(own, 4), (amount // 2,), 0, 1 << 20) % (margin + 1)
    sizes = sizes.at[giver].add(-shifted).at[sink].add(shifted)
    members = jnp.searchsorted(jnp.cumsum(sizes), jnp.arange(rows * top), side="right").astype(jnp.int32)
    table = members.reshape(top, rows).T
    table = table[jax.random.permutation(jax.random.fold_in(own, 1), rows)]
    rotation = jax.random.randint(jax.random.fold_in(own, 2), (rows, 1), 0, top)
    return jnp.take_along_axis(table, (jnp.arange(top)[None, :] + rotation) % top, axis=1)


def shares(number_of, total, reach, skew, full):
    weights = [(1 << 20) // math.isqrt(standing ** skew) + 1 for standing in range(1, number_of + 1)]
    largest = reach if full else min(reach, max(-(-total // number_of), total * weights[0] // sum(weights)))
    least = 1 if total - largest >= number_of - 1 else 0
    given, rest = [largest] + [least] * (number_of - 1), total - largest - least * (number_of - 1)
    while rest > 0:
        candidates = [i for i in range(1, number_of) if given[i] < largest] or [i for i in range(1, number_of) if given[i] < reach]
        whole, remaining = sum([weights[i] for i in candidates]), rest
        for i in candidates:
            addition = min(reach - given[i], max(1, remaining * weights[i] // whole), rest)
            given[i] = given[i] + addition
            rest = rest - addition
    return np.array(given)


def gaussian(own_key, extent, scale, limit, pieces=(), kind=jnp.bfloat16):
    entries = jax.random.normal(own_key, extent, jnp.float32) * scale
    if len(pieces) > 0:
        entries = level_of(own_key, extent, pieces, -0.22, 0.18) * entries
    return jnp.clip(entries, min=-limit, max=limit).astype(kind)


def setup_inputs(seed: int = 0) -> dict:
    arg_keys = jax.random.split(jax.random.key(seed), 13)
    node_owner_keys = jax.random.split(jax.random.fold_in(arg_keys[0], 1), NODES // NODES_DEV)
    node_owner_turns = jax.random.permutation(jax.random.fold_in(arg_keys[0], 3), NODES // NODES_DEV)
    node_owner = jax.vmap(lambda own, number: deal_out(jax.random.fold_in(arg_keys[0], 2), own, number, NODES_DEV, DEVICES, 1, CAP, 2))(node_owner_keys, node_owner_turns).reshape((NODES, 1))
    node_qrow = touch_ends(jax.random.randint(arg_keys[1], (NODES,), 0, QROWS_DEV), jax.random.fold_in(arg_keys[1], 1), 0, QROWS_DEV - 1).astype(jnp.int32)
    node_rem = touch_ends(skewed_ids(arg_keys[2], (NODES,), REM, 2), jax.random.fold_in(arg_keys[2], 3), 0, REM - 1).astype(jnp.int32)
    quotient = gaussian(arg_keys[3], (QROWS_DEV * DEVICES, D), 1.0, 5.0, ((0, 128),))
    remainder = gaussian(arg_keys[4], (REM, D), 1.0, 5.0)
    edge_src = draw_edge_src(jax.random.fold_in(arg_keys[12], 71), 0)
    edge_dst = draw_edge_dst(jax.random.fold_in(arg_keys[12], 71), 0)
    block_count = draw_block_count(jax.random.fold_in(arg_keys[12], 71), 0)
    w_self = gaussian(arg_keys[8], (D, D), D ** -0.5, 0.375)
    w_neigh = gaussian(arg_keys[9], (D, D), D ** -0.5, 0.375)
    bias = gaussian(arg_keys[10], (D,), 0.5, 3.0, (), jnp.float32)
    cotangent = gaussian(arg_keys[11], (NODES, D), 1.0, 6.0, ((0, 128),))
    return dict(node_owner=node_owner, node_qrow=node_qrow, node_rem=node_rem, quotient=quotient, remainder=remainder, edge_src=edge_src, edge_dst=edge_dst, block_count=block_count, w_self=w_self, w_neigh=w_neigh, bias=bias, cotangent=cotangent)


def block_onehot(dst_row, filled):
    live_slot = jnp.arange(dst_row.shape[0], dtype=jnp.int32) < filled
    target = jnp.arange(ROWS_BLK, dtype=jnp.int32)
    return ((dst_row[None, :] == target[:, None]) & live_slot[None, :]).astype(jnp.bfloat16)

def wire_round(values):
    return lax.optimization_barrier(values.astype(jnp.bfloat16)).astype(jnp.float32)

def device_rows(by_device, device):
    dom_index = device // N_BLK
    blk_index = device % N_BLK
    lower_dom = (dom_index + N_DOM - 1) % N_DOM
    upper_dom = (dom_index + 1) % N_DOM
    own_part = lax.dynamic_index_in_dim(by_device, dom_index, 0, keepdims=False).reshape(PART_NODES, D)
    lower_part = lax.dynamic_index_in_dim(by_device, lower_dom, 0, keepdims=False)
    upper_part = lax.dynamic_index_in_dim(by_device, upper_dom, 0, keepdims=False)
    lower_dev = lax.dynamic_index_in_dim(lower_part, blk_index, 0, keepdims=False)
    upper_dev = lax.dynamic_index_in_dim(upper_part, blk_index, 0, keepdims=False)
    return jnp.concatenate([own_part, lower_dev[NODES_DEV - HALO:], upper_dev[:HALO]], axis=0)

def reference(node_owner, node_qrow, node_rem, quotient, remainder, edge_src, edge_dst, block_count, w_self, w_neigh, bias, cotangent):
    qrow_global = (node_owner[:, 0] * QROWS_DEV + node_qrow).astype(jnp.int32)
    quot_rows = quotient[qrow_global].astype(jnp.float32)
    remain_rows = remainder[node_rem].astype(jnp.float32)
    features = (quot_rows * remain_rows).astype(jnp.bfloat16)
    by_device = features.reshape(N_DOM, N_BLK, NODES_DEV, D)
    src_all = edge_src.reshape(DEVICES, NB, EMAX)
    dst_all = edge_dst.reshape(DEVICES, NB, EMAX)
    count_all = block_count.reshape(DEVICES, NB)
    device_ids = jnp.arange(DEVICES, dtype=jnp.int32)

    def device_forward(packed):
        device, src_dev, dst_dev, count_dev = packed
        source_rows = device_rows(by_device, device)

        def block_forward(inner):
            src_row, dst_row, filled = inner
            one_hot = block_onehot(dst_row, filled)
            summed = jnp.dot(one_hot, source_rows[src_row], preferred_element_type=jnp.float32)
            degree = lax.optimization_barrier(jnp.sum(one_hot.astype(jnp.float32), axis=1))
            return (summed, degree)
        return lax.map(block_forward, (src_dev, dst_dev, count_dev))
    agg_sum, degree = lax.map(device_forward, (device_ids, src_all, dst_all, count_all))
    agg_sum = agg_sum.reshape(NODES, D)
    divisor = jnp.maximum(degree.reshape(NODES), 1.0)
    neighbour = (agg_sum / divisor[:, None]).astype(jnp.bfloat16)
    preact = jnp.dot(features, w_self, preferred_element_type=jnp.float32) + jnp.dot(neighbour, w_neigh, preferred_element_type=jnp.float32) + bias
    sigma = jax.nn.sigmoid(preact)
    out = (preact * sigma).astype(jnp.bfloat16)
    dpre = (cotangent.astype(jnp.float32) * sigma * (1.0 + preact * (1.0 - sigma))).astype(jnp.bfloat16)
    weight_scale = 1.0 / math.sqrt(NODES)
    contract_rows = (((0,), (0,)), ((), ()))
    contract_cols = (((1,), (1,)), ((), ()))
    d_w_self = lax.dot_general(features, dpre, contract_rows, preferred_element_type=jnp.float32) * weight_scale
    d_w_neigh = lax.dot_general(neighbour, dpre, contract_rows, preferred_element_type=jnp.float32) * weight_scale
    d_bias = lax.optimization_barrier(jnp.sum(dpre.astype(jnp.float32), axis=0)) * weight_scale
    dagg = lax.dot_general(dpre, w_neigh, contract_cols, preferred_element_type=jnp.float32)
    dagg_scaled = (dagg / divisor[:, None]).astype(jnp.bfloat16)
    dx_self = lax.dot_general(dpre, w_self, contract_cols, preferred_element_type=jnp.float32)
    scaled_all = dagg_scaled.reshape(DEVICES, NB, ROWS_BLK, D)

    def device_backward(running, packed):
        device, src_dev, dst_dev, count_dev, scaled_dev = packed

        def block_back(accum, inner):
            src_row, dst_row, filled, scaled_blk = inner
            one_hot = block_onehot(dst_row, filled)
            edge_vals = lax.dot_general(one_hot, scaled_blk, contract_rows, preferred_element_type=jnp.float32)
            return (accum.at[src_row].add(edge_vals), None)
        start_grad = jnp.zeros((PART_NODES + 2 * HALO, D), jnp.float32)
        source_grad, unused = lax.scan(block_back, start_grad, (src_dev, dst_dev, count_dev, scaled_dev))
        source_grad = wire_round(source_grad)
        dom_index = device // N_BLK
        blk_index = device % N_BLK
        lower_dom = (dom_index + N_DOM - 1) % N_DOM
        upper_dom = (dom_index + 1) % N_DOM
        running = running.at[dom_index].add(source_grad[:PART_NODES].reshape(N_BLK, NODES_DEV, D))
        running = running.at[lower_dom, blk_index, NODES_DEV - HALO:].add(source_grad[PART_NODES:PART_NODES + HALO])
        running = running.at[upper_dom, blk_index, :HALO].add(source_grad[PART_NODES + HALO:])
        return (running, None)
    start_total = jnp.zeros((N_DOM, N_BLK, NODES_DEV, D), jnp.float32)
    edge_total, unused = lax.scan(device_backward, start_total, (device_ids, src_all, dst_all, count_all, scaled_all))
    grad_x = dx_self + edge_total.reshape(NODES, D)
    d_quotient = jax.ops.segment_sum(grad_x * remain_rows, qrow_global, num_segments=QROWS_DEV * DEVICES)
    d_remainder = jax.ops.segment_sum(grad_x * quot_rows, node_rem, num_segments=REM) * math.sqrt(REM / NODES)
    return (out, d_quotient, d_remainder, d_w_self, d_w_neigh, d_bias)
```

```python
import functools
import math

import jax
import jax.numpy as jnp
from jax import lax
from jax.experimental import pallas as pl
from jax.experimental.pallas import tpu as pltpu
from jax.sharding import PartitionSpec as P

ROWS_BLK = 128
HALO = 256
LANES = 128
BATCH = 16
AXES = ("dom", "blk")
ROWS = (((0,), (0,)), ((), ()))
COLS = (((1,), (1,)), ((), ()))


def prep_kernel(dump, src_ref, dst_ref, count_ref, fast_ref, slow_ref, flag_ref):
    blocks, slots = src_ref.shape
    src = src_ref[...]
    lane = lax.broadcasted_iota(jnp.int32, (blocks, slots), 1)
    cell = ((src >> 7) * ROWS_BLK + dst_ref[...]) * LANES + (src & 127)
    live = lane < count_ref[...]
    spare = dump * LANES
    cell = jnp.where(live, cell, spare)
    row = cell >> 7
    clash = jnp.zeros((blocks, slots), jnp.bool_)
    place = lane & (BATCH - 1)
    for s in range(1, BATCH):
        clash = clash | ((pltpu.roll(row, s, 1) == row) & (place >= s))
    clash = clash & live
    fast_ref[...] = jnp.where(clash, spare, cell)
    slow_ref[...] = jnp.where(clash, cell, spare)
    ones = jnp.where(clash, 1.0, 0.0)
    chunks = slots // LANES
    col = lax.broadcasted_iota(jnp.int32, (blocks, LANES), 1)
    flags = jnp.zeros((blocks, LANES), jnp.float32)
    for c in range(chunks):
        total = jnp.sum(ones[:, c * LANES : (c + 1) * LANES], axis=1, keepdims=True)
        flags = flags + jnp.where(col == c, total, 0.0)
    flag_ref[...] = flags.astype(jnp.int32)


def count_kernel(dump, count_ref, fast_ref, slow_ref, flag_ref, main_ref, halo_ref, deg_ref, cells):
    j = pl.program_id(0)
    his = dump // ROWS_BLK
    his_main = main_ref.shape[1] // LANES
    zero = jnp.zeros((ROWS_BLK, LANES), jnp.float32)

    @pl.when(j == 0)
    def _():
        def clear(i, carry):
            cells[pl.ds(pl.multiple_of(i * ROWS_BLK, ROWS_BLK), ROWS_BLK), :] = zero
            return carry

        lax.fori_loop(0, his, clear, 0)
        cells[pl.ds(dump, 8), :] = jnp.zeros((8, LANES), jnp.float32)

    count = count_ref[j]
    lanes = lax.broadcasted_iota(jnp.int32, (1, LANES), 1)

    def batch(t, carry):
        keys = [fast_ref[j, t * BATCH + i] for i in range(BATCH)]
        rows = [k >> 7 for k in keys]
        olds = [cells[pl.ds(r, 1), :] for r in rows]
        news = [old + jnp.where(lanes == (k & 127), 1.0, 0.0) for old, k in zip(olds, keys)]
        for r, new in zip(rows, news):
            cells[pl.ds(r, 1), :] = new
        return carry

    lax.fori_loop(0, (count + BATCH - 1) // BATCH, batch, 0)

    def chunk(c, carry):
        @pl.when(flag_ref[j, c] > 0)
        def _():
            def one(i, inner):
                k = slow_ref[j, c * LANES + i]

                @pl.when(k != dump * LANES)
                def _():
                    r = k >> 7
                    cells[pl.ds(r, 1), :] = cells[pl.ds(r, 1), :] + jnp.where(lanes == (k & 127), 1.0, 0.0)

                return inner

            lax.fori_loop(0, LANES, one, 0)

        return carry

    lax.fori_loop(0, (count + LANES - 1) // LANES, chunk, 0)

    def flush(ref, first):
        def step(h, total):
            at = pl.multiple_of((first + h) * ROWS_BLK, ROWS_BLK)
            value = cells[pl.ds(at, ROWS_BLK), :]
            ref[:, pl.ds(pl.multiple_of(h * LANES, LANES), LANES)] = value.astype(jnp.bfloat16)
            cells[pl.ds(at, ROWS_BLK), :] = zero
            return total + value

        return step

    total = lax.fori_loop(0, his_main, flush(main_ref, 0), zero, unroll=2)
    total = lax.fori_loop(0, his - his_main, flush(halo_ref, his_main), total, unroll=2)
    deg_ref[...] = jnp.sum(total, axis=1, keepdims=True)


def build_counts(edge_src, edge_dst, block_count, part_nodes):
    blocks, slots = edge_src.shape
    width = part_nodes + 2 * HALO
    dump = width // LANES * ROWS_BLK
    edge = jax.ShapeDtypeStruct((blocks, slots), jnp.int32)
    fast, slow, flags = pl.pallas_call(
        functools.partial(prep_kernel, dump),
        out_shape=(edge, edge, jax.ShapeDtypeStruct((blocks, LANES), jnp.int32)),
        compiler_params=pltpu.CompilerParams(vmem_limit_bytes=32 << 20),
        name="edge_prep",
    )(edge_src, edge_dst, block_count[:, None])
    smem = pl.BlockSpec(memory_space=pltpu.SMEM)
    nodes = blocks * ROWS_BLK
    return pl.pallas_call(
        functools.partial(count_kernel, dump),
        grid=(blocks,),
        out_shape=(
            jax.ShapeDtypeStruct((nodes, part_nodes), jnp.bfloat16),
            jax.ShapeDtypeStruct((nodes, 2 * HALO), jnp.bfloat16),
            jax.ShapeDtypeStruct((nodes, 1), jnp.float32),
        ),
        in_specs=[smem, smem, smem, smem],
        out_specs=(
            pl.BlockSpec((ROWS_BLK, part_nodes), lambda j: (j, 0)),
            pl.BlockSpec((ROWS_BLK, 2 * HALO), lambda j: (j, 0)),
            pl.BlockSpec((ROWS_BLK, 1), lambda j: (j, 0)),
        ),
        scratch_shapes=[pltpu.VMEM((dump + 8, LANES), jnp.float32)],
        compiler_params=pltpu.CompilerParams(vmem_limit_bytes=40 << 20),
        cost_estimate=pl.CostEstimate(flops=80_000_000_000, bytes_accessed=40_000_000, transcendentals=0),
        name="edge_counts",
    )(block_count, fast, slow, flags)


def shifted(block, axis, distance):
    devices = range(lax.axis_size(axis))
    route = [((i - distance) % len(devices), i) for i in devices]
    return lax.ppermute(block, axis, route)


def exchange(buffer):
    return lax.all_to_all(buffer, AXES, split_axis=0, concat_axis=0, tiled=True)


def hot(index, size):
    return (index[:, None] == jnp.arange(size, dtype=jnp.int32)[None, :]).astype(jnp.bfloat16)


def dot(a, b, dims=(((1,), (0,)), ((), ()))):
    return lax.dot_general(a, b, dims, preferred_element_type=jnp.float32)


def per_device(
    node_owner,
    node_qrow,
    node_rem,
    quotient,
    remainder,
    edge_src,
    edge_dst,
    block_count,
    w_self,
    w_neigh,
    bias,
    cotangent,
):
    nodes_dev = node_qrow.shape[0]
    feature_dim = quotient.shape[1]
    devices = lax.axis_size("dom") * lax.axis_size("blk")
    part_nodes = nodes_dev * lax.axis_size("blk")
    slot_cap = 2 * nodes_dev // devices
    slots = devices * slot_cap
    owner_dev = node_owner[:, 0]
    owner_hot = hot(owner_dev, devices)
    row_ids = jnp.arange(nodes_dev, dtype=jnp.int32)
    lower_mask = (row_ids[:, None] > row_ids[None, :]).astype(jnp.bfloat16)
    earlier = dot(lower_mask, owner_hot)
    slot_rank = jnp.sum(earlier * owner_hot.astype(jnp.float32), axis=1).astype(jnp.int32)
    slot_index = owner_dev * slot_cap + slot_rank
    rank_hot = hot(slot_rank, slot_cap)
    high = (node_qrow >> 5).astype(jnp.bfloat16)[:, None]
    low = (node_qrow & 31).astype(jnp.bfloat16)[:, None]
    asked = dot(owner_hot, jnp.concatenate([rank_hot * high, rank_hot * low], axis=1), ROWS)
    requests = (asked[:, :slot_cap] * 32.0 + asked[:, slot_cap:]).astype(jnp.int32)
    asked_rows = exchange(requests).reshape(slots)
    asked_hot = hot(asked_rows, quotient.shape[0])
    served = dot(asked_hot, quotient).astype(jnp.bfloat16)
    returned = exchange(served.reshape(devices, slot_cap, feature_dim)).reshape(slots, feature_dim)
    slot_hot = hot(slot_index, slots)
    quot_rows = dot(slot_hot, returned)
    rem_hot = hot(node_rem, remainder.shape[0])
    remain_rows = dot(rem_hot, remainder)
    features = (quot_rows * remain_rows).astype(jnp.bfloat16)
    part_gathered = lax.all_gather(features, "blk", axis=0, tiled=True)
    low_rows = shifted(features[nodes_dev - HALO :], "dom", 1)
    high_rows = shifted(features[:HALO], "dom", -1)
    halo_rows = jnp.concatenate([low_rows, high_rows], axis=0)

    counts, halo_counts, degree = build_counts(edge_src, edge_dst, block_count, part_nodes)
    divisor = jnp.maximum(degree, 1.0)
    agg_sum = dot(counts, part_gathered) + dot(halo_counts, halo_rows)
    neighbour = (agg_sum / divisor).astype(jnp.bfloat16)
    preact = dot(features, w_self) + dot(neighbour, w_neigh) + bias
    sigma = jax.nn.sigmoid(preact)
    out = (preact * sigma).astype(jnp.bfloat16)
    dpre = (cotangent.astype(jnp.float32) * sigma * (1.0 + preact * (1.0 - sigma))).astype(
        jnp.bfloat16
    )
    dagg_scaled = (dot(dpre, w_neigh, COLS) / divisor).astype(jnp.bfloat16)
    halo_grads = dot(halo_counts, dagg_scaled, ROWS).astype(jnp.bfloat16)
    source_grads = dot(counts, dagg_scaled, ROWS).astype(jnp.bfloat16)
    own_grads = lax.psum_scatter(source_grads, "blk", scatter_dimension=0, tiled=True)
    tail_grad = shifted(halo_grads[:HALO], "dom", -1)
    head_grad = shifted(halo_grads[HALO:], "dom", 1)
    local_self = dot(features, dpre, ROWS)
    local_neigh = dot(neighbour, dpre, ROWS)
    local_bias = jnp.sum(dpre.astype(jnp.float32), axis=0)
    dx_self = dot(dpre, w_self, COLS)
    edges = jnp.concatenate(
        [
            head_grad.astype(jnp.float32),
            jnp.zeros((nodes_dev - 2 * HALO, feature_dim), jnp.float32),
            tail_grad.astype(jnp.float32),
        ],
        axis=0,
    )
    grad_x = dx_self + own_grads.astype(jnp.float32) + edges
    outgoing = dot(slot_hot, (grad_x * remain_rows).astype(jnp.bfloat16), ROWS).astype(jnp.bfloat16)
    local_remain = dot(rem_hot, (grad_x * quot_rows).astype(jnp.bfloat16), ROWS)

    def per_owner(value):
        return value.astype(jnp.bfloat16).reshape(devices, -1, feature_dim)

    bias_high = local_bias.astype(jnp.bfloat16)
    bias_low = (local_bias - bias_high.astype(jnp.float32)).astype(jnp.bfloat16)
    bias_pair = jnp.concatenate([bias_high.reshape(devices, -1), bias_low.reshape(devices, -1)], axis=1)
    bias_each = feature_dim // devices
    bias_rows = jnp.pad(bias_pair, ((0, 0), (0, feature_dim - 2 * bias_each)))[:, None, :]
    incoming = exchange(
        jnp.concatenate(
            [
                per_owner(outgoing),
                per_owner(local_remain),
                per_owner(local_self),
                per_owner(local_neigh),
                bias_rows,
            ],
            axis=1,
        )
    )
    returned_grads = incoming[:, :slot_cap].reshape(slots, feature_dim)
    d_quotient = dot(asked_hot, returned_grads, ROWS)
    summed = jnp.sum(incoming[:, slot_cap:].astype(jnp.float32), axis=0)
    gathered = lax.all_gather(summed, AXES, axis=0, tiled=False)
    rem_each = remainder.shape[0] // devices
    w_each = feature_dim // devices
    nodes_total = nodes_dev * devices
    weight_scale = 1.0 / math.sqrt(nodes_total)
    remain_scale = math.sqrt(remainder.shape[0] / nodes_total)
    d_remainder = gathered[:, :rem_each].reshape(-1, feature_dim) * remain_scale
    d_self = gathered[:, rem_each : rem_each + w_each].reshape(-1, feature_dim) * weight_scale
    d_neigh = gathered[:, rem_each + w_each : rem_each + 2 * w_each].reshape(-1, feature_dim) * weight_scale
    last = gathered[:, rem_each + 2 * w_each]
    d_bias = (last[:, :bias_each] + last[:, bias_each : 2 * bias_each]).reshape(-1) * weight_scale
    return (out, d_quotient, d_remainder, d_self, d_neigh, d_bias)


def solution(mesh):
    both = P(AXES)
    rows = P(AXES, None)
    return jax.shard_map(
        per_device,
        mesh=mesh,
        in_specs=(rows, both, both, rows, P(), rows, rows, both, P(), P(), P(), rows),
        out_specs=(rows, rows, P(), P(), P(), P()),
        check_vma=False,
    )
```

```python
import functools
import math

import jax
import jax.numpy as jnp
from jax import lax
from jax.experimental import pallas as pl
from jax.experimental.pallas import tpu as pltpu
from jax.sharding import PartitionSpec as P

ROWS_BLK = 128
HALO = 256
LANES = 128
BATCH = 16
AXES = ("dom", "blk")
MESH = pl.DeviceIdType.MESH
ROWS = (((0,), (0,)), ((), ()))
COLS = (((1,), (1,)), ((), ()))


def prep_kernel(dump, src_ref, dst_ref, count_ref, fast_ref, slow_ref, flag_ref):
    blocks, slots = src_ref.shape
    src = src_ref[...]
    lane = lax.broadcasted_iota(jnp.int32, (blocks, slots), 1)
    cell = ((src >> 7) * ROWS_BLK + dst_ref[...]) * LANES + (src & 127)
    live = lane < count_ref[...]
    spare = dump * LANES
    cell = jnp.where(live, cell, spare)
    row = cell >> 7
    clash = jnp.zeros((blocks, slots), jnp.bool_)
    place = lane & (BATCH - 1)
    for s in range(1, BATCH):
        clash = clash | ((pltpu.roll(row, s, 1) == row) & (place >= s))
    clash = clash & live
    fast_ref[...] = jnp.where(clash, spare, cell)
    slow_ref[...] = jnp.where(clash, cell, spare)
    ones = jnp.where(clash, 1.0, 0.0).astype(jnp.bfloat16)
    chunks = slots // LANES
    col = lax.broadcasted_iota(jnp.int32, (blocks, LANES), 1)
    into = lax.broadcasted_iota(jnp.int32, (LANES, LANES), 0) // BATCH
    group = (into == lax.broadcasted_iota(jnp.int32, (LANES, LANES), 1)).astype(jnp.bfloat16)
    found = jnp.zeros((blocks, LANES), jnp.int32)
    number = jnp.zeros((blocks, 1), jnp.int32)
    for c in range(chunks):
        hits = jnp.dot(ones[:, c * LANES : (c + 1) * LANES], group, preferred_element_type=jnp.float32)
        bits = jnp.sum(jnp.where(hits > 0.5, (1 << (col & 7)).astype(jnp.float32), 0.0), axis=1, keepdims=True)
        bits = bits.astype(jnp.int32)
        some = bits > 0
        found = found + jnp.where((col == number) & some, c * 256 + bits, 0)
        number = number + some.astype(jnp.int32)
    flag_ref[...] = jnp.where(col == LANES - 1, number, found)


def count_kernel(dump, count_ref, fast_ref, slow_ref, flag_ref, main_ref, halo_ref, deg_ref, cells):
    j = pl.program_id(0)
    his = dump // ROWS_BLK
    his_main = main_ref.shape[1] // LANES
    zero = jnp.zeros((ROWS_BLK, LANES), jnp.float32)

    @pl.when(j == 0)
    def _():
        def clear(i, carry):
            cells[pl.ds(pl.multiple_of(i * ROWS_BLK, ROWS_BLK), ROWS_BLK), :] = zero
            return carry

        lax.fori_loop(0, his, clear, 0)
        cells[pl.ds(dump, 8), :] = jnp.zeros((8, LANES), jnp.float32)

    count = count_ref[j]
    lanes = lax.broadcasted_iota(jnp.int32, (1, LANES), 1)

    def batch(t, carry):
        keys = [fast_ref[0, 0, t * BATCH + i] for i in range(BATCH)]
        rows = [k >> 7 for k in keys]
        olds = [cells[pl.ds(r, 1), :] for r in rows]
        news = [old + jnp.where(lanes == (k & 127), 1.0, 0.0) for old, k in zip(olds, keys)]
        for r, new in zip(rows, news):
            cells[pl.ds(r, 1), :] = new
        return carry

    lax.fori_loop(0, (count + BATCH - 1) // BATCH, batch, 0)

    def chunk(c, carry):
        entry = flag_ref[0, 0, c]
        first = (entry >> 8) * LANES

        def some(g, inner):
            @pl.when(((entry >> g) & 1) != 0)
            def _():
                for i in range(BATCH):
                    k = slow_ref[0, 0, first + g * BATCH + i]
                    r = k >> 7
                    cells[pl.ds(r, 1), :] = cells[pl.ds(r, 1), :] + jnp.where(lanes == (k & 127), 1.0, 0.0)

            return inner

        lax.fori_loop(0, LANES // BATCH, some, 0)
        return carry

    lax.fori_loop(0, flag_ref[0, 0, LANES - 1], chunk, 0)

    def flush(ref, first):
        def step(h, total):
            at = pl.multiple_of((first + h) * ROWS_BLK, ROWS_BLK)
            value = cells[pl.ds(at, ROWS_BLK), :]
            ref[:, pl.ds(pl.multiple_of(h * LANES, LANES), LANES)] = value.astype(jnp.bfloat16)
            cells[pl.ds(at, ROWS_BLK), :] = zero
            return total + value

        return step

    total = lax.fori_loop(0, his_main, flush(main_ref, 0), zero, unroll=2)
    total = lax.fori_loop(0, his - his_main, flush(halo_ref, his_main), total, unroll=2)
    deg_ref[...] = jnp.sum(total, axis=1, keepdims=True)


def build_counts(edge_src, edge_dst, block_count, part_nodes):
    blocks, slots = edge_src.shape
    width = part_nodes + 2 * HALO
    dump = width // LANES * ROWS_BLK
    edge = jax.ShapeDtypeStruct((blocks, slots), jnp.int32)
    fast, slow, flags = pl.pallas_call(
        functools.partial(prep_kernel, dump),
        out_shape=(edge, edge, jax.ShapeDtypeStruct((blocks, LANES), jnp.int32)),
        compiler_params=pltpu.CompilerParams(vmem_limit_bytes=32 << 20),
        name="edge_prep",
    )(edge_src, edge_dst, block_count[:, None])
    nodes = blocks * ROWS_BLK
    return pl.pallas_call(
        functools.partial(count_kernel, dump),
        grid=(blocks,),
        out_shape=(
            jax.ShapeDtypeStruct((nodes, part_nodes), jnp.bfloat16),
            jax.ShapeDtypeStruct((nodes, 2 * HALO), jnp.bfloat16),
            jax.ShapeDtypeStruct((nodes, 1), jnp.float32),
        ),
        in_specs=[
            pl.BlockSpec(memory_space=pltpu.SMEM),
            pl.BlockSpec((1, 1, slots), lambda j: (j, 0, 0), memory_space=pltpu.SMEM),
            pl.BlockSpec((1, 1, slots), lambda j: (j, 0, 0), memory_space=pltpu.SMEM),
            pl.BlockSpec((1, 1, LANES), lambda j: (j, 0, 0), memory_space=pltpu.SMEM),
        ],
        out_specs=(
            pl.BlockSpec((ROWS_BLK, part_nodes), lambda j: (j, 0)),
            pl.BlockSpec((ROWS_BLK, 2 * HALO), lambda j: (j, 0)),
            pl.BlockSpec((ROWS_BLK, 1), lambda j: (j, 0)),
        ),
        scratch_shapes=[pltpu.VMEM((dump + 8, LANES), jnp.float32)],
        compiler_params=pltpu.CompilerParams(vmem_limit_bytes=40 << 20),
        cost_estimate=pl.CostEstimate(flops=80_000_000_000, bytes_accessed=40_000_000, transcendentals=0),
        name="edge_counts",
    )(block_count, fast[:, None], slow[:, None], flags[:, None])


def ring_place():
    blk = lax.axis_size("blk")
    return lax.axis_index("dom") * blk + lax.axis_index("blk")


def meet_all(devices):
    barrier = pltpu.get_barrier_semaphore()
    me = ring_place()

    def greet(k, carry):
        other = lax.rem(me + k, devices)
        pl.semaphore_signal(barrier, inc=1, device_id=coords(other), device_id_type=MESH)
        return carry

    lax.fori_loop(1, devices, greet, 0)
    pl.semaphore_wait(barrier, devices - 1)


def coords(device):
    blk = lax.axis_size("blk")
    return (device // blk, lax.rem(device, blk))


def send(src, dst, device, send_sem, recv_sem):
    pltpu.make_async_remote_copy(
        src_ref=src,
        dst_ref=dst,
        send_sem=send_sem,
        recv_sem=recv_sem,
        device_id=coords(device),
        device_id_type=MESH,
    ).start()


def drain(ref, sem):
    pltpu.make_async_copy(ref, ref, sem).wait()


def fetch_kernel(devices, ids_ref, table_ref, rows_ref, asked_ref, ids_in, served, rows_in, sems):
    slot_cap = served.shape[0] // devices
    slots = served.shape[0]
    me = ring_place()
    meet_all(devices)

    def ask(k, carry):
        other = lax.rem(me + k, devices)
        send(ids_ref.at[other], ids_in.at[me], other, sems.at[0], sems.at[1])
        return carry

    lax.fori_loop(1, devices, ask, 0)
    own = pltpu.make_async_copy(ids_ref.at[me], ids_in.at[me], sems.at[2])
    own.start()
    own.wait()
    drain(ids_in.at[pl.ds(0, devices - 1)], sems.at[1])
    ids = ids_in[:, 0, :].astype(jnp.bfloat16)
    step = 16
    part = step * slot_cap
    lanes = ids.shape[1]
    lane = lax.broadcasted_iota(jnp.int32, (part, lanes), 1)
    slot = lax.broadcasted_iota(jnp.int32, (part, lanes), 0)
    rank = lax.rem(slot, slot_cap)
    weight = jnp.where(lane == rank, 32.0, 0.0) + jnp.where(lane == rank + slot_cap, 1.0, 0.0)
    column = lax.broadcasted_iota(jnp.int32, (part, table_ref.shape[0]), 1)

    def serve(c, carry):
        turn = lax.rem(c + me // step, devices // step)
        pick = (lane - turn * step == slot // slot_cap).astype(jnp.bfloat16)
        spread = jnp.dot(pick, ids, preferred_element_type=jnp.float32)
        asked = jnp.sum(spread * weight, axis=1, keepdims=True).astype(jnp.int32)
        at = pl.multiple_of(turn * part, part)
        asked_ref[pl.ds(at, part), :] = asked
        pick_row = (column == asked).astype(jnp.bfloat16)
        served[pl.ds(at, part), :] = jnp.dot(
            pick_row, table_ref[...], preferred_element_type=jnp.float32
        ).astype(jnp.bfloat16)

        def back(i, inner):
            other = turn * step + lax.rem(me + i, step)

            @pl.when(other != me)
            def _():
                send(
                    served.at[pl.ds(pl.multiple_of(other * slot_cap, slot_cap), slot_cap)],
                    rows_in.at[pl.ds(pl.multiple_of(me * slot_cap, slot_cap), slot_cap)],
                    other,
                    sems.at[3],
                    sems.at[4],
                )

            return inner

        lax.fori_loop(0, step, back, 0)
        return carry

    lax.fori_loop(0, devices // step, serve, 0)
    mine = pl.ds(pl.multiple_of(me * slot_cap, slot_cap), slot_cap)
    own_rows = pltpu.make_async_copy(served.at[mine], rows_in.at[mine], sems.at[2])
    own_rows.start()
    own_rows.wait()
    drain(rows_in.at[pl.ds(0, slots - slot_cap)], sems.at[4])
    rows_ref[...] = rows_in[...]
    drain(ids_in.at[pl.ds(0, devices - 1)], sems.at[0])
    drain(rows_in.at[pl.ds(0, slots - slot_cap)], sems.at[3])


def fetch_rows(ids, quotient, slot_cap):
    devices, _, lanes = ids.shape
    slots = devices * slot_cap
    width = quotient.shape[1]
    vmem = pl.BlockSpec(memory_space=pltpu.VMEM)
    return pl.pallas_call(
        functools.partial(fetch_kernel, devices),
        out_shape=(
            jax.ShapeDtypeStruct((slots, width), jnp.bfloat16),
            jax.ShapeDtypeStruct((slots, 1), jnp.int32),
        ),
        in_specs=[vmem, vmem],
        out_specs=(vmem, vmem),
        scratch_shapes=[
            pltpu.VMEM((devices, 1, lanes), jnp.float32),
            pltpu.VMEM((slots, width), jnp.bfloat16),
            pltpu.VMEM((slots, width), jnp.bfloat16),
            pltpu.SemaphoreType.DMA((5,)),
        ],
        compiler_params=pltpu.CompilerParams(
            collective_id=1, has_side_effects=True, vmem_limit_bytes=32 << 20
        ),
        name="fetch_rows",
    )(ids, quotient)


def spread_kernel(devices, scale, grads_ref, rem_ref, back_ref, total_ref, grads_in, rem_in, piece, whole, sems):
    slot_cap = grads_ref.shape[0] // devices
    slots = grads_ref.shape[0]
    tall = piece.shape[0]
    wide = piece.shape[1]
    across = rem_ref.shape[1] // wide
    me = ring_place()
    meet_all(devices)

    def tile(device):
        top = pl.multiple_of(device // across * tall, tall)
        return (pl.ds(top, tall), pl.ds(pl.multiple_of(lax.rem(device, across) * wide, wide), wide))

    def slot(device):
        return pl.ds(pl.multiple_of(device * slot_cap, slot_cap), slot_cap)

    def send_rem(k, carry):
        other = lax.rem(me + k, devices)
        send(rem_ref.at[tile(other)], rem_in.at[me], other, sems.at[0], sems.at[1])
        return carry

    def send_grads(k, carry):
        other = lax.rem(me + k, devices)
        send(grads_ref.at[slot(other)], grads_in.at[slot(me)], other, sems.at[2], sems.at[3])
        return carry

    def send_total(k, carry):
        other = lax.rem(me + k, devices)
        send(piece, whole.at[me], other, sems.at[4], sems.at[5])
        return carry

    lax.fori_loop(1, devices, send_rem, 0)
    lax.fori_loop(1, devices, send_grads, 0)
    own_rem = pltpu.make_async_copy(rem_ref.at[tile(me)], rem_in.at[me], sems.at[6])
    own_rem.start()
    own_rem.wait()
    own_grads = pltpu.make_async_copy(grads_ref.at[slot(me)], grads_in.at[slot(me)], sems.at[6])
    own_grads.start()
    own_grads.wait()
    drain(rem_in.at[pl.ds(0, devices - 1)], sems.at[1])
    piece[...] = jnp.sum(rem_in[...].astype(jnp.float32), axis=0) * scale
    lax.fori_loop(1, devices, send_total, 0)
    own_total = pltpu.make_async_copy(piece, whole.at[me], sems.at[6])
    own_total.start()
    own_total.wait()
    drain(grads_in.at[pl.ds(0, slots - slot_cap)], sems.at[3])
    back_ref[...] = grads_in[...]

    drain(whole.at[pl.ds(0, devices - 1)], sems.at[5])

    def lay(k, carry):
        for part in range(across):
            total_ref[pl.ds(pl.multiple_of(k * tall, tall), tall), part * wide : (part + 1) * wide] = whole[
                k * across + part
            ]
        return carry

    lax.fori_loop(0, devices // across, lay, 0)
    drain(rem_in.at[pl.ds(0, devices - 1)], sems.at[0])
    drain(grads_in.at[pl.ds(0, slots - slot_cap)], sems.at[2])
    drain(whole.at[pl.ds(0, devices - 1)], sems.at[4])


def spread_grads(outgoing, local_remain, devices, scale):
    rows, width = local_remain.shape
    wide = LANES
    tall = rows * width // devices // wide
    vmem = pl.BlockSpec(memory_space=pltpu.VMEM)
    return pl.pallas_call(
        functools.partial(spread_kernel, devices, scale),
        out_shape=(
            jax.ShapeDtypeStruct(outgoing.shape, jnp.bfloat16),
            jax.ShapeDtypeStruct((rows, width), jnp.float32),
        ),
        in_specs=[vmem, vmem],
        out_specs=(vmem, vmem),
        scratch_shapes=[
            pltpu.VMEM(outgoing.shape, jnp.bfloat16),
            pltpu.VMEM((devices, tall, wide), jnp.bfloat16),
            pltpu.VMEM((tall, wide), jnp.float32),
            pltpu.VMEM((devices, tall, wide), jnp.float32),
            pltpu.SemaphoreType.DMA((7,)),
        ],
        compiler_params=pltpu.CompilerParams(
            collective_id=2, has_side_effects=True, vmem_limit_bytes=32 << 20
        ),
        name="spread_grads",
    )(outgoing, local_remain)


def shifted(block, axis, distance):
    devices = range(lax.axis_size(axis))
    route = [((i - distance) % len(devices), i) for i in devices]
    return lax.ppermute(block, axis, route)


def hot(index, size):
    return (index[:, None] == jnp.arange(size, dtype=jnp.int32)[None, :]).astype(jnp.bfloat16)


def dot(a, b, dims=(((1,), (0,)), ((), ()))):
    return lax.dot_general(a, b, dims, preferred_element_type=jnp.float32)


def per_device(
    node_owner,
    node_qrow,
    node_rem,
    quotient,
    remainder,
    edge_src,
    edge_dst,
    block_count,
    w_self,
    w_neigh,
    bias,
    cotangent,
):
    nodes_dev = node_qrow.shape[0]
    feature_dim = quotient.shape[1]
    devices = lax.axis_size("dom") * lax.axis_size("blk")
    part_nodes = nodes_dev * lax.axis_size("blk")
    slot_cap = 2 * nodes_dev // devices
    slots = devices * slot_cap
    owner_dev = node_owner[:, 0]
    owner_hot = hot(owner_dev, devices)
    row_ids = jnp.arange(nodes_dev, dtype=jnp.int32)
    lower_mask = (row_ids[:, None] > row_ids[None, :]).astype(jnp.bfloat16)
    earlier = dot(lower_mask, owner_hot)
    slot_rank = jnp.sum(earlier * owner_hot.astype(jnp.float32), axis=1).astype(jnp.int32)
    slot_index = owner_dev * slot_cap + slot_rank
    rank_hot = hot(slot_rank, slot_cap)
    high = (node_qrow >> 5).astype(jnp.bfloat16)[:, None]
    low = (node_qrow & 31).astype(jnp.bfloat16)[:, None]
    asked = dot(owner_hot, jnp.concatenate([rank_hot * high, rank_hot * low], axis=1), ROWS)
    ids = jnp.pad(asked, ((0, 0), (0, LANES - 2 * slot_cap)))[:, None, :]
    returned, asked_rows = fetch_rows(ids, quotient, slot_cap)
    asked_hot = hot(asked_rows[:, 0], quotient.shape[0])
    slot_hot = hot(slot_index, slots)
    quot_rows = dot(slot_hot, returned)
    rem_hot = hot(node_rem, remainder.shape[0])
    remain_rows = dot(rem_hot, remainder)
    features = (quot_rows * remain_rows).astype(jnp.bfloat16)
    part_gathered = lax.all_gather(features, "blk", axis=0, tiled=True)
    low_rows = shifted(features[nodes_dev - HALO :], "dom", 1)
    high_rows = shifted(features[:HALO], "dom", -1)
    halo_rows = jnp.concatenate([low_rows, high_rows], axis=0)

    counts, halo_counts, degree = build_counts(edge_src, edge_dst, block_count, part_nodes)
    divisor = jnp.maximum(degree, 1.0)
    agg_sum = dot(counts, part_gathered) + dot(halo_counts, halo_rows)
    neighbour = (agg_sum / divisor).astype(jnp.bfloat16)
    preact = dot(features, w_self) + dot(neighbour, w_neigh) + bias
    sigma = jax.nn.sigmoid(preact)
    out = (preact * sigma).astype(jnp.bfloat16)
    dpre = (cotangent.astype(jnp.float32) * sigma * (1.0 + preact * (1.0 - sigma))).astype(
        jnp.bfloat16
    )
    dagg_scaled = (dot(dpre, w_neigh, COLS) / divisor).astype(jnp.bfloat16)
    halo_grads = dot(halo_counts, dagg_scaled, ROWS).astype(jnp.bfloat16)
    source_grads = dot(counts, dagg_scaled, ROWS).astype(jnp.bfloat16)
    own_grads = lax.psum_scatter(source_grads, "blk", scatter_dimension=0, tiled=True)
    tail_grad = shifted(halo_grads[:HALO], "dom", -1)
    head_grad = shifted(halo_grads[HALO:], "dom", 1)
    local_self = dot(features, dpre, ROWS)
    local_neigh = dot(neighbour, dpre, ROWS)
    local_bias = jnp.sum(dpre.astype(jnp.float32), axis=0)
    bias_rows = jnp.pad(local_bias[None, :], ((0, 7), (0, 0)))
    summed = lax.psum(jnp.concatenate([local_self, local_neigh, bias_rows], axis=0), AXES)
    dx_self = dot(dpre, w_self, COLS)
    edges = jnp.concatenate(
        [
            head_grad.astype(jnp.float32),
            jnp.zeros((nodes_dev - 2 * HALO, feature_dim), jnp.float32),
            tail_grad.astype(jnp.float32),
        ],
        axis=0,
    )
    grad_x = dx_self + own_grads.astype(jnp.float32) + edges
    outgoing = dot(slot_hot, (grad_x * remain_rows).astype(jnp.bfloat16), ROWS).astype(jnp.bfloat16)
    local_remain = dot(rem_hot, (grad_x * quot_rows).astype(jnp.bfloat16), ROWS)

    nodes_total = nodes_dev * devices
    weight_scale = 1.0 / math.sqrt(nodes_total)
    remain_scale = math.sqrt(remainder.shape[0] / nodes_total)
    returned_grads, d_remainder = spread_grads(
        outgoing, local_remain.astype(jnp.bfloat16), devices, remain_scale
    )
    d_quotient = dot(asked_hot, returned_grads, ROWS)
    d_self = summed[:feature_dim] * weight_scale
    d_neigh = summed[feature_dim : 2 * feature_dim] * weight_scale
    d_bias = summed[2 * feature_dim] * weight_scale
    return (out, d_quotient, d_remainder, d_self, d_neigh, d_bias)


def solution(mesh):
    both = P(AXES)
    rows = P(AXES, None)
    return jax.shard_map(
        per_device,
        mesh=mesh,
        in_specs=(rows, both, both, rows, P(), rows, rows, both, P(), P(), P(), rows),
        out_specs=(rows, rows, P(), P(), P(), P()),
        check_vma=False,
    )
```

```python
import functools
import math

import jax
import jax.numpy as jnp
from jax import lax
from jax.experimental import pallas as pl
from jax.experimental.pallas import tpu as pltpu
from jax.sharding import PartitionSpec as P

ROWS_BLK = 128
HALO = 256
LANES = 128
BATCH = 16
AXES = ("dom", "blk")
MESH = pl.DeviceIdType.MESH
ROWS = (((0,), (0,)), ((), ()))
COLS = (((1,), (1,)), ((), ()))


def prep_kernel(dump, src_ref, dst_ref, count_ref, fast_ref, slow_ref, flag_ref):
    blocks, slots = src_ref.shape
    src = src_ref[...]
    lane = lax.broadcasted_iota(jnp.int32, (blocks, slots), 1)
    cell = ((src >> 7) * ROWS_BLK + dst_ref[...]) * LANES + (src & 127)
    live = lane < count_ref[...]
    spare = dump * LANES
    cell = jnp.where(live, cell, spare)
    row = cell >> 7
    clash = jnp.zeros((blocks, slots), jnp.bool_)
    place = lane & (BATCH - 1)
    for s in range(1, BATCH):
        clash = clash | ((pltpu.roll(row, s, 1) == row) & (place >= s))
    clash = clash & live
    fast_ref[...] = jnp.where(clash, spare, cell)
    slow_ref[...] = jnp.where(clash, cell, spare)
    ones = jnp.where(clash, 1.0, 0.0).astype(jnp.bfloat16)
    chunks = slots // LANES
    col = lax.broadcasted_iota(jnp.int32, (blocks, LANES), 1)
    into = lax.broadcasted_iota(jnp.int32, (LANES, LANES), 0) // BATCH
    group = (into == lax.broadcasted_iota(jnp.int32, (LANES, LANES), 1)).astype(jnp.bfloat16)
    found = jnp.zeros((blocks, LANES), jnp.int32)
    number = jnp.zeros((blocks, 1), jnp.int32)
    for c in range(chunks):
        hits = jnp.dot(ones[:, c * LANES : (c + 1) * LANES], group, preferred_element_type=jnp.float32)
        bits = jnp.sum(jnp.where(hits > 0.5, (1 << (col & 7)).astype(jnp.float32), 0.0), axis=1, keepdims=True)
        bits = bits.astype(jnp.int32)
        some = bits > 0
        found = found + jnp.where((col == number) & some, c * 256 + bits, 0)
        number = number + some.astype(jnp.int32)
    flag_ref[...] = jnp.where(col == LANES - 1, number, found)


def count_kernel(dump, count_ref, fast_ref, slow_ref, flag_ref, main_ref, halo_ref, deg_ref, cells):
    j = pl.program_id(0)
    his = dump // ROWS_BLK
    his_main = main_ref.shape[1] // LANES
    zero = jnp.zeros((ROWS_BLK, LANES), jnp.float32)

    @pl.when(j == 0)
    def _():
        def clear(i, carry):
            cells[pl.ds(pl.multiple_of(i * ROWS_BLK, ROWS_BLK), ROWS_BLK), :] = zero
            return carry

        lax.fori_loop(0, his, clear, 0)
        cells[pl.ds(dump, 8), :] = jnp.zeros((8, LANES), jnp.float32)

    count = count_ref[j]
    lanes = lax.broadcasted_iota(jnp.int32, (1, LANES), 1)

    def batch(t, carry):
        keys = [fast_ref[0, 0, t * BATCH + i] for i in range(BATCH)]
        rows = [k >> 7 for k in keys]
        olds = [cells[pl.ds(r, 1), :] for r in rows]
        news = [old + jnp.where(lanes == (k & 127), 1.0, 0.0) for old, k in zip(olds, keys)]
        for r, new in zip(rows, news):
            cells[pl.ds(r, 1), :] = new
        return carry

    lax.fori_loop(0, (count + BATCH - 1) // BATCH, batch, 0)

    def chunk(c, carry):
        entry = flag_ref[0, 0, c]
        first = (entry >> 8) * LANES

        def some(g, inner):
            @pl.when(((entry >> g) & 1) != 0)
            def _():
                for i in range(BATCH):
                    k = slow_ref[0, 0, first + g * BATCH + i]
                    r = k >> 7
                    cells[pl.ds(r, 1), :] = cells[pl.ds(r, 1), :] + jnp.where(lanes == (k & 127), 1.0, 0.0)

            return inner

        lax.fori_loop(0, LANES // BATCH, some, 0)
        return carry

    lax.fori_loop(0, flag_ref[0, 0, LANES - 1], chunk, 0)

    def flush(ref, first):
        def step(h, total):
            at = pl.multiple_of((first + h) * ROWS_BLK, ROWS_BLK)
            value = cells[pl.ds(at, ROWS_BLK), :]
            ref[:, pl.ds(pl.multiple_of(h * LANES, LANES), LANES)] = value.astype(jnp.bfloat16)
            cells[pl.ds(at, ROWS_BLK), :] = zero
            return total + value

        return step

    total = lax.fori_loop(0, his_main, flush(main_ref, 0), zero, unroll=2)
    total = lax.fori_loop(0, his - his_main, flush(halo_ref, his_main), total, unroll=2)
    deg_ref[...] = jnp.sum(total, axis=1, keepdims=True)


def build_counts(edge_src, edge_dst, block_count, part_nodes):
    blocks, slots = edge_src.shape
    width = part_nodes + 2 * HALO
    dump = width // LANES * ROWS_BLK
    edge = jax.ShapeDtypeStruct((blocks, slots), jnp.int32)
    fast, slow, flags = pl.pallas_call(
        functools.partial(prep_kernel, dump),
        out_shape=(edge, edge, jax.ShapeDtypeStruct((blocks, LANES), jnp.int32)),
        compiler_params=pltpu.CompilerParams(vmem_limit_bytes=32 << 20),
        name="edge_prep",
    )(edge_src, edge_dst, block_count[:, None])
    nodes = blocks * ROWS_BLK
    return pl.pallas_call(
        functools.partial(count_kernel, dump),
        grid=(blocks,),
        out_shape=(
            jax.ShapeDtypeStruct((nodes, part_nodes), jnp.bfloat16),
            jax.ShapeDtypeStruct((nodes, 2 * HALO), jnp.bfloat16),
            jax.ShapeDtypeStruct((nodes, 1), jnp.float32),
        ),
        in_specs=[
            pl.BlockSpec(memory_space=pltpu.SMEM),
            pl.BlockSpec((1, 1, slots), lambda j: (j, 0, 0), memory_space=pltpu.SMEM),
            pl.BlockSpec((1, 1, slots), lambda j: (j, 0, 0), memory_space=pltpu.SMEM),
            pl.BlockSpec((1, 1, LANES), lambda j: (j, 0, 0), memory_space=pltpu.SMEM),
        ],
        out_specs=(
            pl.BlockSpec((ROWS_BLK, part_nodes), lambda j: (j, 0)),
            pl.BlockSpec((ROWS_BLK, 2 * HALO), lambda j: (j, 0)),
            pl.BlockSpec((ROWS_BLK, 1), lambda j: (j, 0)),
        ),
        scratch_shapes=[pltpu.VMEM((dump + 8, LANES), jnp.float32)],
        compiler_params=pltpu.CompilerParams(vmem_limit_bytes=40 << 20),
        cost_estimate=pl.CostEstimate(flops=80_000_000_000, bytes_accessed=40_000_000, transcendentals=0),
        name="edge_counts",
    )(block_count, fast[:, None], slow[:, None], flags[:, None])


def ring_place():
    blk = lax.axis_size("blk")
    return lax.axis_index("dom") * blk + lax.axis_index("blk")


def meet_all(devices):
    barrier = pltpu.get_barrier_semaphore()
    me = ring_place()

    def greet(k, carry):
        other = lax.rem(me + k, devices)
        pl.semaphore_signal(barrier, inc=1, device_id=coords(other), device_id_type=MESH)
        return carry

    lax.fori_loop(1, devices, greet, 0)
    pl.semaphore_wait(barrier, devices - 1)


def coords(device):
    blk = lax.axis_size("blk")
    return (device // blk, lax.rem(device, blk))


def send(src, dst, device, send_sem, recv_sem):
    pltpu.make_async_remote_copy(
        src_ref=src,
        dst_ref=dst,
        send_sem=send_sem,
        recv_sem=recv_sem,
        device_id=coords(device),
        device_id_type=MESH,
    ).start()


def drain(ref, sem):
    pltpu.make_async_copy(ref, ref, sem).wait()


def fetch_kernel(devices, ids_ref, table_ref, rows_ref, asked_ref, ids_in, served, rows_in, sems):
    slot_cap = served.shape[0] // devices
    slots = served.shape[0]
    me = ring_place()
    meet_all(devices)

    def ask(k, carry):
        other = lax.rem(me + k, devices)
        send(ids_ref.at[other], ids_in.at[me], other, sems.at[0], sems.at[1])
        return carry

    lax.fori_loop(1, devices, ask, 0)
    own = pltpu.make_async_copy(ids_ref.at[me], ids_in.at[me], sems.at[2])
    own.start()
    own.wait()
    drain(ids_in.at[pl.ds(0, devices - 1)], sems.at[1])
    ids = ids_in[:, 0, :].astype(jnp.bfloat16)
    step = 16
    part = step * slot_cap
    lanes = ids.shape[1]
    lane = lax.broadcasted_iota(jnp.int32, (part, lanes), 1)
    slot = lax.broadcasted_iota(jnp.int32, (part, lanes), 0)
    rank = lax.rem(slot, slot_cap)
    weight = jnp.where(lane == rank, 32.0, 0.0) + jnp.where(lane == rank + slot_cap, 1.0, 0.0)
    column = lax.broadcasted_iota(jnp.int32, (part, table_ref.shape[0]), 1)

    def serve(c, carry):
        turn = lax.rem(c + me // step, devices // step)
        pick = (lane - turn * step == slot // slot_cap).astype(jnp.bfloat16)
        spread = jnp.dot(pick, ids, preferred_element_type=jnp.float32)
        asked = jnp.sum(spread * weight, axis=1, keepdims=True).astype(jnp.int32)
        at = pl.multiple_of(turn * part, part)
        asked_ref[pl.ds(at, part), :] = asked
        pick_row = (column == asked).astype(jnp.bfloat16)
        served[pl.ds(at, part), :] = jnp.dot(
            pick_row, table_ref[...], preferred_element_type=jnp.float32
        ).astype(jnp.bfloat16)

        def back(i, inner):
            other = turn * step + lax.rem(me + i, step)

            @pl.when(other != me)
            def _():
                send(
                    served.at[pl.ds(pl.multiple_of(other * slot_cap, slot_cap), slot_cap)],
                    rows_in.at[pl.ds(pl.multiple_of(me * slot_cap, slot_cap), slot_cap)],
                    other,
                    sems.at[3],
                    sems.at[4],
                )

            return inner

        lax.fori_loop(0, step, back, 0)
        return carry

    lax.fori_loop(0, devices // step, serve, 0)
    mine = pl.ds(pl.multiple_of(me * slot_cap, slot_cap), slot_cap)
    own_rows = pltpu.make_async_copy(served.at[mine], rows_in.at[mine], sems.at[2])
    own_rows.start()
    own_rows.wait()
    drain(rows_in.at[pl.ds(0, slots - slot_cap)], sems.at[4])
    rows_ref[...] = rows_in[...]
    drain(ids_in.at[pl.ds(0, devices - 1)], sems.at[0])
    drain(rows_in.at[pl.ds(0, slots - slot_cap)], sems.at[3])


def fetch_rows(ids, quotient, slot_cap):
    devices, _, lanes = ids.shape
    slots = devices * slot_cap
    width = quotient.shape[1]
    vmem = pl.BlockSpec(memory_space=pltpu.VMEM)
    return pl.pallas_call(
        functools.partial(fetch_kernel, devices),
        out_shape=(
            jax.ShapeDtypeStruct((slots, width), jnp.bfloat16),
            jax.ShapeDtypeStruct((slots, 1), jnp.int32),
        ),
        in_specs=[vmem, vmem],
        out_specs=(vmem, vmem),
        scratch_shapes=[
            pltpu.VMEM((devices, 1, lanes), jnp.float32),
            pltpu.VMEM((slots, width), jnp.bfloat16),
            pltpu.VMEM((slots, width), jnp.bfloat16),
            pltpu.SemaphoreType.DMA((5,)),
        ],
        compiler_params=pltpu.CompilerParams(
            collective_id=1, has_side_effects=True, vmem_limit_bytes=32 << 20
        ),
        name="fetch_rows",
    )(ids, quotient)


def spread_kernel(
    devices, rem_scale, scale, grads_ref, rem_ref, sums_ref, back_ref, total_ref, weight_ref, bias_ref,
    grads_in, rem_in, sums_in, piece, whole, sems
):
    slot_cap = grads_ref.shape[0] // devices
    slots = grads_ref.shape[0]
    tall, wide = rem_in.shape[1:]
    across = rem_ref.shape[1] // wide
    peers = sums_in.shape[0]
    high = sums_ref.shape[0] - 8
    me = ring_place()
    dom = lax.axis_index("dom")
    blk = lax.axis_index("blk")
    meet_all(devices)

    def tile(device):
        top = pl.multiple_of(device // across * tall, tall)
        return (pl.ds(top, tall), pl.ds(pl.multiple_of(lax.rem(device, across) * wide, wide), wide))

    def slot(device):
        return pl.ds(pl.multiple_of(device * slot_cap, slot_cap), slot_cap)

    def share(peer):
        top = pl.multiple_of(peer // across * 8, 8)
        return (pl.ds(top, 8), pl.ds(pl.multiple_of(lax.rem(peer, across) * wide, wide), wide))

    def send_rem(k, carry):
        other = lax.rem(me + k, devices)
        send(rem_ref.at[tile(other)], rem_in.at[me], other, sems.at[0], sems.at[1])
        return carry

    def send_sums(k, carry):
        other = lax.rem(blk + k, peers)
        to = dom * peers + other
        send(sums_ref.at[share(other)], sums_in.at[blk, pl.ds(0, 8), :], to, sems.at[7], sems.at[8])
        send(sums_ref.at[pl.ds(high, 8), pl.ds(0, wide)], sums_in.at[blk, pl.ds(8, 8), :], to, sems.at[7], sems.at[8])
        return carry

    def send_grads(k, carry):
        other = lax.rem(me + k, devices)
        send(grads_ref.at[slot(other)], grads_in.at[slot(me)], other, sems.at[2], sems.at[3])
        return carry

    def send_total(k, carry):
        other = lax.rem(me + k, devices)
        send(piece, whole.at[me], other, sems.at[4], sems.at[5])
        return carry

    def keep(src, dst):
        copy = pltpu.make_async_copy(src, dst, sems.at[6])
        copy.start()
        copy.wait()

    lax.fori_loop(1, peers, send_sums, 0)
    lax.fori_loop(1, devices, send_rem, 0)
    lax.fori_loop(1, devices, send_grads, 0)
    keep(rem_ref.at[tile(me)], rem_in.at[me])
    keep(grads_ref.at[slot(me)], grads_in.at[slot(me)])
    keep(sums_ref.at[share(blk)], sums_in.at[blk, pl.ds(0, 8), :])
    keep(sums_ref.at[pl.ds(high, 8), pl.ds(0, wide)], sums_in.at[blk, pl.ds(8, 8), :])
    drain(sums_in.at[pl.ds(0, peers - 1)], sems.at[8])
    drain(rem_in.at[pl.ds(0, devices - 1)], sems.at[1])
    piece[:tall] = (jnp.sum(rem_in[...].astype(jnp.float32), axis=0) * rem_scale).astype(jnp.bfloat16)
    piece[tall:] = (jnp.sum(sums_in[...], axis=0) * scale).astype(jnp.bfloat16)
    lax.fori_loop(1, devices, send_total, 0)
    keep(piece, whole.at[me])
    drain(grads_in.at[pl.ds(0, slots - slot_cap)], sems.at[3])
    back_ref[...] = grads_in[...]
    drain(whole.at[pl.ds(0, devices - 1)], sems.at[5])

    def lay(k, carry):
        for part in range(across):
            got = whole[k * across + part].astype(jnp.float32)
            lanes = slice(part * wide, (part + 1) * wide)
            total_ref[pl.ds(pl.multiple_of(k * tall, tall), tall), lanes] = got[:tall]
            weight_ref[pl.ds(pl.multiple_of(k * 8, 8), 8), lanes] = got[tall : tall + 8]
        return carry

    lax.fori_loop(0, devices // across, lay, 0)
    for d in range(devices // peers):
        bias_ref[d : d + 1, :] = whole[d * peers, tall + 8 : tall + 16, :].astype(jnp.float32)[0:1]
    drain(rem_in.at[pl.ds(0, devices - 1)], sems.at[0])
    drain(grads_in.at[pl.ds(0, slots - slot_cap)], sems.at[2])
    drain(whole.at[pl.ds(0, devices - 1)], sems.at[4])
    drain(sums_in.at[pl.ds(0, peers - 1)], sems.at[7])


def spread_grads(outgoing, local_remain, sums, devices, peers, rem_scale, scale):
    rows, width = local_remain.shape
    wide = LANES
    tall = rows * width // devices // wide
    doms = devices // peers
    vmem = pl.BlockSpec(memory_space=pltpu.VMEM)
    return pl.pallas_call(
        functools.partial(spread_kernel, devices, rem_scale, scale),
        out_shape=(
            jax.ShapeDtypeStruct(outgoing.shape, jnp.bfloat16),
            jax.ShapeDtypeStruct((rows, width), jnp.float32),
            jax.ShapeDtypeStruct((doms * (sums.shape[0] - 8), width), jnp.float32),
            jax.ShapeDtypeStruct((doms, wide), jnp.float32),
        ),
        in_specs=[vmem, vmem, vmem],
        out_specs=(vmem, vmem, vmem, vmem),
        scratch_shapes=[
            pltpu.VMEM(outgoing.shape, jnp.bfloat16),
            pltpu.VMEM((devices, tall, wide), jnp.bfloat16),
            pltpu.VMEM((peers, 16, wide), jnp.float32),
            pltpu.VMEM((tall + 16, wide), jnp.bfloat16),
            pltpu.VMEM((devices, tall + 16, wide), jnp.bfloat16),
            pltpu.SemaphoreType.DMA((9,)),
        ],
        compiler_params=pltpu.CompilerParams(
            collective_id=2, has_side_effects=True, vmem_limit_bytes=32 << 20
        ),
        name="spread_grads",
    )(outgoing, local_remain, sums)


def reduce_kernel(
    counts_ref, grad_ref, weights_ref, out_ref, sums_ref, load, part, mid, fin, half_sum, mid2, fin2, sems_load, s_out, s_mid, s_fin, t_out, t_mid, t_fin, weights_in, w_out, w_in
):
    side = 4
    nodes = grad_ref.shape[1]
    feats = grad_ref.shape[0] // 2
    span = nodes // 2
    dom = lax.axis_index("dom")
    blk = lax.axis_index("blk")
    x, y = blk // side, lax.rem(blk, side)

    def at(dx, dy):
        return lax.rem(x + dx, side) * side + lax.rem(y + dy, side)

    def device(half, first, second):
        dx, dy = (first, second) if half == 0 else (second, first)
        return (dom, at(dx, dy))

    barrier = pltpu.get_barrier_semaphore()
    for dx, dy in ((1, 0), (3, 0), (0, 1), (0, 3)):
        pl.semaphore_signal(barrier, inc=1, device_id=(dom, at(dx, dy)), device_id_type=MESH)
    doms = weights_ref.shape[0]
    for k in range(1, doms):
        pl.semaphore_signal(barrier, inc=1, device_id=(lax.rem(dom + k, doms), blk), device_id_type=MESH)

    order = [(2, 2), (2, 1), (1, 2), (2, 3), (3, 2), (2, 0), (0, 2), (1, 1), (3, 3), (1, 3), (3, 1)]
    order += [(1, 0), (0, 1), (3, 0), (0, 3), (0, 0)]
    depth = load.shape[0]

    def fetch(i):
        dx, dy = order[i]
        columns = pl.ds(pl.multiple_of(at(dx, dy) * nodes, nodes), nodes)
        return pltpu.make_async_copy(counts_ref.at[:, columns], load.at[i % depth], sems_load.at[i % depth])

    for i in range(depth - 1):
        fetch(i).start()
    pl.semaphore_wait(barrier, 4 + doms - 1)

    def to_dom(k):
        other = lax.rem(dom + k, doms)
        return pltpu.make_async_remote_copy(
            src_ref=weights_ref.at[other],
            dst_ref=weights_in.at[k],
            send_sem=w_out.at[k],
            recv_sem=w_in.at[k],
            device_id=(other, blk),
            device_id_type=MESH,
        )

    for k in range(1, doms):
        to_dom(k).start()

    def remote(src, dst, half, first, second, send_sem, recv_sem):
        return pltpu.make_async_remote_copy(
            src_ref=src,
            dst_ref=dst,
            send_sem=send_sem,
            recv_sem=recv_sem,
            device_id=device(half, first, second),
            device_id_type=MESH,
        )

    def along(unit):
        return unit % 2 == 0

    def to_mid(half, unit):
        return remote(
            part.at[half, 2, unit], mid.at[half, unit], half, 1 if along(unit) else 3, 0,
            s_out.at[half, 0, unit], s_mid.at[half, unit],
        )

    def to_fin(half, first, unit):
        way = 0 if first == 1 else 1
        return remote(
            part.at[half, first, unit], fin.at[half, way, unit], half, first, 0,
            s_out.at[half, 1 + way, unit], s_fin.at[half, way, unit],
        )

    def relays(first, unit):
        return along(unit) == (first == 1)

    tile = 256
    waiting = []
    for i, (dx, dy) in enumerate(order):
        if i + depth - 1 < len(order):
            fetch(i + depth - 1).start()
        fetch(i).wait()

        def columns(n, carry, slot=i % depth, dx=dx, dy=dy):
            cut = pl.ds(pl.multiple_of(n * tile, tile), tile)
            value = jnp.dot(grad_ref[...], load[slot, :, cut], preferred_element_type=jnp.float32)
            part[0, dx, dy, :, cut] = value[:feats].astype(jnp.bfloat16)
            part[1, dy, dx, :, cut] = value[feats:].astype(jnp.bfloat16)
            return carry

        lax.fori_loop(0, nodes // tile, columns, 0)
        for half, first, unit in ((0, dx, dy), (1, dy, dx)):
            if first == 2:
                to_mid(half, unit).start()
            elif first != 0:
                if relays(first, unit):
                    waiting.append((half, first, unit))
                else:
                    to_fin(half, first, unit).start()
    waiting.sort(key=lambda item: (2, 1, 3, 0).index(item[2]))
    for half, first, unit in waiting:
        to_mid(half, unit).wait_recv()
        mine = part[half, first, unit].astype(jnp.float32)
        part[half, first, unit] = (mine + mid[half, unit].astype(jnp.float32)).astype(jnp.bfloat16)
        to_fin(half, first, unit).start()

    def cut(piece):
        return pl.ds(piece * span, span)

    def to_mid2(half, piece):
        return remote(
            half_sum.at[half, 1, :, cut(piece)], mid2.at[half, piece], half, 0, 1 if piece == 0 else 3,
            t_out.at[half, 0, piece], t_mid.at[half, piece],
        )

    def to_fin2(half, second, piece):
        way = 0 if second == 1 else 1
        return remote(
            half_sum.at[half, 0 if second == 1 else 2, :, cut(piece)], fin2.at[half, way, piece], half, 0, second,
            t_out.at[half, 1 + way, piece], t_fin.at[half, way, piece],
        )

    def summed(half, unit):
        to_fin(half, 1, unit).wait_recv()
        to_fin(half, 3, unit).wait_recv()
        total = part[half, 0, unit].astype(jnp.float32) + fin[half, 0, unit].astype(jnp.float32)
        return total + fin[half, 1, unit].astype(jnp.float32)

    for half in range(2):
        half_sum[half, 1] = summed(half, 2).astype(jnp.bfloat16)
        to_mid2(half, 0).start()
        to_mid2(half, 1).start()
    for second in (1, 3):
        direct, relayed = (1, 0) if second == 1 else (0, 1)
        for half in range(2):
            half_sum[half, second - 1] = summed(half, second).astype(jnp.bfloat16)
            to_fin2(half, second, direct).start()
    for second in (1, 3):
        direct, relayed = (1, 0) if second == 1 else (0, 1)
        for half in range(2):
            to_mid2(half, relayed).wait_recv()
            mine = half_sum[half, second - 1, :, cut(relayed)].astype(jnp.float32)
            both = mine + mid2[half, relayed].astype(jnp.float32)
            half_sum[half, second - 1, :, cut(relayed)] = both.astype(jnp.bfloat16)
            to_fin2(half, second, relayed).start()
    for half in range(2):
        rows = pl.ds(half * feats, feats)
        out_ref[rows, :] = summed(half, 0)
    for half in range(2):
        rows = pl.ds(half * feats, feats)
        for piece in range(2):
            to_fin2(half, 1, piece).wait_recv()
            to_fin2(half, 3, piece).wait_recv()
            total = out_ref[rows, cut(piece)] + fin2[half, 0, piece].astype(jnp.float32)
            out_ref[rows, cut(piece)] = total + fin2[half, 1, piece].astype(jnp.float32)
    sums = weights_ref[dom]
    for k in range(1, doms):
        to_dom(k).wait_recv()
        sums = sums + weights_in[k]
    sums_ref[...] = sums
    for k in range(1, doms):
        to_dom(k).wait_send()
    for half in range(2):
        for unit in range(side):
            to_mid(half, unit).wait_send()
            to_fin(half, 1, unit).wait_send()
            to_fin(half, 3, unit).wait_send()
        for piece in range(2):
            to_mid2(half, piece).wait_send()
            to_fin2(half, 1, piece).wait_send()
            to_fin2(half, 3, piece).wait_send()


def reduce_sources(counts, grad, weights):
    feats, nodes = grad.shape
    half = feats // 2
    kind = jnp.bfloat16
    dma = pltpu.SemaphoreType.DMA
    vmem = pl.BlockSpec(memory_space=pltpu.VMEM)
    return pl.pallas_call(
        reduce_kernel,
        out_shape=(
            jax.ShapeDtypeStruct((feats, nodes), jnp.float32),
            jax.ShapeDtypeStruct(weights.shape[1:], jnp.float32),
        ),
        in_specs=[pl.BlockSpec(memory_space=pl.ANY), vmem, vmem],
        out_specs=(vmem, vmem),
        scratch_shapes=[
            pltpu.VMEM((3, nodes, nodes), kind),
            pltpu.VMEM((2, 4, 4, half, nodes), kind),
            pltpu.VMEM((2, 4, half, nodes), kind),
            pltpu.VMEM((2, 2, 4, half, nodes), kind),
            pltpu.VMEM((2, 3, half, nodes), kind),
            pltpu.VMEM((2, 2, half, nodes // 2), kind),
            pltpu.VMEM((2, 2, 2, half, nodes // 2), kind),
            dma((3,)),
            dma((2, 3, 4)),
            dma((2, 4)),
            dma((2, 2, 4)),
            dma((2, 3, 2)),
            dma((2, 2)),
            dma((2, 2, 2)),
            pltpu.VMEM(weights.shape, jnp.float32),
            dma((weights.shape[0],)),
            dma((weights.shape[0],)),
        ],
        compiler_params=pltpu.CompilerParams(
            collective_id=3, has_side_effects=True, vmem_limit_bytes=44 << 20
        ),
        name="reduce_sources",
    )(counts, grad, weights)


def shifted(block, axis, distance):
    devices = range(lax.axis_size(axis))
    route = [((i - distance) % len(devices), i) for i in devices]
    return lax.ppermute(block, axis, route)


def hot(index, size):
    return (index[:, None] == jnp.arange(size, dtype=jnp.int32)[None, :]).astype(jnp.bfloat16)


def dot(a, b, dims=(((1,), (0,)), ((), ()))):
    return lax.dot_general(a, b, dims, preferred_element_type=jnp.float32)


def per_device(
    node_owner,
    node_qrow,
    node_rem,
    quotient,
    remainder,
    edge_src,
    edge_dst,
    block_count,
    w_self,
    w_neigh,
    bias,
    cotangent,
):
    nodes_dev = node_qrow.shape[0]
    feature_dim = quotient.shape[1]
    devices = lax.axis_size("dom") * lax.axis_size("blk")
    part_nodes = nodes_dev * lax.axis_size("blk")
    slot_cap = 2 * nodes_dev // devices
    slots = devices * slot_cap
    owner_dev = node_owner[:, 0]
    owner_hot = hot(owner_dev, devices)
    row_ids = jnp.arange(nodes_dev, dtype=jnp.int32)
    lower_mask = (row_ids[:, None] > row_ids[None, :]).astype(jnp.bfloat16)
    earlier = dot(lower_mask, owner_hot)
    slot_rank = jnp.sum(earlier * owner_hot.astype(jnp.float32), axis=1).astype(jnp.int32)
    slot_index = owner_dev * slot_cap + slot_rank
    rank_hot = hot(slot_rank, slot_cap)
    high = (node_qrow >> 5).astype(jnp.bfloat16)[:, None]
    low = (node_qrow & 31).astype(jnp.bfloat16)[:, None]
    asked = dot(owner_hot, jnp.concatenate([rank_hot * high, rank_hot * low], axis=1), ROWS)
    ids = jnp.pad(asked, ((0, 0), (0, LANES - 2 * slot_cap)))[:, None, :]
    returned, asked_rows = fetch_rows(ids, quotient, slot_cap)
    asked_hot = hot(asked_rows[:, 0], quotient.shape[0])
    slot_hot = hot(slot_index, slots)
    quot_rows = dot(slot_hot, returned)
    rem_hot = hot(node_rem, remainder.shape[0])
    remain_rows = dot(rem_hot, remainder)
    features = (quot_rows * remain_rows).astype(jnp.bfloat16)
    part_gathered = lax.all_gather(features, "blk", axis=0, tiled=True)
    low_rows = shifted(features[nodes_dev - HALO :], "dom", 1)
    high_rows = shifted(features[:HALO], "dom", -1)
    halo_rows = jnp.concatenate([low_rows, high_rows], axis=0)

    counts, halo_counts, degree = build_counts(edge_src, edge_dst, block_count, part_nodes)
    divisor = jnp.maximum(degree, 1.0)
    agg_sum = dot(counts, part_gathered) + dot(halo_counts, halo_rows)
    neighbour = (agg_sum / divisor).astype(jnp.bfloat16)
    preact = dot(features, w_self) + dot(neighbour, w_neigh) + bias
    sigma = jax.nn.sigmoid(preact)
    out = (preact * sigma).astype(jnp.bfloat16)
    dpre = (cotangent.astype(jnp.float32) * sigma * (1.0 + preact * (1.0 - sigma))).astype(
        jnp.bfloat16
    )
    dagg_scaled = (dot(dpre, w_neigh, COLS) / divisor).astype(jnp.bfloat16)
    halo_grads = dot(halo_counts, dagg_scaled, ROWS).astype(jnp.bfloat16)
    tail_grad = shifted(halo_grads[:HALO], "dom", -1)
    head_grad = shifted(halo_grads[HALO:], "dom", 1)
    local_self = dot(features, dpre, ROWS)
    local_neigh = dot(neighbour, dpre, ROWS)
    local_bias = jnp.sum(dpre.astype(jnp.float32), axis=0)
    doms = lax.axis_size("dom")
    bias_rows = jnp.pad(local_bias.reshape(doms, 1, -1), ((0, 0), (0, 7), (0, feature_dim - feature_dim // doms)))
    weights = jnp.concatenate([local_self, local_neigh], axis=0).reshape(doms, -1, feature_dim)
    weights = jnp.concatenate([weights, bias_rows], axis=1)
    own_grads, weight_sums = reduce_sources(counts, dagg_scaled.T, weights)
    own_grads = own_grads.T
    dx_self = dot(dpre, w_self, COLS)
    edges = jnp.concatenate(
        [
            head_grad.astype(jnp.float32),
            jnp.zeros((nodes_dev - 2 * HALO, feature_dim), jnp.float32),
            tail_grad.astype(jnp.float32),
        ],
        axis=0,
    )
    grad_x = dx_self + own_grads + edges
    outgoing = dot(slot_hot, (grad_x * remain_rows).astype(jnp.bfloat16), ROWS).astype(jnp.bfloat16)
    local_remain = dot(rem_hot, (grad_x * quot_rows).astype(jnp.bfloat16), ROWS)

    nodes_total = nodes_dev * devices
    weight_scale = 1.0 / math.sqrt(nodes_total)
    remain_scale = math.sqrt(remainder.shape[0] / nodes_total)
    returned_grads, d_remainder, d_weights, d_bias = spread_grads(
        outgoing,
        local_remain.astype(jnp.bfloat16),
        weight_sums,
        devices,
        lax.axis_size("blk"),
        remain_scale,
        weight_scale,
    )
    d_quotient = dot(asked_hot, returned_grads, ROWS)
    d_self, d_neigh = d_weights[:feature_dim], d_weights[feature_dim:]
    d_bias = d_bias[:, : feature_dim // doms].reshape(-1)
    return (out, d_quotient, d_remainder, d_self, d_neigh, d_bias)


def solution(mesh):
    both = P(AXES)
    rows = P(AXES, None)
    return jax.shard_map(
        per_device,
        mesh=mesh,
        in_specs=(rows, both, both, rows, P(), rows, rows, both, P(), P(), P(), rows),
        out_specs=(rows, rows, P(), P(), P(), P()),
        check_vma=False,
    )
```

```python
import functools
import math

import jax
import jax.numpy as jnp
from jax import lax
from jax.experimental import pallas as pl
from jax.experimental.pallas import tpu as pltpu
from jax.sharding import PartitionSpec as P

ROWS_BLK = 128
HALO = 256
LANES = 128
BATCH = 8
AXES = ("dom", "blk")
MESH = pl.DeviceIdType.MESH
ROWS = (((0,), (0,)), ((), ()))
COLS = (((1,), (1,)), ((), ()))


def prep_kernel(dump, src_ref, dst_ref, count_ref, fast_ref, slow_ref, flag_ref):
    blocks, slots = src_ref.shape
    src = src_ref[...]
    lane = lax.broadcasted_iota(jnp.int32, (blocks, slots), 1)
    cell = ((src >> 7) * ROWS_BLK + dst_ref[...]) * LANES + (src & 127)
    live = lane < count_ref[...]
    spare = dump * LANES
    cell = jnp.where(live, cell, spare)
    row = cell >> 7
    clash = jnp.zeros((blocks, slots), jnp.bool_)
    place = lane & (BATCH - 1)
    for s in range(1, BATCH):
        clash = clash | ((pltpu.roll(row, s, 1) == row) & (place >= s))
    clash = clash & live
    fast_ref[...] = jnp.where(clash, spare, cell)
    slow_ref[...] = jnp.where(clash, cell, spare)
    ones = jnp.where(clash, 1.0, 0.0).astype(jnp.bfloat16)
    chunks = slots // LANES
    col = lax.broadcasted_iota(jnp.int32, (blocks, LANES), 1)
    into = lax.broadcasted_iota(jnp.int32, (LANES, LANES), 0) // BATCH
    group = (into == lax.broadcasted_iota(jnp.int32, (LANES, LANES), 1)).astype(jnp.bfloat16)
    found = jnp.zeros((blocks, LANES), jnp.int32)
    number = jnp.zeros((blocks, 1), jnp.int32)
    for c in range(chunks):
        hits = jnp.dot(ones[:, c * LANES : (c + 1) * LANES], group, preferred_element_type=jnp.float32)
        bits = jnp.sum(jnp.where(hits > 0.5, (1 << (col & (LANES // BATCH - 1))).astype(jnp.float32), 0.0), axis=1, keepdims=True)
        bits = bits.astype(jnp.int32)
        some = bits > 0
        found = found + jnp.where((col == number) & some, c * 65536 + bits, 0)
        number = number + some.astype(jnp.int32)
    flag_ref[...] = jnp.where(col == LANES - 1, number, found)


def count_kernel(dump, count_ref, fast_ref, slow_ref, flag_ref, main_ref, halo_ref, deg_ref, *cells):
    j = pl.program_id(0)
    blocks = pl.num_programs(0) - 1
    his = dump // ROWS_BLK
    his_main = main_ref.shape[1] // LANES
    zero = jnp.zeros((ROWS_BLK, LANES), jnp.float32)
    lanes = lax.broadcasted_iota(jnp.int32, (1, LANES), 1)

    @pl.when(j == 0)
    def _():
        def clear(i, carry):
            for ref in cells[:2]:
                ref[pl.ds(pl.multiple_of(i * ROWS_BLK, ROWS_BLK), ROWS_BLK), :] = zero
            return carry

        lax.fori_loop(0, his, clear, 0)
        for ref in cells:
            ref[pl.ds(dump, 8), :] = jnp.zeros((8, LANES), jnp.float32)

    count = jnp.where(j < blocks, count_ref[jnp.minimum(j, blocks - 1)], 0)
    pairs = (count + 2 * BATCH - 1) // (2 * BATCH)

    def add_batch(ref, first):
        keys = [fast_ref[0, 0, first + i] for i in range(BATCH)]
        rows = [k >> 7 for k in keys]
        olds = [ref[pl.ds(r, 1), :] for r in rows]
        news = [old + jnp.where(lanes == (k & 127), 1.0, 0.0) for old, k in zip(olds, keys)]
        for r, new in zip(rows, news):
            ref[pl.ds(r, 1), :] = new

    def turn(fill, leave):
        def add_pair(t, carry):
            add_batch(fill[0], t * 2 * BATCH)
            add_batch(fill[1], t * 2 * BATCH + BATCH)
            return carry

        def flush(ref, first):
            def step(h, total):
                at = pl.multiple_of((first + h) * ROWS_BLK, ROWS_BLK)
                rows = pl.ds(at, ROWS_BLK)
                value = leave[0][rows, :] + leave[1][rows, :]
                ref[:, pl.ds(pl.multiple_of(h * LANES, LANES), LANES)] = value.astype(jnp.bfloat16)
                leave[0][rows, :] = zero
                leave[1][rows, :] = zero
                return total + value

            return step

        def both(t, total):
            add_pair(t, 0)
            return flush(main_ref, 0)(t, total)

        steps = his_main
        joint = jnp.minimum(pairs, steps)
        total = lax.fori_loop(0, joint, both, zero)
        lax.fori_loop(joint, pairs, add_pair, 0)
        total = lax.fori_loop(joint, steps, flush(main_ref, 0), total)

        total = lax.fori_loop(0, his - his_main, flush(halo_ref, his_main), total)
        deg_ref[...] = jnp.sum(total, axis=1, keepdims=True)

        def chunk(c, carry):
            entry = flag_ref[0, 0, c]
            first = (entry >> 16) * LANES

            def some(g, inner):
                @pl.when(((entry >> g) & 1) != 0)
                def _():
                    for i in range(BATCH):
                        k = slow_ref[0, 0, first + g * BATCH + i]
                        r = k >> 7
                        old = fill[0][pl.ds(r, 1), :]
                        fill[0][pl.ds(r, 1), :] = old + jnp.where(lanes == (k & 127), 1.0, 0.0)

                return inner

            lax.fori_loop(0, LANES // BATCH, some, 0)
            return carry

        lax.fori_loop(0, jnp.where(j < blocks, flag_ref[0, 0, LANES - 1], 0), chunk, 0)

    @pl.when(lax.rem(j, 2) == 0)
    def _():
        turn(cells[:2], cells[2:])

    @pl.when(lax.rem(j, 2) == 1)
    def _():
        turn(cells[2:], cells[:2])


def build_counts(edge_src, edge_dst, block_count, part_nodes):
    blocks, slots = edge_src.shape
    width = part_nodes + 2 * HALO
    dump = width // LANES * ROWS_BLK
    edge = jax.ShapeDtypeStruct((blocks, slots), jnp.int32)
    fast, slow, flags = pl.pallas_call(
        functools.partial(prep_kernel, dump),
        out_shape=(edge, edge, jax.ShapeDtypeStruct((blocks, LANES), jnp.int32)),
        compiler_params=pltpu.CompilerParams(vmem_limit_bytes=32 << 20),
        name="edge_prep",
    )(edge_src, edge_dst, block_count[:, None])
    nodes = blocks * ROWS_BLK

    def filled(j):
        return (jnp.minimum(j, blocks - 1), 0, 0)

    def left(j):
        return (jnp.maximum(j - 1, 0), 0)

    return pl.pallas_call(
        functools.partial(count_kernel, dump),
        grid=(blocks + 1,),
        out_shape=(
            jax.ShapeDtypeStruct((nodes, part_nodes), jnp.bfloat16),
            jax.ShapeDtypeStruct((nodes, 2 * HALO), jnp.bfloat16),
            jax.ShapeDtypeStruct((nodes, 1), jnp.float32),
        ),
        in_specs=[
            pl.BlockSpec(memory_space=pltpu.SMEM),
            pl.BlockSpec((1, 1, slots), filled, memory_space=pltpu.SMEM),
            pl.BlockSpec((1, 1, slots), filled, memory_space=pltpu.SMEM),
            pl.BlockSpec((1, 1, LANES), filled, memory_space=pltpu.SMEM),
        ],
        out_specs=(
            pl.BlockSpec((ROWS_BLK, part_nodes), left),
            pl.BlockSpec((ROWS_BLK, 2 * HALO), left),
            pl.BlockSpec((ROWS_BLK, 1), left),
        ),
        scratch_shapes=[pltpu.VMEM((dump + 8, LANES), jnp.float32)] * 4,
        compiler_params=pltpu.CompilerParams(vmem_limit_bytes=52 << 20),
        cost_estimate=pl.CostEstimate(flops=80_000_000_000, bytes_accessed=40_000_000, transcendentals=0),
        name="edge_counts",
    )(block_count, fast[:, None], slow[:, None], flags[:, None])


def ring_place():
    blk = lax.axis_size("blk")
    return lax.axis_index("dom") * blk + lax.axis_index("blk")


def meet_all(devices):
    barrier = pltpu.get_barrier_semaphore()
    me = ring_place()

    def greet(k, carry):
        other = lax.rem(me + k, devices)
        pl.semaphore_signal(barrier, inc=1, device_id=coords(other), device_id_type=MESH)
        return carry

    lax.fori_loop(1, devices, greet, 0)
    pl.semaphore_wait(barrier, devices - 1)


def coords(device):
    blk = lax.axis_size("blk")
    return (device // blk, lax.rem(device, blk))


def send(src, dst, device, send_sem, recv_sem):
    pltpu.make_async_remote_copy(
        src_ref=src,
        dst_ref=dst,
        send_sem=send_sem,
        recv_sem=recv_sem,
        device_id=coords(device),
        device_id_type=MESH,
    ).start()


def drain(ref, sem):
    pltpu.make_async_copy(ref, ref, sem).wait()


def fetch_kernel(devices, ids_ref, table_ref, rows_ref, asked_ref, ids_in, served, rows_in, sems):
    slot_cap = served.shape[0] // devices
    slots = served.shape[0]
    me = ring_place()
    meet_all(devices)

    def ask(k, carry):
        other = lax.rem(me + k, devices)
        send(ids_ref.at[other], ids_in.at[me], other, sems.at[0], sems.at[1])
        return carry

    lax.fori_loop(1, devices, ask, 0)
    own = pltpu.make_async_copy(ids_ref.at[me], ids_in.at[me], sems.at[2])
    own.start()
    own.wait()
    drain(ids_in.at[pl.ds(0, devices - 1)], sems.at[1])
    ids = ids_in[:, 0, :].astype(jnp.bfloat16)
    step = 16
    part = step * slot_cap
    lanes = ids.shape[1]
    lane = lax.broadcasted_iota(jnp.int32, (part, lanes), 1)
    slot = lax.broadcasted_iota(jnp.int32, (part, lanes), 0)
    rank = lax.rem(slot, slot_cap)
    weight = jnp.where(lane == rank, 32.0, 0.0) + jnp.where(lane == rank + slot_cap, 1.0, 0.0)
    column = lax.broadcasted_iota(jnp.int32, (part, table_ref.shape[0]), 1)

    def serve(c, carry):
        turn = lax.rem(c + me // step, devices // step)
        pick = (lane - turn * step == slot // slot_cap).astype(jnp.bfloat16)
        spread = jnp.dot(pick, ids, preferred_element_type=jnp.float32)
        asked = jnp.sum(spread * weight, axis=1, keepdims=True).astype(jnp.int32)
        at = pl.multiple_of(turn * part, part)
        asked_ref[pl.ds(at, part), :] = asked
        pick_row = (column == asked).astype(jnp.bfloat16)
        served[pl.ds(at, part), :] = jnp.dot(
            pick_row, table_ref[...], preferred_element_type=jnp.float32
        ).astype(jnp.bfloat16)

        def back(i, inner):
            other = turn * step + lax.rem(me + i, step)

            @pl.when(other != me)
            def _():
                send(
                    served.at[pl.ds(pl.multiple_of(other * slot_cap, slot_cap), slot_cap)],
                    rows_in.at[pl.ds(pl.multiple_of(me * slot_cap, slot_cap), slot_cap)],
                    other,
                    sems.at[3],
                    sems.at[4],
                )

            return inner

        lax.fori_loop(0, step, back, 0)
        return carry

    lax.fori_loop(0, devices // step, serve, 0)
    mine = pl.ds(pl.multiple_of(me * slot_cap, slot_cap), slot_cap)
    own_rows = pltpu.make_async_copy(served.at[mine], rows_in.at[mine], sems.at[2])
    own_rows.start()
    own_rows.wait()
    drain(rows_in.at[pl.ds(0, slots - slot_cap)], sems.at[4])
    rows_ref[...] = rows_in[...]
    drain(ids_in.at[pl.ds(0, devices - 1)], sems.at[0])
    drain(rows_in.at[pl.ds(0, slots - slot_cap)], sems.at[3])


def fetch_rows(ids, quotient, slot_cap):
    devices, _, lanes = ids.shape
    slots = devices * slot_cap
    width = quotient.shape[1]
    vmem = pl.BlockSpec(memory_space=pltpu.VMEM)
    return pl.pallas_call(
        functools.partial(fetch_kernel, devices),
        out_shape=(
            jax.ShapeDtypeStruct((slots, width), jnp.bfloat16),
            jax.ShapeDtypeStruct((slots, 1), jnp.int32),
        ),
        in_specs=[vmem, vmem],
        out_specs=(vmem, vmem),
        scratch_shapes=[
            pltpu.VMEM((devices, 1, lanes), jnp.float32),
            pltpu.VMEM((slots, width), jnp.bfloat16),
            pltpu.VMEM((slots, width), jnp.bfloat16),
            pltpu.SemaphoreType.DMA((5,)),
        ],
        compiler_params=pltpu.CompilerParams(
            collective_id=1, has_side_effects=True, vmem_limit_bytes=32 << 20
        ),
        name="fetch_rows",
    )(ids, quotient)


def spread_kernel(
    devices, rem_scale, scale, grads_ref, rem_ref, sums_ref, back_ref, total_ref, weight_ref, bias_ref,
    grads_in, rem_in, sums_in, piece, whole, sems
):
    slot_cap = grads_ref.shape[0] // devices
    slots = grads_ref.shape[0]
    tall, wide = rem_in.shape[1:]
    across = rem_ref.shape[1] // wide
    peers = sums_in.shape[0]
    high = sums_ref.shape[0] - 8
    me = ring_place()
    dom = lax.axis_index("dom")
    blk = lax.axis_index("blk")
    meet_all(devices)

    def tile(device):
        top = pl.multiple_of(device // across * tall, tall)
        return (pl.ds(top, tall), pl.ds(pl.multiple_of(lax.rem(device, across) * wide, wide), wide))

    def slot(device):
        return pl.ds(pl.multiple_of(device * slot_cap, slot_cap), slot_cap)

    def share(peer):
        top = pl.multiple_of(peer // across * 8, 8)
        return (pl.ds(top, 8), pl.ds(pl.multiple_of(lax.rem(peer, across) * wide, wide), wide))

    def send_rem(k, carry):
        other = lax.rem(me + k, devices)
        send(rem_ref.at[tile(other)], rem_in.at[me], other, sems.at[0], sems.at[1])
        return carry

    def send_sums(k, carry):
        other = lax.rem(blk + k, peers)
        to = dom * peers + other
        send(sums_ref.at[share(other)], sums_in.at[blk, pl.ds(0, 8), :], to, sems.at[7], sems.at[8])
        send(sums_ref.at[pl.ds(high, 8), pl.ds(0, wide)], sums_in.at[blk, pl.ds(8, 8), :], to, sems.at[7], sems.at[8])
        return carry

    def send_grads(k, carry):
        other = lax.rem(me + k, devices)
        send(grads_ref.at[slot(other)], grads_in.at[slot(me)], other, sems.at[2], sems.at[3])
        return carry

    def send_total(k, carry):
        other = lax.rem(me + k, devices)
        send(piece, whole.at[me], other, sems.at[4], sems.at[5])
        return carry

    def keep(src, dst):
        copy = pltpu.make_async_copy(src, dst, sems.at[6])
        copy.start()
        copy.wait()

    lax.fori_loop(1, peers, send_sums, 0)
    lax.fori_loop(1, devices, send_rem, 0)
    lax.fori_loop(1, devices, send_grads, 0)
    keep(rem_ref.at[tile(me)], rem_in.at[me])
    keep(grads_ref.at[slot(me)], grads_in.at[slot(me)])
    keep(sums_ref.at[share(blk)], sums_in.at[blk, pl.ds(0, 8), :])
    keep(sums_ref.at[pl.ds(high, 8), pl.ds(0, wide)], sums_in.at[blk, pl.ds(8, 8), :])
    drain(sums_in.at[pl.ds(0, peers - 1)], sems.at[8])
    drain(rem_in.at[pl.ds(0, devices - 1)], sems.at[1])
    piece[:tall] = (jnp.sum(rem_in[...].astype(jnp.float32), axis=0) * rem_scale).astype(jnp.bfloat16)
    piece[tall:] = (jnp.sum(sums_in[...], axis=0) * scale).astype(jnp.bfloat16)
    lax.fori_loop(1, devices, send_total, 0)
    keep(piece, whole.at[me])
    drain(grads_in.at[pl.ds(0, slots - slot_cap)], sems.at[3])
    back_ref[...] = grads_in[...]
    drain(whole.at[pl.ds(0, devices - 1)], sems.at[5])

    def lay(k, carry):
        for part in range(across):
            got = whole[k * across + part].astype(jnp.float32)
            lanes = slice(part * wide, (part + 1) * wide)
            total_ref[pl.ds(pl.multiple_of(k * tall, tall), tall), lanes] = got[:tall]
            weight_ref[pl.ds(pl.multiple_of(k * 8, 8), 8), lanes] = got[tall : tall + 8]
        return carry

    lax.fori_loop(0, devices // across, lay, 0)
    for d in range(devices // peers):
        bias_ref[d : d + 1, :] = whole[d * peers, tall + 8 : tall + 16, :].astype(jnp.float32)[0:1]
    drain(rem_in.at[pl.ds(0, devices - 1)], sems.at[0])
    drain(grads_in.at[pl.ds(0, slots - slot_cap)], sems.at[2])
    drain(whole.at[pl.ds(0, devices - 1)], sems.at[4])
    drain(sums_in.at[pl.ds(0, peers - 1)], sems.at[7])


def spread_grads(outgoing, local_remain, sums, devices, peers, rem_scale, scale):
    rows, width = local_remain.shape
    wide = LANES
    tall = rows * width // devices // wide
    doms = devices // peers
    vmem = pl.BlockSpec(memory_space=pltpu.VMEM)
    return pl.pallas_call(
        functools.partial(spread_kernel, devices, rem_scale, scale),
        out_shape=(
            jax.ShapeDtypeStruct(outgoing.shape, jnp.bfloat16),
            jax.ShapeDtypeStruct((rows, width), jnp.float32),
            jax.ShapeDtypeStruct((doms * (sums.shape[0] - 8), width), jnp.float32),
            jax.ShapeDtypeStruct((doms, wide), jnp.float32),
        ),
        in_specs=[vmem, vmem, vmem],
        out_specs=(vmem, vmem, vmem, vmem),
        scratch_shapes=[
            pltpu.VMEM(outgoing.shape, jnp.bfloat16),
            pltpu.VMEM((devices, tall, wide), jnp.bfloat16),
            pltpu.VMEM((peers, 16, wide), jnp.float32),
            pltpu.VMEM((tall + 16, wide), jnp.bfloat16),
            pltpu.VMEM((devices, tall + 16, wide), jnp.bfloat16),
            pltpu.SemaphoreType.DMA((9,)),
        ],
        compiler_params=pltpu.CompilerParams(
            collective_id=2, has_side_effects=True, vmem_limit_bytes=32 << 20
        ),
        name="spread_grads",
    )(outgoing, local_remain, sums)


def forward_kernel(
    counts_ref, rows_ref, halo_counts_ref, halo_rows_ref, deg_ref, x_ref, w_self_ref, w_neigh_ref, bias_ref, cot_ref,
    out_ref, grad_ref, halo_ref, dx_ref, weights_ref, total, acc_self, acc_neigh
):
    k = pl.program_id(0)
    nodes, feats = total.shape
    tile = 256

    def cut(r):
        return pl.ds(pl.multiple_of(r * tile, tile), tile)

    @pl.when(k == 0)
    def _():
        def start(r, carry):
            total[cut(r), :] = dot(halo_counts_ref[cut(r), :], halo_rows_ref[...])
            return carry

        lax.fori_loop(0, nodes // tile, start, 0)

    def step(r, carry):
        total[cut(r), :] += dot(counts_ref[cut(r), :], rows_ref[...])
        return carry

    lax.fori_loop(0, nodes // tile, step, 0)

    @pl.when(k == pl.num_programs(0) - 1)
    def _():
        acc_self[...] = jnp.zeros_like(acc_self)
        acc_neigh[...] = jnp.zeros_like(acc_neigh)

        def layer(r, bias_sum):
            rows = cut(r)
            divisor = jnp.maximum(deg_ref[rows, :], 1.0)
            x = x_ref[rows, :]
            neighbour = (total[rows, :] / divisor).astype(jnp.bfloat16)
            preact = dot(x, w_self_ref[...]) + dot(neighbour, w_neigh_ref[...]) + bias_ref[...]
            sigma = jax.nn.sigmoid(preact)
            out_ref[rows, :] = (preact * sigma).astype(jnp.bfloat16)
            slope = sigma * (1.0 + preact * (1.0 - sigma))
            dpre = (cot_ref[rows, :].astype(jnp.float32) * slope).astype(jnp.bfloat16)
            scaled = dot(dpre, w_neigh_ref[...], COLS) / divisor
            grad_ref[:, rows] = scaled.T.astype(jnp.bfloat16)
            dx_ref[rows, :] = dot(dpre, w_self_ref[...], COLS)
            acc_self[...] += dot(x, dpre, ROWS)
            acc_neigh[...] += dot(neighbour, dpre, ROWS)
            return bias_sum + jnp.sum(dpre.astype(jnp.float32), axis=0, keepdims=True)

        bias_sum = lax.fori_loop(0, nodes // tile, layer, jnp.zeros((1, feats), jnp.float32))
        halo_ref[...] = dot(grad_ref[...], halo_counts_ref[...]).T.astype(jnp.bfloat16)
        doms = weights_ref.shape[0]
        each = 2 * feats // doms
        wide = feats // doms
        spread = jnp.broadcast_to(bias_sum, (8, feats))
        for c in range(doms):
            source, at = (acc_self, c * each) if c * each < feats else (acc_neigh, c * each - feats)
            weights_ref[c, :each, :] = source[at : at + each, :]
            shift = (feats - c * wide) % feats
            weights_ref[c, each:, :] = pltpu.roll(spread, shift, 1) if shift else spread


def forward(counts, gathered, halo_counts, halo_rows, degree, features, w_self, w_neigh, bias, cotangent, doms):
    nodes, feats = features.shape
    steps = counts.shape[1] // nodes

    def whole(array):
        return pl.BlockSpec(array.shape, lambda k: (0,) * len(array.shape))

    out_shape = (
        jax.ShapeDtypeStruct((nodes, feats), jnp.bfloat16),
        jax.ShapeDtypeStruct((feats, nodes), jnp.bfloat16),
        jax.ShapeDtypeStruct(halo_rows.shape, jnp.bfloat16),
        jax.ShapeDtypeStruct((nodes, feats), jnp.float32),
        jax.ShapeDtypeStruct((doms, 2 * feats // doms + 8, feats), jnp.float32),
    )
    kept = (halo_counts, halo_rows, degree, features, w_self, w_neigh, bias, cotangent)
    return pl.pallas_call(
        forward_kernel,
        grid=(steps,),
        out_shape=out_shape,
        in_specs=[
            pl.BlockSpec((nodes, nodes), lambda k: (0, k)),
            pl.BlockSpec((nodes, feats), lambda k: (k, 0)),
        ]
        + [whole(array) for array in kept],
        out_specs=tuple(whole(array) for array in out_shape),
        scratch_shapes=[
            pltpu.VMEM((nodes, feats), jnp.float32),
            pltpu.VMEM((feats, feats), jnp.float32),
            pltpu.VMEM((feats, feats), jnp.float32),
        ],
        compiler_params=pltpu.CompilerParams(vmem_limit_bytes=40 << 20),
        name="forward_layer",
    )(counts, gathered, *kept)


def reduce_kernel(
    counts_ref, grad_ref, weights_ref, halo_ref, dx_ref, out_ref, sums_ref, load, part, mid, fin, half_sum, mid2, fin2, sems_load, s_out, s_mid, s_fin, t_out, t_mid, t_fin, weights_in, w_out, w_in, halo_in, own, h_out, h_in
):
    side = 4
    nodes = grad_ref.shape[1]
    feats = grad_ref.shape[0] // 2
    span = nodes // 2
    dom = lax.axis_index("dom")
    blk = lax.axis_index("blk")
    x, y = blk // side, lax.rem(blk, side)

    def at(dx, dy):
        return lax.rem(x + dx, side) * side + lax.rem(y + dy, side)

    def device(half, first, second):
        dx, dy = (first, second) if half == 0 else (second, first)
        return (dom, at(dx, dy))

    barrier = pltpu.get_barrier_semaphore()
    for dx, dy in ((1, 0), (3, 0), (0, 1), (0, 3)):
        pl.semaphore_signal(barrier, inc=1, device_id=(dom, at(dx, dy)), device_id_type=MESH)
    doms = weights_ref.shape[0]
    for k in range(1, doms):
        pl.semaphore_signal(barrier, inc=1, device_id=(lax.rem(dom + k, doms), blk), device_id_type=MESH)

    order = [(2, 2), (2, 1), (1, 2), (2, 3), (3, 2), (2, 0), (0, 2), (1, 1), (3, 3), (1, 3), (3, 1)]
    order += [(1, 0), (0, 1), (3, 0), (0, 3), (0, 0)]
    depth = load.shape[0]

    def fetch(i):
        dx, dy = order[i]
        columns = pl.ds(pl.multiple_of(at(dx, dy) * nodes, nodes), nodes)
        return pltpu.make_async_copy(counts_ref.at[:, columns], load.at[i % depth], sems_load.at[i % depth])

    for i in range(depth - 1):
        fetch(i).start()
    pl.semaphore_wait(barrier, 4 + doms - 1)

    def to_dom(k):
        other = lax.rem(dom + k, doms)
        return pltpu.make_async_remote_copy(
            src_ref=weights_ref.at[other],
            dst_ref=weights_in.at[k],
            send_sem=w_out.at[k],
            recv_sem=w_in.at[k],
            device_id=(other, blk),
            device_id_type=MESH,
        )

    halo = halo_in.shape[1]

    def to_side(side_index):
        return pltpu.make_async_remote_copy(
            src_ref=halo_ref.at[pl.ds(side_index * halo, halo)],
            dst_ref=halo_in.at[side_index],
            send_sem=h_out.at[side_index],
            recv_sem=h_in.at[side_index],
            device_id=(lax.rem(dom + (doms - 1 if side_index == 0 else 1), doms), blk),
            device_id_type=MESH,
        )

    for k in range(1, doms):
        to_dom(k).start()
    to_side(0).start()
    to_side(1).start()

    def remote(src, dst, half, first, second, send_sem, recv_sem):
        return pltpu.make_async_remote_copy(
            src_ref=src,
            dst_ref=dst,
            send_sem=send_sem,
            recv_sem=recv_sem,
            device_id=device(half, first, second),
            device_id_type=MESH,
        )

    def along(unit):
        return unit % 2 == 0

    def to_mid(half, unit):
        return remote(
            part.at[half, 2, unit], mid.at[half, unit], half, 1 if along(unit) else 3, 0,
            s_out.at[half, 0, unit], s_mid.at[half, unit],
        )

    def to_fin(half, first, unit):
        way = 0 if first == 1 else 1
        return remote(
            part.at[half, first, unit], fin.at[half, way, unit], half, first, 0,
            s_out.at[half, 1 + way, unit], s_fin.at[half, way, unit],
        )

    def relays(first, unit):
        return along(unit) == (first == 1)

    tile = 256
    waiting = []
    for i, (dx, dy) in enumerate(order):
        if i + depth - 1 < len(order):
            fetch(i + depth - 1).start()
        fetch(i).wait()

        def columns(n, carry, slot=i % depth, dx=dx, dy=dy):
            cut = pl.ds(pl.multiple_of(n * tile, tile), tile)
            value = jnp.dot(grad_ref[...], load[slot, :, cut], preferred_element_type=jnp.float32)
            part[0, dx, dy, :, cut] = value[:feats].astype(jnp.bfloat16)
            part[1, dy, dx, :, cut] = value[feats:].astype(jnp.bfloat16)
            return carry

        lax.fori_loop(0, nodes // tile, columns, 0)
        for half, first, unit in ((0, dx, dy), (1, dy, dx)):
            if first == 2:
                to_mid(half, unit).start()
            elif first != 0:
                if relays(first, unit):
                    waiting.append((half, first, unit))
                else:
                    to_fin(half, first, unit).start()
    waiting.sort(key=lambda item: (2, 1, 3, 0).index(item[2]))
    for half, first, unit in waiting:
        to_mid(half, unit).wait_recv()
        mine = part[half, first, unit].astype(jnp.float32)
        part[half, first, unit] = (mine + mid[half, unit].astype(jnp.float32)).astype(jnp.bfloat16)
        to_fin(half, first, unit).start()

    def cut(piece):
        return pl.ds(piece * span, span)

    def to_mid2(half, piece):
        return remote(
            half_sum.at[half, 1, :, cut(piece)], mid2.at[half, piece], half, 0, 1 if piece == 0 else 3,
            t_out.at[half, 0, piece], t_mid.at[half, piece],
        )

    def to_fin2(half, second, piece):
        way = 0 if second == 1 else 1
        return remote(
            half_sum.at[half, 0 if second == 1 else 2, :, cut(piece)], fin2.at[half, way, piece], half, 0, second,
            t_out.at[half, 1 + way, piece], t_fin.at[half, way, piece],
        )

    def summed(half, unit):
        to_fin(half, 1, unit).wait_recv()
        to_fin(half, 3, unit).wait_recv()
        total = part[half, 0, unit].astype(jnp.float32) + fin[half, 0, unit].astype(jnp.float32)
        return total + fin[half, 1, unit].astype(jnp.float32)

    for half in range(2):
        half_sum[half, 1] = summed(half, 2).astype(jnp.bfloat16)
        to_mid2(half, 0).start()
        to_mid2(half, 1).start()
    for second in (1, 3):
        direct, relayed = (1, 0) if second == 1 else (0, 1)
        for half in range(2):
            half_sum[half, second - 1] = summed(half, second).astype(jnp.bfloat16)
            to_fin2(half, second, direct).start()
    for second in (1, 3):
        direct, relayed = (1, 0) if second == 1 else (0, 1)
        for half in range(2):
            to_mid2(half, relayed).wait_recv()
            mine = half_sum[half, second - 1, :, cut(relayed)].astype(jnp.float32)
            both = mine + mid2[half, relayed].astype(jnp.float32)
            half_sum[half, second - 1, :, cut(relayed)] = both.astype(jnp.bfloat16)
            to_fin2(half, second, relayed).start()
    for half in range(2):
        own[half * feats : (half + 1) * feats, :] = summed(half, 0)
    to_side(0).wait_recv()
    to_side(1).wait_recv()
    for half in range(2):
        rows = slice(half * feats, (half + 1) * feats)
        for piece in range(2):
            to_fin2(half, 1, piece).wait_recv()
            to_fin2(half, 3, piece).wait_recv()
            total = own[rows, piece * span : (piece + 1) * span] + fin2[half, 0, piece].astype(jnp.float32)
            total = (total + fin2[half, 1, piece].astype(jnp.float32)).T
            near = slice(piece * span, (piece + 1) * span)
            out_ref[near, rows] = dx_ref[near, rows] + total
            edge = slice(0, halo) if piece == 0 else slice(nodes - halo, nodes)
            out_ref[edge, rows] += halo_in[1 - piece, :, rows].astype(jnp.float32)
    to_side(0).wait_send()
    to_side(1).wait_send()
    sums = weights_ref[dom]
    for k in range(1, doms):
        to_dom(k).wait_recv()
        sums = sums + weights_in[k]
    sums_ref[...] = sums
    for k in range(1, doms):
        to_dom(k).wait_send()
    for half in range(2):
        for unit in range(side):
            to_mid(half, unit).wait_send()
            to_fin(half, 1, unit).wait_send()
            to_fin(half, 3, unit).wait_send()
        for piece in range(2):
            to_mid2(half, piece).wait_send()
            to_fin2(half, 1, piece).wait_send()
            to_fin2(half, 3, piece).wait_send()


def reduce_sources(counts, grad, weights, halo, dx):
    feats, nodes = grad.shape
    half = feats // 2
    kind = jnp.bfloat16
    dma = pltpu.SemaphoreType.DMA
    vmem = pl.BlockSpec(memory_space=pltpu.VMEM)
    return pl.pallas_call(
        reduce_kernel,
        out_shape=(
            jax.ShapeDtypeStruct((nodes, feats), jnp.float32),
            jax.ShapeDtypeStruct(weights.shape[1:], jnp.float32),
        ),
        in_specs=[pl.BlockSpec(memory_space=pl.ANY), vmem, vmem, vmem, vmem],
        out_specs=(vmem, vmem),
        scratch_shapes=[
            pltpu.VMEM((3, nodes, nodes), kind),
            pltpu.VMEM((2, 4, 4, half, nodes), kind),
            pltpu.VMEM((2, 4, half, nodes), kind),
            pltpu.VMEM((2, 2, 4, half, nodes), kind),
            pltpu.VMEM((2, 3, half, nodes), kind),
            pltpu.VMEM((2, 2, half, nodes // 2), kind),
            pltpu.VMEM((2, 2, 2, half, nodes // 2), kind),
            dma((3,)),
            dma((2, 3, 4)),
            dma((2, 4)),
            dma((2, 2, 4)),
            dma((2, 3, 2)),
            dma((2, 2)),
            dma((2, 2, 2)),
            pltpu.VMEM(weights.shape, jnp.float32),
            dma((weights.shape[0],)),
            dma((weights.shape[0],)),
            pltpu.VMEM((2, halo.shape[0] // 2, feats), kind),
            pltpu.VMEM((feats, nodes), jnp.float32),
            dma((2,)),
            dma((2,)),
        ],
        compiler_params=pltpu.CompilerParams(
            collective_id=3, has_side_effects=True, vmem_limit_bytes=48 << 20
        ),
        name="reduce_sources",
    )(counts, grad, weights, halo, dx)


def shifted(block, axis, distance):
    devices = range(lax.axis_size(axis))
    route = [((i - distance) % len(devices), i) for i in devices]
    return lax.ppermute(block, axis, route)


def hot(index, size):
    return (index[:, None] == jnp.arange(size, dtype=jnp.int32)[None, :]).astype(jnp.bfloat16)


def dot(a, b, dims=(((1,), (0,)), ((), ()))):
    return lax.dot_general(a, b, dims, preferred_element_type=jnp.float32)


def per_device(
    node_owner,
    node_qrow,
    node_rem,
    quotient,
    remainder,
    edge_src,
    edge_dst,
    block_count,
    w_self,
    w_neigh,
    bias,
    cotangent,
):
    nodes_dev = node_qrow.shape[0]
    feature_dim = quotient.shape[1]
    devices = lax.axis_size("dom") * lax.axis_size("blk")
    part_nodes = nodes_dev * lax.axis_size("blk")
    slot_cap = 2 * nodes_dev // devices
    slots = devices * slot_cap
    owner_dev = node_owner[:, 0]
    owner_hot = hot(owner_dev, devices)
    row_ids = jnp.arange(nodes_dev, dtype=jnp.int32)
    lower_mask = (row_ids[:, None] > row_ids[None, :]).astype(jnp.bfloat16)
    earlier = dot(lower_mask, owner_hot)
    slot_rank = jnp.sum(earlier * owner_hot.astype(jnp.float32), axis=1).astype(jnp.int32)
    slot_index = owner_dev * slot_cap + slot_rank
    rank_hot = hot(slot_rank, slot_cap)
    high = (node_qrow >> 5).astype(jnp.bfloat16)[:, None]
    low = (node_qrow & 31).astype(jnp.bfloat16)[:, None]
    asked = dot(owner_hot, jnp.concatenate([rank_hot * high, rank_hot * low], axis=1), ROWS)
    ids = jnp.pad(asked, ((0, 0), (0, LANES - 2 * slot_cap)))[:, None, :]
    returned, asked_rows = fetch_rows(ids, quotient, slot_cap)
    asked_hot = hot(asked_rows[:, 0], quotient.shape[0])
    slot_hot = hot(slot_index, slots)
    quot_rows = dot(slot_hot, returned)
    rem_hot = hot(node_rem, remainder.shape[0])
    remain_rows = dot(rem_hot, remainder)
    features = (quot_rows * remain_rows).astype(jnp.bfloat16)
    part_gathered = lax.all_gather(features, "blk", axis=0, tiled=True)
    low_rows = shifted(features[nodes_dev - HALO :], "dom", 1)
    high_rows = shifted(features[:HALO], "dom", -1)
    halo_rows = jnp.concatenate([low_rows, high_rows], axis=0)

    counts, halo_counts, degree = build_counts(edge_src, edge_dst, block_count, part_nodes)
    doms = lax.axis_size("dom")
    out, grad_t, halo_grads, dx_self, weights = forward(
        counts, part_gathered, halo_counts, halo_rows, degree, features, w_self, w_neigh, bias[None], cotangent, doms
    )
    grad_x, weight_sums = reduce_sources(counts, grad_t, weights, halo_grads, dx_self)
    outgoing = dot(slot_hot, (grad_x * remain_rows).astype(jnp.bfloat16), ROWS).astype(jnp.bfloat16)
    local_remain = dot(rem_hot, (grad_x * quot_rows).astype(jnp.bfloat16), ROWS)

    nodes_total = nodes_dev * devices
    weight_scale = 1.0 / math.sqrt(nodes_total)
    remain_scale = math.sqrt(remainder.shape[0] / nodes_total)
    returned_grads, d_remainder, d_weights, d_bias = spread_grads(
        outgoing,
        local_remain.astype(jnp.bfloat16),
        weight_sums,
        devices,
        lax.axis_size("blk"),
        remain_scale,
        weight_scale,
    )
    d_quotient = dot(asked_hot, returned_grads, ROWS)
    d_self, d_neigh = d_weights[:feature_dim], d_weights[feature_dim:]
    d_bias = d_bias[:, : feature_dim // doms].reshape(-1)
    return (out, d_quotient, d_remainder, d_self, d_neigh, d_bias)


def solution(mesh):
    both = P(AXES)
    rows = P(AXES, None)
    return jax.shard_map(
        per_device,
        mesh=mesh,
        in_specs=(rows, both, both, rows, P(), rows, rows, both, P(), P(), P(), rows),
        out_specs=(rows, rows, P(), P(), P(), P()),
        check_vma=False,
    )
```

```python
import functools
import math

import jax
import jax.numpy as jnp
from jax import lax
from jax.experimental import pallas as pl
from jax.experimental.pallas import tpu as pltpu
from jax.sharding import PartitionSpec as P

ROWS_BLK = 128
HALO = 256
LANES = 128
BATCH = 8
AXES = ("dom", "blk")
MESH = pl.DeviceIdType.MESH
ROWS = (((0,), (0,)), ((), ()))
COLS = (((1,), (1,)), ((), ()))


def prep_kernel(dump, src_ref, dst_ref, count_ref, fast_ref, slow_ref, flag_ref):
    blocks, slots = src_ref.shape
    src = src_ref[...]
    lane = lax.broadcasted_iota(jnp.int32, (blocks, slots), 1)
    cell = ((src >> 7) * ROWS_BLK + dst_ref[...]) * LANES + (src & 127)
    live = lane < count_ref[...]
    spare = dump * LANES
    cell = jnp.where(live, cell, spare)
    row = cell >> 7
    clash = jnp.zeros((blocks, slots), jnp.bool_)
    place = lane & (BATCH - 1)
    for s in range(1, BATCH):
        clash = clash | ((pltpu.roll(row, s, 1) == row) & (place >= s))
    clash = clash & live
    fast_ref[...] = jnp.where(clash, spare, cell)
    slow_ref[...] = jnp.where(clash, cell, spare)
    ones = jnp.where(clash, 1.0, 0.0).astype(jnp.bfloat16)
    chunks = slots // LANES
    col = lax.broadcasted_iota(jnp.int32, (blocks, LANES), 1)
    into = lax.broadcasted_iota(jnp.int32, (LANES, LANES), 0) // BATCH
    group = (into == lax.broadcasted_iota(jnp.int32, (LANES, LANES), 1)).astype(jnp.bfloat16)
    found = jnp.zeros((blocks, LANES), jnp.int32)
    number = jnp.zeros((blocks, 1), jnp.int32)
    for c in range(chunks):
        hits = jnp.dot(ones[:, c * LANES : (c + 1) * LANES], group, preferred_element_type=jnp.float32)
        bits = jnp.sum(jnp.where(hits > 0.5, (1 << (col & (LANES // BATCH - 1))).astype(jnp.float32), 0.0), axis=1, keepdims=True)
        bits = bits.astype(jnp.int32)
        some = bits > 0
        found = found + jnp.where((col == number) & some, c * 65536 + bits, 0)
        number = number + some.astype(jnp.int32)
    flag_ref[...] = jnp.where(col == LANES - 1, number, found)


def count_kernel(dump, count_ref, fast_ref, slow_ref, flag_ref, main_ref, halo_ref, deg_ref, *cells):
    j = pl.program_id(0)
    blocks = pl.num_programs(0) - 1
    his = dump // ROWS_BLK
    his_main = main_ref.shape[1] // LANES
    zero = jnp.zeros((ROWS_BLK, LANES), jnp.float32)
    lanes = lax.broadcasted_iota(jnp.int32, (1, LANES), 1)

    @pl.when(j == 0)
    def _():
        def clear(i, carry):
            for ref in cells[:2]:
                ref[pl.ds(pl.multiple_of(i * ROWS_BLK, ROWS_BLK), ROWS_BLK), :] = zero
            return carry

        lax.fori_loop(0, his, clear, 0)
        for ref in cells:
            ref[pl.ds(dump, 8), :] = jnp.zeros((8, LANES), jnp.float32)

    count = jnp.where(j < blocks, count_ref[jnp.minimum(j, blocks - 1)], 0)
    pairs = (count + 2 * BATCH - 1) // (2 * BATCH)

    def add_batch(ref, first):
        keys = [fast_ref[0, 0, first + i] for i in range(BATCH)]
        rows = [k >> 7 for k in keys]
        olds = [ref[pl.ds(r, 1), :] for r in rows]
        news = [old + jnp.where(lanes == (k & 127), 1.0, 0.0) for old, k in zip(olds, keys)]
        for r, new in zip(rows, news):
            ref[pl.ds(r, 1), :] = new

    def turn(fill, leave):
        def add_pair(t, carry):
            add_batch(fill[0], t * 2 * BATCH)
            add_batch(fill[1], t * 2 * BATCH + BATCH)
            return carry

        def flush(ref, first):
            def step(h, total):
                at = pl.multiple_of((first + h) * ROWS_BLK, ROWS_BLK)
                rows = pl.ds(at, ROWS_BLK)
                value = leave[0][rows, :] + leave[1][rows, :]
                ref[:, pl.ds(pl.multiple_of(h * LANES, LANES), LANES)] = value.astype(jnp.bfloat16)
                leave[0][rows, :] = zero
                leave[1][rows, :] = zero
                return total + value

            return step

        def both(t, total):
            add_pair(t, 0)
            return flush(main_ref, 0)(t, total)

        steps = his_main
        joint = jnp.minimum(pairs, steps)
        total = lax.fori_loop(0, joint, both, zero)
        lax.fori_loop(joint, pairs, add_pair, 0)
        total = lax.fori_loop(joint, steps, flush(main_ref, 0), total)

        total = lax.fori_loop(0, his - his_main, flush(halo_ref, his_main), total)
        deg_ref[...] = jnp.sum(total, axis=1, keepdims=True)

        def chunk(c, carry):
            entry = flag_ref[0, 0, c]
            first = (entry >> 16) * LANES

            def some(g, inner):
                @pl.when(((entry >> g) & 1) != 0)
                def _():
                    for i in range(BATCH):
                        k = slow_ref[0, 0, first + g * BATCH + i]
                        r = k >> 7
                        old = fill[0][pl.ds(r, 1), :]
                        fill[0][pl.ds(r, 1), :] = old + jnp.where(lanes == (k & 127), 1.0, 0.0)

                return inner

            lax.fori_loop(0, LANES // BATCH, some, 0)
            return carry

        lax.fori_loop(0, jnp.where(j < blocks, flag_ref[0, 0, LANES - 1], 0), chunk, 0)

    @pl.when(lax.rem(j, 2) == 0)
    def _():
        turn(cells[:2], cells[2:])

    @pl.when(lax.rem(j, 2) == 1)
    def _():
        turn(cells[2:], cells[:2])


def build_counts(edge_src, edge_dst, block_count, part_nodes):
    blocks, slots = edge_src.shape
    width = part_nodes + 2 * HALO
    dump = width // LANES * ROWS_BLK
    edge = jax.ShapeDtypeStruct((blocks, slots), jnp.int32)
    fast, slow, flags = pl.pallas_call(
        functools.partial(prep_kernel, dump),
        out_shape=(edge, edge, jax.ShapeDtypeStruct((blocks, LANES), jnp.int32)),
        compiler_params=pltpu.CompilerParams(vmem_limit_bytes=32 << 20),
        name="edge_prep",
    )(edge_src, edge_dst, block_count[:, None])
    nodes = blocks * ROWS_BLK

    def filled(j):
        return (jnp.minimum(j, blocks - 1), 0, 0)

    def left(j):
        return (jnp.maximum(j - 1, 0), 0)

    return pl.pallas_call(
        functools.partial(count_kernel, dump),
        grid=(blocks + 1,),
        out_shape=(
            jax.ShapeDtypeStruct((nodes, part_nodes), jnp.bfloat16),
            jax.ShapeDtypeStruct((nodes, 2 * HALO), jnp.bfloat16),
            jax.ShapeDtypeStruct((nodes, 1), jnp.float32),
        ),
        in_specs=[
            pl.BlockSpec(memory_space=pltpu.SMEM),
            pl.BlockSpec((1, 1, slots), filled, memory_space=pltpu.SMEM),
            pl.BlockSpec((1, 1, slots), filled, memory_space=pltpu.SMEM),
            pl.BlockSpec((1, 1, LANES), filled, memory_space=pltpu.SMEM),
        ],
        out_specs=(
            pl.BlockSpec((ROWS_BLK, part_nodes), left),
            pl.BlockSpec((ROWS_BLK, 2 * HALO), left),
            pl.BlockSpec((ROWS_BLK, 1), left),
        ),
        scratch_shapes=[pltpu.VMEM((dump + 8, LANES), jnp.float32)] * 4,
        compiler_params=pltpu.CompilerParams(vmem_limit_bytes=52 << 20),
        cost_estimate=pl.CostEstimate(flops=80_000_000_000, bytes_accessed=40_000_000, transcendentals=0),
        name="edge_counts",
    )(block_count, fast[:, None], slow[:, None], flags[:, None])


def ring_place():
    blk = lax.axis_size("blk")
    return lax.axis_index("dom") * blk + lax.axis_index("blk")


def greet_all(devices):
    me = ring_place()

    def greet(k, carry):
        other = lax.rem(me + k, devices)
        barrier = pltpu.get_barrier_semaphore()
        pl.semaphore_signal(barrier, inc=1, device_id=coords(other), device_id_type=MESH)
        return carry

    lax.fori_loop(1, devices, greet, 0)


def meet_all(devices):
    pl.semaphore_wait(pltpu.get_barrier_semaphore(), devices - 1)


def as_row(column):
    wide = jnp.broadcast_to(column.astype(jnp.float32), (column.shape[0], LANES))
    return wide.T[0:1].astype(jnp.int32)


def pick(column, first, size):
    lane = lax.broadcasted_iota(jnp.int32, (column.shape[0], size), 1) + first
    return (lane == column).astype(jnp.bfloat16)


def pick_rows(row, first, size):
    line = lax.broadcasted_iota(jnp.int32, (size, row.shape[1]), 0) + first
    return (line == row).astype(jnp.bfloat16)


def coords(device):
    blk = lax.axis_size("blk")
    return (device // blk, lax.rem(device, blk))


def send(src, dst, device, send_sem, recv_sem):
    pltpu.make_async_remote_copy(
        src_ref=src,
        dst_ref=dst,
        send_sem=send_sem,
        recv_sem=recv_sem,
        device_id=coords(device),
        device_id_type=MESH,
    ).start()


def drain(ref, sem):
    pltpu.make_async_copy(ref, ref, sem).wait()


def fetch_kernel(
    devices, owner_ref, qrow_ref, rem_ref, table_ref, remainder_ref, x_ref, qv_ref, rv_ref, asked_ref, slot_ref,
    ids_out, ids_in, served, rows_in, slot_col, slot_hot, sems
):
    slots, width = served.shape
    slot_cap = slots // devices
    nodes = owner_ref.shape[0]
    me = ring_place()
    tile = 256
    greet_all(devices)

    def cut(r):
        return pl.ds(pl.multiple_of(r * tile, tile), tile)

    owner_hot = pick(owner_ref[...], 0, devices)
    lane = lax.broadcasted_iota(jnp.int32, (tile, devices), 1)
    wish = jnp.zeros((devices, devices), jnp.float32)
    for r in range(nodes // tile):
        rows = slice(r * tile, (r + 1) * tile)
        line = lax.broadcasted_iota(jnp.int32, (tile, nodes), 0) + r * tile
        before = (line > lax.broadcasted_iota(jnp.int32, (tile, nodes), 1)).astype(jnp.bfloat16)
        mine = owner_hot[rows]
        rank = jnp.sum(dot(before, owner_hot) * mine.astype(jnp.float32), axis=1, keepdims=True).astype(jnp.int32)
        slot_col[rows, :] = owner_ref[rows, :] * slot_cap + rank
        qrow = qrow_ref[rows, :]
        parts = jnp.where(lane == rank, qrow >> 5, 0) + jnp.where(lane == rank + slot_cap, qrow & 31, 0)
        wish = wish + dot(mine, parts.astype(jnp.float32).astype(jnp.bfloat16), ROWS)
    ids_out[:, 0, :] = wish
    meet_all(devices)

    def ask(k, carry):
        other = lax.rem(me + k, devices)
        send(ids_out.at[other], ids_in.at[me], other, sems.at[0], sems.at[1])
        return carry

    lax.fori_loop(1, devices, ask, 0)

    def remain(r, carry):
        rows = cut(r)
        rv_ref[rows, :] = dot(pick(rem_ref[rows, :], 0, remainder_ref.shape[0]), remainder_ref[...]).astype(jnp.bfloat16)
        return carry

    lax.fori_loop(0, nodes // tile, remain, 0)
    slot_ref[...] = as_row(slot_col[...])
    own = pltpu.make_async_copy(ids_out.at[me], ids_in.at[me], sems.at[2])
    own.start()
    own.wait()
    drain(ids_in.at[pl.ds(0, devices - 1)], sems.at[1])
    ids = ids_in[:, 0, :].astype(jnp.bfloat16)
    step = 16
    part = step * slot_cap
    slot = lax.broadcasted_iota(jnp.int32, (part, devices), 0)
    place = lax.broadcasted_iota(jnp.int32, (part, devices), 1)
    rank_of = lax.rem(slot, slot_cap)
    weight = jnp.where(place == rank_of, 32.0, 0.0) + jnp.where(place == rank_of + slot_cap, 1.0, 0.0)

    def serve(c, carry):
        turn = lax.rem(c + me // step, devices // step)
        whose = (place - turn * step == slot // slot_cap).astype(jnp.bfloat16)
        asked = jnp.sum(dot(whose, ids) * weight, axis=1, keepdims=True).astype(jnp.int32)
        at = pl.multiple_of(turn * part, part)
        asked_ref[:, pl.ds(at, part)] = as_row(asked)
        served[pl.ds(at, part), :] = dot(pick(asked, 0, table_ref.shape[0]), table_ref[...]).astype(jnp.bfloat16)

        def back(i, inner):
            other = turn * step + lax.rem(me + i, step)

            @pl.when(other != me)
            def _():
                send(
                    served.at[pl.ds(pl.multiple_of(other * slot_cap, slot_cap), slot_cap)],
                    rows_in.at[pl.ds(pl.multiple_of(me * slot_cap, slot_cap), slot_cap)],
                    other,
                    sems.at[3],
                    sems.at[4],
                )

            return inner

        lax.fori_loop(0, step, back, 0)
        return carry

    lax.fori_loop(0, devices // step, serve, 0)
    mine = pl.ds(pl.multiple_of(me * slot_cap, slot_cap), slot_cap)
    own_rows = pltpu.make_async_copy(served.at[mine], rows_in.at[mine], sems.at[2])
    own_rows.start()

    def prepare(r, carry):
        slot_hot[cut(r), :] = pick(slot_col[cut(r), :], 0, slots)
        return carry

    lax.fori_loop(0, nodes // tile, prepare, 0)
    own_rows.wait()
    drain(rows_in.at[pl.ds(0, slots - slot_cap)], sems.at[4])

    def finish(r, carry):
        rows = cut(r)
        qv = dot(slot_hot[rows, :], rows_in[...])
        qv_ref[rows, :] = qv.astype(jnp.bfloat16)
        x_ref[rows, :] = (qv * rv_ref[rows, :].astype(jnp.float32)).astype(jnp.bfloat16)
        return carry

    lax.fori_loop(0, nodes // tile, finish, 0)
    drain(ids_in.at[pl.ds(0, devices - 1)], sems.at[0])
    drain(rows_in.at[pl.ds(0, slots - slot_cap)], sems.at[3])


def fetch_rows(owner, qrow, rem, quotient, remainder, devices):
    nodes = owner.shape[0]
    slots = 2 * nodes
    width = quotient.shape[1]
    vmem = pl.BlockSpec(memory_space=pltpu.VMEM)
    rows = jax.ShapeDtypeStruct((nodes, width), jnp.bfloat16)
    return pl.pallas_call(
        functools.partial(fetch_kernel, devices),
        out_shape=(
            rows,
            rows,
            rows,
            jax.ShapeDtypeStruct((1, slots), jnp.int32),
            jax.ShapeDtypeStruct((1, nodes), jnp.int32),
        ),
        in_specs=[vmem] * 5,
        out_specs=(vmem,) * 5,
        scratch_shapes=[
            pltpu.VMEM((devices, 1, devices), jnp.float32),
            pltpu.VMEM((devices, 1, devices), jnp.float32),
            pltpu.VMEM((slots, width), jnp.bfloat16),
            pltpu.VMEM((slots, width), jnp.bfloat16),
            pltpu.VMEM((nodes, 1), jnp.int32),
            pltpu.VMEM((nodes, slots), jnp.bfloat16),
            pltpu.SemaphoreType.DMA((5,)),
        ],
        compiler_params=pltpu.CompilerParams(
            collective_id=1, has_side_effects=True, vmem_limit_bytes=40 << 20
        ),
        name="fetch_rows",
    )(owner, qrow, rem, quotient, remainder)


def spread_kernel(
    devices, rem_scale, scale, grad_ref, qv_ref, rv_ref, slot_ref, node_rem_ref, asked_ref, sums_ref,
    quot_ref, total_ref, weight_ref, bias_ref, grads_ref, rem_ref, by_rv, grads_in, rem_in, sums_in, piece, whole, sems
):
    slot_cap = grads_ref.shape[0] // devices
    slots = grads_ref.shape[0]
    tall, wide = rem_in.shape[1:]
    across = rem_ref.shape[1] // wide
    peers = sums_in.shape[0]
    high = sums_ref.shape[0] - 8
    size = 256
    me = ring_place()
    dom = lax.axis_index("dom")
    blk = lax.axis_index("blk")
    greet_all(devices)

    def cut(r):
        return pl.ds(pl.multiple_of(r * size, size), size)

    by_rv[...] = (grad_ref[...] * qv_ref[...].astype(jnp.float32)).astype(jnp.bfloat16)

    def remain(r, carry):
        rem_ref[cut(r), :] = dot(pick_rows(node_rem_ref[...], r * size, size), by_rv[...]).astype(jnp.bfloat16)
        return carry

    lax.fori_loop(0, rem_ref.shape[0] // size, remain, 0)
    by_rv[...] = (grad_ref[...] * rv_ref[...].astype(jnp.float32)).astype(jnp.bfloat16)
    meet_all(devices)

    def tile(device):
        top = pl.multiple_of(device // across * tall, tall)
        return (pl.ds(top, tall), pl.ds(pl.multiple_of(lax.rem(device, across) * wide, wide), wide))

    def slot(device):
        return pl.ds(pl.multiple_of(device * slot_cap, slot_cap), slot_cap)

    def share(peer):
        top = pl.multiple_of(peer // across * 8, 8)
        return (pl.ds(top, 8), pl.ds(pl.multiple_of(lax.rem(peer, across) * wide, wide), wide))

    def send_rem(k, carry):
        other = lax.rem(me + k, devices)
        send(rem_ref.at[tile(other)], rem_in.at[me], other, sems.at[0], sems.at[1])
        return carry

    def send_sums(k, carry):
        other = lax.rem(blk + k, peers)
        to = dom * peers + other
        send(sums_ref.at[share(other)], sums_in.at[blk, pl.ds(0, 8), :], to, sems.at[7], sems.at[8])
        send(sums_ref.at[pl.ds(high, 8), pl.ds(0, wide)], sums_in.at[blk, pl.ds(8, 8), :], to, sems.at[7], sems.at[8])
        return carry

    step = size // slot_cap

    def send_grads(c, carry):
        turn = lax.rem(c + me // step, devices // step)
        grads_ref[cut(turn), :] = dot(pick_rows(slot_ref[...], turn * size, size), by_rv[...]).astype(jnp.bfloat16)

        def one(i, inner):
            other = turn * step + lax.rem(me + i, step)

            @pl.when(other != me)
            def _():
                send(grads_ref.at[slot(other)], grads_in.at[slot(me)], other, sems.at[2], sems.at[3])

            return inner

        lax.fori_loop(0, step, one, 0)
        return carry

    def send_total(k, carry):
        other = lax.rem(me + k, devices)
        send(piece, whole.at[me], other, sems.at[4], sems.at[5])
        return carry

    def keep(src, dst):
        copy = pltpu.make_async_copy(src, dst, sems.at[6])
        copy.start()
        copy.wait()

    lax.fori_loop(1, peers, send_sums, 0)
    lax.fori_loop(1, devices, send_rem, 0)
    lax.fori_loop(0, devices // step, send_grads, 0)
    keep(rem_ref.at[tile(me)], rem_in.at[me])
    keep(grads_ref.at[slot(me)], grads_in.at[slot(me)])
    keep(sums_ref.at[share(blk)], sums_in.at[blk, pl.ds(0, 8), :])
    keep(sums_ref.at[pl.ds(high, 8), pl.ds(0, wide)], sums_in.at[blk, pl.ds(8, 8), :])
    drain(sums_in.at[pl.ds(0, peers - 1)], sems.at[8])
    drain(rem_in.at[pl.ds(0, devices - 1)], sems.at[1])
    piece[:tall] = (jnp.sum(rem_in[...].astype(jnp.float32), axis=0) * rem_scale).astype(jnp.bfloat16)
    piece[tall:] = (jnp.sum(sums_in[...], axis=0) * scale).astype(jnp.bfloat16)
    lax.fori_loop(1, devices, send_total, 0)
    keep(piece, whole.at[me])
    drain(grads_in.at[pl.ds(0, slots - slot_cap)], sems.at[3])

    def collect(r, carry):
        quot_ref[cut(r), :] = dot(pick_rows(asked_ref[...], r * size, size), grads_in[...])
        return carry

    lax.fori_loop(0, quot_ref.shape[0] // size, collect, 0)
    drain(whole.at[pl.ds(0, devices - 1)], sems.at[5])

    def lay(k, carry):
        for part in range(across):
            got = whole[k * across + part].astype(jnp.float32)
            lanes = slice(part * wide, (part + 1) * wide)
            total_ref[pl.ds(pl.multiple_of(k * tall, tall), tall), lanes] = got[:tall]
            weight_ref[pl.ds(pl.multiple_of(k * 8, 8), 8), lanes] = got[tall : tall + 8]
        return carry

    lax.fori_loop(0, devices // across, lay, 0)
    for d in range(devices // peers):
        bias_ref[d : d + 1, :] = whole[d * peers, tall + 8 : tall + 16, :].astype(jnp.float32)[0:1]
    drain(rem_in.at[pl.ds(0, devices - 1)], sems.at[0])
    drain(grads_in.at[pl.ds(0, slots - slot_cap)], sems.at[2])
    drain(whole.at[pl.ds(0, devices - 1)], sems.at[4])
    drain(sums_in.at[pl.ds(0, peers - 1)], sems.at[7])


def spread_grads(grad, qv, rv, slot_row, rem_row, asked_row, sums, table_rows, rem_rows, peers, rem_scale, scale):
    nodes, width = grad.shape
    slots = asked_row.shape[1]
    doms = lax.axis_size("dom")
    devices = doms * peers
    wide = LANES
    tall = rem_rows * width // devices // wide
    kind = jnp.bfloat16
    vmem = pl.BlockSpec(memory_space=pltpu.VMEM)
    return pl.pallas_call(
        functools.partial(spread_kernel, devices, rem_scale, scale),
        out_shape=(
            jax.ShapeDtypeStruct((table_rows, width), jnp.float32),
            jax.ShapeDtypeStruct((rem_rows, width), jnp.float32),
            jax.ShapeDtypeStruct((doms * (sums.shape[0] - 8), width), jnp.float32),
            jax.ShapeDtypeStruct((doms, wide), jnp.float32),
        ),
        in_specs=[vmem] * 7,
        out_specs=(vmem, vmem, vmem, vmem),
        scratch_shapes=[
            pltpu.VMEM((slots, width), kind),
            pltpu.VMEM((rem_rows, width), kind),
            pltpu.VMEM((nodes, width), kind),
            pltpu.VMEM((slots, width), kind),
            pltpu.VMEM((devices, tall, wide), kind),
            pltpu.VMEM((peers, 16, wide), jnp.float32),
            pltpu.VMEM((tall + 16, wide), kind),
            pltpu.VMEM((devices, tall + 16, wide), kind),
            pltpu.SemaphoreType.DMA((9,)),
        ],
        compiler_params=pltpu.CompilerParams(
            collective_id=2, has_side_effects=True, vmem_limit_bytes=40 << 20
        ),
        name="spread_grads",
    )(grad, qv, rv, slot_row, rem_row, asked_row, sums)


def forward_kernel(
    counts_ref, rows_ref, halo_counts_ref, halo_rows_ref, deg_ref, x_ref, w_self_ref, w_neigh_ref, bias_ref, cot_ref,
    out_ref, grad_ref, halo_ref, dx_ref, weights_ref, total, acc_self, acc_neigh
):
    k = pl.program_id(0)
    nodes, feats = total.shape
    tile = 256

    def cut(r):
        return pl.ds(pl.multiple_of(r * tile, tile), tile)

    @pl.when(k == 0)
    def _():
        def start(r, carry):
            total[cut(r), :] = dot(halo_counts_ref[cut(r), :], halo_rows_ref[...])
            return carry

        lax.fori_loop(0, nodes // tile, start, 0)

    total[...] += dot(counts_ref[...], rows_ref[...])

    @pl.when(k == pl.num_programs(0) - 1)
    def _():
        acc_self[...] = jnp.zeros_like(acc_self)
        acc_neigh[...] = jnp.zeros_like(acc_neigh)

        def layer(r, bias_sum):
            rows = cut(r)
            divisor = jnp.maximum(deg_ref[rows, :], 1.0)
            x = x_ref[rows, :]
            neighbour = (total[rows, :] / divisor).astype(jnp.bfloat16)
            preact = dot(x, w_self_ref[...]) + dot(neighbour, w_neigh_ref[...]) + bias_ref[...]
            sigma = jax.nn.sigmoid(preact)
            out_ref[rows, :] = (preact * sigma).astype(jnp.bfloat16)
            slope = sigma * (1.0 + preact * (1.0 - sigma))
            dpre = (cot_ref[rows, :].astype(jnp.float32) * slope).astype(jnp.bfloat16)
            scaled = dot(dpre, w_neigh_ref[...], COLS) / divisor
            grad_ref[:, rows] = scaled.T.astype(jnp.bfloat16)
            dx_ref[rows, :] = dot(dpre, w_self_ref[...], COLS)
            acc_self[...] += dot(x, dpre, ROWS)
            acc_neigh[...] += dot(neighbour, dpre, ROWS)
            return bias_sum + jnp.sum(dpre.astype(jnp.float32), axis=0, keepdims=True)

        bias_sum = lax.fori_loop(0, nodes // tile, layer, jnp.zeros((1, feats), jnp.float32))
        halo_ref[...] = dot(grad_ref[...], halo_counts_ref[...]).T.astype(jnp.bfloat16)
        doms = weights_ref.shape[0]
        each = 2 * feats // doms
        wide = feats // doms
        spread = jnp.broadcast_to(bias_sum, (8, feats))
        for c in range(doms):
            source, at = (acc_self, c * each) if c * each < feats else (acc_neigh, c * each - feats)
            weights_ref[c, :each, :] = source[at : at + each, :]
            shift = (feats - c * wide) % feats
            weights_ref[c, each:, :] = pltpu.roll(spread, shift, 1) if shift else spread


def forward(counts, gathered, halo_counts, halo_rows, degree, features, w_self, w_neigh, bias, cotangent, doms):
    nodes, feats = features.shape
    wide = 4 * nodes
    steps = counts.shape[1] // wide

    def whole(array):
        return pl.BlockSpec(array.shape, lambda k: (0,) * len(array.shape))

    out_shape = (
        jax.ShapeDtypeStruct((nodes, feats), jnp.bfloat16),
        jax.ShapeDtypeStruct((feats, nodes), jnp.bfloat16),
        jax.ShapeDtypeStruct(halo_rows.shape, jnp.bfloat16),
        jax.ShapeDtypeStruct((nodes, feats), jnp.float32),
        jax.ShapeDtypeStruct((doms, 2 * feats // doms + 8, feats), jnp.float32),
    )
    kept = (halo_counts, halo_rows, degree, features, w_self, w_neigh, bias, cotangent)
    return pl.pallas_call(
        forward_kernel,
        grid=(steps,),
        out_shape=out_shape,
        in_specs=[
            pl.BlockSpec((nodes, wide), lambda k: (0, k)),
            pl.BlockSpec((wide, feats), lambda k: (k, 0)),
        ]
        + [whole(array) for array in kept],
        out_specs=tuple(whole(array) for array in out_shape),
        scratch_shapes=[
            pltpu.VMEM((nodes, feats), jnp.float32),
            pltpu.VMEM((feats, feats), jnp.float32),
            pltpu.VMEM((feats, feats), jnp.float32),
        ],
        compiler_params=pltpu.CompilerParams(vmem_limit_bytes=58 << 20),
        name="forward_layer",
    )(counts, gathered, *kept)


def reduce_kernel(
    counts_ref, grad_ref, weights_ref, halo_ref, dx_ref, out_ref, sums_ref, load, part, mid, fin, half_sum, mid2, fin2, sems_load, s_out, s_mid, s_fin, t_out, t_mid, t_fin, weights_in, w_out, w_in, halo_in, own, h_out, h_in
):
    side = 4
    nodes = grad_ref.shape[1]
    feats = grad_ref.shape[0] // 2
    span = nodes // 2
    dom = lax.axis_index("dom")
    blk = lax.axis_index("blk")
    x, y = blk // side, lax.rem(blk, side)

    def at(dx, dy):
        return lax.rem(x + dx, side) * side + lax.rem(y + dy, side)

    def device(half, first, second):
        dx, dy = (first, second) if half == 0 else (second, first)
        return (dom, at(dx, dy))

    barrier = pltpu.get_barrier_semaphore()
    for dx, dy in ((1, 0), (3, 0), (0, 1), (0, 3)):
        pl.semaphore_signal(barrier, inc=1, device_id=(dom, at(dx, dy)), device_id_type=MESH)
    doms = weights_ref.shape[0]
    for k in range(1, doms):
        pl.semaphore_signal(barrier, inc=1, device_id=(lax.rem(dom + k, doms), blk), device_id_type=MESH)

    order = [(2, 2), (2, 1), (1, 2), (2, 3), (3, 2), (2, 0), (0, 2), (1, 1), (3, 3), (1, 3), (3, 1)]
    order += [(1, 0), (0, 1), (3, 0), (0, 3), (0, 0)]
    depth = load.shape[0]

    def fetch(i):
        dx, dy = order[i]
        columns = pl.ds(pl.multiple_of(at(dx, dy) * nodes, nodes), nodes)
        return pltpu.make_async_copy(counts_ref.at[:, columns], load.at[i % depth], sems_load.at[i % depth])

    for i in range(depth - 1):
        fetch(i).start()
    pl.semaphore_wait(barrier, 4 + doms - 1)

    def to_dom(k):
        other = lax.rem(dom + k, doms)
        return pltpu.make_async_remote_copy(
            src_ref=weights_ref.at[other],
            dst_ref=weights_in.at[k],
            send_sem=w_out.at[k],
            recv_sem=w_in.at[k],
            device_id=(other, blk),
            device_id_type=MESH,
        )

    halo = halo_in.shape[1]

    def to_side(side_index):
        return pltpu.make_async_remote_copy(
            src_ref=halo_ref.at[pl.ds(side_index * halo, halo)],
            dst_ref=halo_in.at[side_index],
            send_sem=h_out.at[side_index],
            recv_sem=h_in.at[side_index],
            device_id=(lax.rem(dom + (doms - 1 if side_index == 0 else 1), doms), blk),
            device_id_type=MESH,
        )

    for k in range(1, doms):
        to_dom(k).start()
    to_side(0).start()
    to_side(1).start()

    def remote(src, dst, half, first, second, send_sem, recv_sem):
        return pltpu.make_async_remote_copy(
            src_ref=src,
            dst_ref=dst,
            send_sem=send_sem,
            recv_sem=recv_sem,
            device_id=device(half, first, second),
            device_id_type=MESH,
        )

    def along(unit):
        return unit % 2 == 0

    def to_mid(half, unit):
        return remote(
            part.at[half, 2, unit], mid.at[half, unit], half, 1 if along(unit) else 3, 0,
            s_out.at[half, 0, unit], s_mid.at[half, unit],
        )

    def to_fin(half, first, unit):
        way = 0 if first == 1 else 1
        return remote(
            part.at[half, first, unit], fin.at[half, way, unit], half, first, 0,
            s_out.at[half, 1 + way, unit], s_fin.at[half, way, unit],
        )

    def relays(first, unit):
        return along(unit) == (first == 1)

    tile = 256
    waiting = []
    for i, (dx, dy) in enumerate(order):
        if i + depth - 1 < len(order):
            fetch(i + depth - 1).start()
        fetch(i).wait()

        def columns(n, carry, slot=i % depth, dx=dx, dy=dy):
            cut = pl.ds(pl.multiple_of(n * tile, tile), tile)
            value = jnp.dot(grad_ref[...], load[slot, :, cut], preferred_element_type=jnp.float32)
            part[0, dx, dy, :, cut] = value[:feats].astype(jnp.bfloat16)
            part[1, dy, dx, :, cut] = value[feats:].astype(jnp.bfloat16)
            return carry

        lax.fori_loop(0, nodes // tile, columns, 0)
        for half, first, unit in ((0, dx, dy), (1, dy, dx)):
            if first == 2:
                to_mid(half, unit).start()
            elif first != 0:
                if relays(first, unit):
                    waiting.append((half, first, unit))
                else:
                    to_fin(half, first, unit).start()
    waiting.sort(key=lambda item: (2, 1, 3, 0).index(item[2]))
    for half, first, unit in waiting:
        to_mid(half, unit).wait_recv()
        mine = part[half, first, unit].astype(jnp.float32)
        part[half, first, unit] = (mine + mid[half, unit].astype(jnp.float32)).astype(jnp.bfloat16)
        to_fin(half, first, unit).start()

    def cut(piece):
        return pl.ds(piece * span, span)

    def to_mid2(half, piece):
        return remote(
            half_sum.at[half, 1, :, cut(piece)], mid2.at[half, piece], half, 0, 1 if piece == 0 else 3,
            t_out.at[half, 0, piece], t_mid.at[half, piece],
        )

    def to_fin2(half, second, piece):
        way = 0 if second == 1 else 1
        return remote(
            half_sum.at[half, 0 if second == 1 else 2, :, cut(piece)], fin2.at[half, way, piece], half, 0, second,
            t_out.at[half, 1 + way, piece], t_fin.at[half, way, piece],
        )

    def summed(half, unit):
        to_fin(half, 1, unit).wait_recv()
        to_fin(half, 3, unit).wait_recv()
        total = part[half, 0, unit].astype(jnp.float32) + fin[half, 0, unit].astype(jnp.float32)
        return total + fin[half, 1, unit].astype(jnp.float32)

    for half in range(2):
        half_sum[half, 1] = summed(half, 2).astype(jnp.bfloat16)
        to_mid2(half, 0).start()
        to_mid2(half, 1).start()
    for second in (1, 3):
        direct, relayed = (1, 0) if second == 1 else (0, 1)
        for half in range(2):
            half_sum[half, second - 1] = summed(half, second).astype(jnp.bfloat16)
            to_fin2(half, second, direct).start()
    for second in (1, 3):
        direct, relayed = (1, 0) if second == 1 else (0, 1)
        for half in range(2):
            to_mid2(half, relayed).wait_recv()
            mine = half_sum[half, second - 1, :, cut(relayed)].astype(jnp.float32)
            both = mine + mid2[half, relayed].astype(jnp.float32)
            half_sum[half, second - 1, :, cut(relayed)] = both.astype(jnp.bfloat16)
            to_fin2(half, second, relayed).start()
    for half in range(2):
        own[half * feats : (half + 1) * feats, :] = summed(half, 0)
    to_side(0).wait_recv()
    to_side(1).wait_recv()
    for half in range(2):
        rows = slice(half * feats, (half + 1) * feats)
        for piece in range(2):
            to_fin2(half, 1, piece).wait_recv()
            to_fin2(half, 3, piece).wait_recv()
            total = own[rows, piece * span : (piece + 1) * span] + fin2[half, 0, piece].astype(jnp.float32)
            total = (total + fin2[half, 1, piece].astype(jnp.float32)).T
            near = slice(piece * span, (piece + 1) * span)
            out_ref[near, rows] = dx_ref[near, rows] + total
            edge = slice(0, halo) if piece == 0 else slice(nodes - halo, nodes)
            out_ref[edge, rows] += halo_in[1 - piece, :, rows].astype(jnp.float32)
    to_side(0).wait_send()
    to_side(1).wait_send()
    sums = weights_ref[dom]
    for k in range(1, doms):
        to_dom(k).wait_recv()
        sums = sums + weights_in[k]
    sums_ref[...] = sums
    for k in range(1, doms):
        to_dom(k).wait_send()
    for half in range(2):
        for unit in range(side):
            to_mid(half, unit).wait_send()
            to_fin(half, 1, unit).wait_send()
            to_fin(half, 3, unit).wait_send()
        for piece in range(2):
            to_mid2(half, piece).wait_send()
            to_fin2(half, 1, piece).wait_send()
            to_fin2(half, 3, piece).wait_send()


def reduce_sources(counts, grad, weights, halo, dx):
    feats, nodes = grad.shape
    half = feats // 2
    kind = jnp.bfloat16
    dma = pltpu.SemaphoreType.DMA
    vmem = pl.BlockSpec(memory_space=pltpu.VMEM)
    return pl.pallas_call(
        reduce_kernel,
        out_shape=(
            jax.ShapeDtypeStruct((nodes, feats), jnp.float32),
            jax.ShapeDtypeStruct(weights.shape[1:], jnp.float32),
        ),
        in_specs=[pl.BlockSpec(memory_space=pl.ANY), vmem, vmem, vmem, vmem],
        out_specs=(vmem, vmem),
        scratch_shapes=[
            pltpu.VMEM((3, nodes, nodes), kind),
            pltpu.VMEM((2, 4, 4, half, nodes), kind),
            pltpu.VMEM((2, 4, half, nodes), kind),
            pltpu.VMEM((2, 2, 4, half, nodes), kind),
            pltpu.VMEM((2, 3, half, nodes), kind),
            pltpu.VMEM((2, 2, half, nodes // 2), kind),
            pltpu.VMEM((2, 2, 2, half, nodes // 2), kind),
            dma((3,)),
            dma((2, 3, 4)),
            dma((2, 4)),
            dma((2, 2, 4)),
            dma((2, 3, 2)),
            dma((2, 2)),
            dma((2, 2, 2)),
            pltpu.VMEM(weights.shape, jnp.float32),
            dma((weights.shape[0],)),
            dma((weights.shape[0],)),
            pltpu.VMEM((2, halo.shape[0] // 2, feats), kind),
            pltpu.VMEM((feats, nodes), jnp.float32),
            dma((2,)),
            dma((2,)),
        ],
        compiler_params=pltpu.CompilerParams(
            collective_id=3, has_side_effects=True, vmem_limit_bytes=48 << 20
        ),
        name="reduce_sources",
    )(counts, grad, weights, halo, dx)


def shifted(block, axis, distance):
    devices = range(lax.axis_size(axis))
    route = [((i - distance) % len(devices), i) for i in devices]
    return lax.ppermute(block, axis, route)


def dot(a, b, dims=(((1,), (0,)), ((), ()))):
    return lax.dot_general(a, b, dims, preferred_element_type=jnp.float32)


def per_device(
    node_owner,
    node_qrow,
    node_rem,
    quotient,
    remainder,
    edge_src,
    edge_dst,
    block_count,
    w_self,
    w_neigh,
    bias,
    cotangent,
):
    nodes_dev = node_qrow.shape[0]
    feature_dim = quotient.shape[1]
    devices = lax.axis_size("dom") * lax.axis_size("blk")
    part_nodes = nodes_dev * lax.axis_size("blk")
    doms = lax.axis_size("dom")
    features, quot_rows, remain_rows, asked_row, slot_row = fetch_rows(
        node_owner, node_qrow[:, None], node_rem[:, None], quotient, remainder, devices
    )
    part_gathered = lax.all_gather(features, "blk", axis=0, tiled=True)
    low_rows = shifted(features[nodes_dev - HALO :], "dom", 1)
    high_rows = shifted(features[:HALO], "dom", -1)
    halo_rows = jnp.concatenate([low_rows, high_rows], axis=0)

    counts, halo_counts, degree = build_counts(edge_src, edge_dst, block_count, part_nodes)
    out, grad_t, halo_grads, dx_self, weights = forward(
        counts, part_gathered, halo_counts, halo_rows, degree, features, w_self, w_neigh, bias[None], cotangent, doms
    )
    grad_x, weight_sums = reduce_sources(counts, grad_t, weights, halo_grads, dx_self)
    nodes_total = nodes_dev * devices
    weight_scale = 1.0 / math.sqrt(nodes_total)
    remain_scale = math.sqrt(remainder.shape[0] / nodes_total)
    d_quotient, d_remainder, d_weights, d_bias = spread_grads(
        grad_x,
        quot_rows,
        remain_rows,
        slot_row,
        node_rem[None],
        asked_row,
        weight_sums,
        quotient.shape[0],
        remainder.shape[0],
        lax.axis_size("blk"),
        remain_scale,
        weight_scale,
    )
    d_self, d_neigh = d_weights[:feature_dim], d_weights[feature_dim:]
    d_bias = d_bias[:, : feature_dim // doms].reshape(-1)
    return (out, d_quotient, d_remainder, d_self, d_neigh, d_bias)


def solution(mesh):
    both = P(AXES)
    rows = P(AXES, None)
    return jax.shard_map(
        per_device,
        mesh=mesh,
        in_specs=(rows, both, both, rows, P(), rows, rows, both, P(), P(), P(), rows),
        out_specs=(rows, rows, P(), P(), P(), P()),
        check_vma=False,
    )
```

```python
import functools
import math

import jax
import jax.numpy as jnp
from jax import lax
from jax.experimental import pallas as pl
from jax.experimental.pallas import tpu as pltpu
from jax.sharding import PartitionSpec as P

ROWS_BLK = 128
HALO = 256
LANES = 128
BATCH = 8
AXES = ("dom", "blk")
MESH = pl.DeviceIdType.MESH
ROWS = (((0,), (0,)), ((), ()))
COLS = (((1,), (1,)), ((), ()))


def place_edges(dump, src_ref, dst_ref, counts, fast_ref, slow_ref, flag_ref):
    blocks, slots = src_ref.shape
    src = src_ref[...]
    lane = lax.broadcasted_iota(jnp.int32, (blocks, slots), 1)
    cell = ((src >> 7) * ROWS_BLK + dst_ref[...]) * LANES + (src & 127)
    live = lane < counts
    spare = dump * LANES
    cell = jnp.where(live, cell, spare)
    row = cell >> 7
    clash = jnp.zeros((blocks, slots), jnp.bool_)
    place = lane & (BATCH - 1)
    for s in range(1, BATCH):
        clash = clash | ((pltpu.roll(row, s, 1) == row) & (place >= s))
    clash = clash & live
    fast_ref[...] = jnp.where(clash, spare, cell)
    slow_ref[...] = jnp.where(clash, cell, spare)
    ones = jnp.where(clash, 1.0, 0.0).astype(jnp.bfloat16)
    chunks = slots // LANES
    col = lax.broadcasted_iota(jnp.int32, (blocks, LANES), 1)
    into = lax.broadcasted_iota(jnp.int32, (LANES, LANES), 0) // BATCH
    group = (into == lax.broadcasted_iota(jnp.int32, (LANES, LANES), 1)).astype(jnp.bfloat16)
    found = jnp.zeros((blocks, LANES), jnp.int32)
    number = jnp.zeros((blocks, 1), jnp.int32)
    for c in range(chunks):
        hits = jnp.dot(ones[:, c * LANES : (c + 1) * LANES], group, preferred_element_type=jnp.float32)
        bits = jnp.sum(jnp.where(hits > 0.5, (1 << (col & (LANES // BATCH - 1))).astype(jnp.float32), 0.0), axis=1, keepdims=True)
        bits = bits.astype(jnp.int32)
        some = bits > 0
        found = found + jnp.where((col == number) & some, c * 65536 + bits, 0)
        number = number + some.astype(jnp.int32)
    flag_ref[...] = jnp.where(col == LANES - 1, number, found)


def count_kernel(dump, count_ref, fast_ref, slow_ref, flag_ref, main_ref, halo_ref, deg_ref, *cells):
    j = pl.program_id(0)
    blocks = pl.num_programs(0) - 1
    his = dump // ROWS_BLK
    his_main = main_ref.shape[1] // LANES
    zero = jnp.zeros((ROWS_BLK, LANES), jnp.float32)
    lanes = lax.broadcasted_iota(jnp.int32, (1, LANES), 1)

    @pl.when(j == 0)
    def _():
        def clear(i, carry):
            for ref in cells[:2]:
                ref[pl.ds(pl.multiple_of(i * ROWS_BLK, ROWS_BLK), ROWS_BLK), :] = zero
            return carry

        lax.fori_loop(0, his, clear, 0)
        for ref in cells:
            ref[pl.ds(dump, 8), :] = jnp.zeros((8, LANES), jnp.float32)

    count = jnp.where(j < blocks, count_ref[jnp.minimum(j, blocks - 1)], 0)
    pairs = (count + 2 * BATCH - 1) // (2 * BATCH)

    def add_batch(ref, first):
        keys = [fast_ref[0, 0, first + i] for i in range(BATCH)]
        rows = [k >> 7 for k in keys]
        olds = [ref[pl.ds(r, 1), :] for r in rows]
        news = [old + jnp.where(lanes == (k & 127), 1.0, 0.0) for old, k in zip(olds, keys)]
        for r, new in zip(rows, news):
            ref[pl.ds(r, 1), :] = new

    def turn(fill, leave):
        def add_pair(t, carry):
            add_batch(fill[0], t * 2 * BATCH)
            add_batch(fill[1], t * 2 * BATCH + BATCH)
            return carry

        def flush(ref, first):
            def step(h, total):
                at = pl.multiple_of((first + h) * ROWS_BLK, ROWS_BLK)
                rows = pl.ds(at, ROWS_BLK)
                value = leave[0][rows, :] + leave[1][rows, :]
                ref[:, pl.ds(pl.multiple_of(h * LANES, LANES), LANES)] = value.astype(jnp.bfloat16)
                leave[0][rows, :] = zero
                leave[1][rows, :] = zero
                return total + value

            return step

        def both(t, total):
            add_pair(t, 0)
            return flush(main_ref, 0)(t, total)

        steps = his_main
        joint = jnp.minimum(pairs, steps)
        total = lax.fori_loop(0, joint, both, zero)
        lax.fori_loop(joint, pairs, add_pair, 0)
        total = lax.fori_loop(joint, steps, flush(main_ref, 0), total)

        total = lax.fori_loop(0, his - his_main, flush(halo_ref, his_main), total)
        deg_ref[...] = jnp.sum(total, axis=1, keepdims=True)

        def chunk(c, carry):
            entry = flag_ref[0, 0, c]
            first = (entry >> 16) * LANES

            def some(g, inner):
                @pl.when(((entry >> g) & 1) != 0)
                def _():
                    for i in range(BATCH):
                        k = slow_ref[0, 0, first + g * BATCH + i]
                        r = k >> 7
                        old = fill[0][pl.ds(r, 1), :]
                        fill[0][pl.ds(r, 1), :] = old + jnp.where(lanes == (k & 127), 1.0, 0.0)

                return inner

            lax.fori_loop(0, LANES // BATCH, some, 0)
            return carry

        lax.fori_loop(0, jnp.where(j < blocks, flag_ref[0, 0, LANES - 1], 0), chunk, 0)

    @pl.when(lax.rem(j, 2) == 0)
    def _():
        turn(cells[:2], cells[2:])

    @pl.when(lax.rem(j, 2) == 1)
    def _():
        turn(cells[2:], cells[:2])


def build_counts(fast, slow, flags, block_count, part_nodes):
    blocks, slots = fast.shape
    width = part_nodes + 2 * HALO
    dump = width // LANES * ROWS_BLK
    nodes = blocks * ROWS_BLK

    def filled(j):
        return (jnp.minimum(j, blocks - 1), 0, 0)

    def left(j):
        return (jnp.maximum(j - 1, 0), 0)

    return pl.pallas_call(
        functools.partial(count_kernel, dump),
        grid=(blocks + 1,),
        out_shape=(
            jax.ShapeDtypeStruct((nodes, part_nodes), jnp.bfloat16),
            jax.ShapeDtypeStruct((nodes, 2 * HALO), jnp.bfloat16),
            jax.ShapeDtypeStruct((nodes, 1), jnp.float32),
        ),
        in_specs=[
            pl.BlockSpec(memory_space=pltpu.SMEM),
            pl.BlockSpec((1, 1, slots), filled, memory_space=pltpu.SMEM),
            pl.BlockSpec((1, 1, slots), filled, memory_space=pltpu.SMEM),
            pl.BlockSpec((1, 1, LANES), filled, memory_space=pltpu.SMEM),
        ],
        out_specs=(
            pl.BlockSpec((ROWS_BLK, part_nodes), left),
            pl.BlockSpec((ROWS_BLK, 2 * HALO), left),
            pl.BlockSpec((ROWS_BLK, 1), left),
        ),
        scratch_shapes=[pltpu.VMEM((dump + 8, LANES), jnp.float32)] * 4,
        compiler_params=pltpu.CompilerParams(vmem_limit_bytes=60 << 20),
        cost_estimate=pl.CostEstimate(flops=80_000_000_000, bytes_accessed=40_000_000, transcendentals=0),
        name="edge_counts",
    )(block_count, fast[:, None], slow[:, None], flags[:, None])


def ring_place():
    blk = lax.axis_size("blk")
    return lax.axis_index("dom") * blk + lax.axis_index("blk")


def greet_all(devices):
    me = ring_place()

    def greet(k, carry):
        other = lax.rem(me + k, devices)
        barrier = pltpu.get_barrier_semaphore()
        pl.semaphore_signal(barrier, inc=1, device_id=coords(other), device_id_type=MESH)
        return carry

    lax.fori_loop(1, devices, greet, 0)


def meet_all(devices):
    pl.semaphore_wait(pltpu.get_barrier_semaphore(), devices - 1)


def as_row(column):
    wide = jnp.broadcast_to(column.astype(jnp.float32), (column.shape[0], LANES))
    return wide.T[0:1].astype(jnp.int32)


def as_column(row):
    tall = jnp.broadcast_to(row.astype(jnp.float32), (LANES, row.shape[1]))
    return tall.T[:, 0:1].astype(jnp.int32)


def pick(column, first, size):
    lane = lax.broadcasted_iota(jnp.int32, (column.shape[0], size), 1) + first
    return (lane == column).astype(jnp.bfloat16)


def pick_rows(row, first, size):
    line = lax.broadcasted_iota(jnp.int32, (size, row.shape[1]), 0) + first
    return (line == row).astype(jnp.bfloat16)


def coords(device):
    blk = lax.axis_size("blk")
    return (device // blk, lax.rem(device, blk))


def send(src, dst, device, send_sem, recv_sem):
    pltpu.make_async_remote_copy(
        src_ref=src,
        dst_ref=dst,
        send_sem=send_sem,
        recv_sem=recv_sem,
        device_id=coords(device),
        device_id_type=MESH,
    ).start()


def drain(ref, sem):
    pltpu.make_async_copy(ref, ref, sem).wait()


def fetch_kernel(
    devices, dump, owner_row, qrow_row, rem_row, table_hbm, remainder_hbm, src_hbm, dst_hbm, count_ref,
    x_ref, qv_ref, rv_ref, asked_ref, slot_ref, fast_ref, slow_ref, flag_ref,
    ids_out, ids_in, served, rows_in, slot_col, slot_hot, owner_ref, qrow_ref, rem_ref, table_ref, remainder_ref,
    src_ref, dst_ref, sems
):
    slots, width = served.shape
    slot_cap = slots // devices
    nodes = owner_ref.shape[0]
    me = ring_place()
    tile = 256
    greet_all(devices)
    loads = [
        pltpu.make_async_copy(table_hbm, table_ref, sems.at[5]),
        pltpu.make_async_copy(remainder_hbm, remainder_ref, sems.at[6]),
        pltpu.make_async_copy(src_hbm, src_ref, sems.at[7]),
        pltpu.make_async_copy(dst_hbm, dst_ref, sems.at[8]),
    ]
    for load in loads:
        load.start()

    def cut(r):
        return pl.ds(pl.multiple_of(r * tile, tile), tile)

    owner_ref[...] = as_column(owner_row[...])
    qrow_ref[...] = as_column(qrow_row[...])
    rem_ref[...] = as_column(rem_row[...])

    owner_hot = pick(owner_ref[...], 0, devices)
    lane = lax.broadcasted_iota(jnp.int32, (tile, devices), 1)
    wish = jnp.zeros((devices, devices), jnp.float32)
    for r in range(nodes // tile):
        rows = slice(r * tile, (r + 1) * tile)
        line = lax.broadcasted_iota(jnp.int32, (tile, nodes), 0) + r * tile
        before = (line > lax.broadcasted_iota(jnp.int32, (tile, nodes), 1)).astype(jnp.bfloat16)
        mine = owner_hot[rows]
        rank = jnp.sum(dot(before, owner_hot) * mine.astype(jnp.float32), axis=1, keepdims=True).astype(jnp.int32)
        slot_col[rows, :] = owner_ref[rows, :] * slot_cap + rank
        qrow = qrow_ref[rows, :]
        parts = jnp.where(lane == rank, qrow >> 5, 0) + jnp.where(lane == rank + slot_cap, qrow & 31, 0)
        wish = wish + dot(mine, parts.astype(jnp.float32).astype(jnp.bfloat16), ROWS)
    ids_out[:, 0, :] = wish
    meet_all(devices)

    def ask(k, carry):
        other = lax.rem(me + k, devices)
        send(ids_out.at[other], ids_in.at[me], other, sems.at[0], sems.at[1])
        return carry

    lax.fori_loop(1, devices, ask, 0)
    loads[1].wait()

    def remain(r, carry):
        rows = cut(r)
        rv_ref[rows, :] = dot(pick(rem_ref[rows, :], 0, remainder_ref.shape[0]), remainder_ref[...]).astype(jnp.bfloat16)
        return carry

    lax.fori_loop(0, nodes // tile, remain, 0)
    slot_ref[...] = as_row(slot_col[...])
    own = pltpu.make_async_copy(ids_out.at[me], ids_in.at[me], sems.at[2])
    own.start()
    own.wait()
    loads[0].wait()
    drain(ids_in.at[pl.ds(0, devices - 1)], sems.at[1])
    ids = ids_in[:, 0, :].astype(jnp.bfloat16)
    step = 16
    part = step * slot_cap
    slot = lax.broadcasted_iota(jnp.int32, (part, devices), 0)
    place = lax.broadcasted_iota(jnp.int32, (part, devices), 1)
    rank_of = lax.rem(slot, slot_cap)
    weight = jnp.where(place == rank_of, 32.0, 0.0) + jnp.where(place == rank_of + slot_cap, 1.0, 0.0)

    def serve(c, carry):
        turn = lax.rem(c + me // step, devices // step)
        whose = (place - turn * step == slot // slot_cap).astype(jnp.bfloat16)
        asked = jnp.sum(dot(whose, ids) * weight, axis=1, keepdims=True).astype(jnp.int32)
        at = pl.multiple_of(turn * part, part)
        asked_ref[:, pl.ds(at, part)] = as_row(asked)
        served[pl.ds(at, part), :] = dot(pick(asked, 0, table_ref.shape[0]), table_ref[...]).astype(jnp.bfloat16)

        def back(i, inner):
            other = turn * step + lax.rem(me + i, step)

            @pl.when(other != me)
            def _():
                send(
                    served.at[pl.ds(pl.multiple_of(other * slot_cap, slot_cap), slot_cap)],
                    rows_in.at[pl.ds(pl.multiple_of(me * slot_cap, slot_cap), slot_cap)],
                    other,
                    sems.at[3],
                    sems.at[4],
                )

            return inner

        lax.fori_loop(0, step, back, 0)
        return carry

    lax.fori_loop(0, devices // step, serve, 0)
    mine = pl.ds(pl.multiple_of(me * slot_cap, slot_cap), slot_cap)
    own_rows = pltpu.make_async_copy(served.at[mine], rows_in.at[mine], sems.at[2])
    own_rows.start()

    def prepare(r, carry):
        slot_hot[cut(r), :] = pick(slot_col[cut(r), :], 0, slots)
        return carry

    lax.fori_loop(0, nodes // tile, prepare, 0)
    loads[2].wait()
    loads[3].wait()
    blocks = src_ref.shape[0]
    which = lax.broadcasted_iota(jnp.int32, (blocks, 1), 0)
    counts = jnp.zeros((blocks, 1), jnp.int32)
    for j in range(blocks):
        counts = counts + jnp.where(which == j, count_ref[j], 0)
    place_edges(dump, src_ref, dst_ref, counts, fast_ref, slow_ref, flag_ref)
    own_rows.wait()
    drain(rows_in.at[pl.ds(0, slots - slot_cap)], sems.at[4])

    def finish(r, carry):
        rows = cut(r)
        qv = dot(slot_hot[rows, :], rows_in[...])
        qv_ref[rows, :] = qv.astype(jnp.bfloat16)
        x_ref[rows, :] = (qv * rv_ref[rows, :].astype(jnp.float32)).astype(jnp.bfloat16)
        return carry

    lax.fori_loop(0, nodes // tile, finish, 0)
    drain(ids_in.at[pl.ds(0, devices - 1)], sems.at[0])
    drain(rows_in.at[pl.ds(0, slots - slot_cap)], sems.at[3])


def fetch_rows(owner, qrow, rem, quotient, remainder, edge_src, edge_dst, block_count, devices, part_nodes):
    nodes = owner.shape[1]
    slots = 2 * nodes
    width = quotient.shape[1]
    vmem = pl.BlockSpec(memory_space=pltpu.VMEM)
    anywhere = pl.BlockSpec(memory_space=pl.ANY)
    rows = jax.ShapeDtypeStruct((nodes, width), jnp.bfloat16)
    edge = jax.ShapeDtypeStruct(edge_src.shape, jnp.int32)
    dump = (part_nodes + 2 * HALO) // LANES * ROWS_BLK
    column = pltpu.VMEM((nodes, 1), jnp.int32)
    return pl.pallas_call(
        functools.partial(fetch_kernel, devices, dump),
        out_shape=(
            rows,
            rows,
            rows,
            jax.ShapeDtypeStruct((1, slots), jnp.int32),
            jax.ShapeDtypeStruct((1, nodes), jnp.int32),
            edge,
            edge,
            jax.ShapeDtypeStruct((edge_src.shape[0], LANES), jnp.int32),
        ),
        in_specs=[vmem] * 3 + [anywhere] * 4 + [pl.BlockSpec(memory_space=pltpu.SMEM)],
        out_specs=(vmem,) * 8,
        scratch_shapes=[
            pltpu.VMEM((devices, 1, devices), jnp.float32),
            pltpu.VMEM((devices, 1, devices), jnp.float32),
            pltpu.VMEM((slots, width), jnp.bfloat16),
            pltpu.VMEM((slots, width), jnp.bfloat16),
            column,
            pltpu.VMEM((nodes, slots), jnp.bfloat16),
            column,
            column,
            column,
            pltpu.VMEM(quotient.shape, jnp.bfloat16),
            pltpu.VMEM(remainder.shape, jnp.bfloat16),
            pltpu.VMEM(edge_src.shape, jnp.int32),
            pltpu.VMEM(edge_src.shape, jnp.int32),
            pltpu.SemaphoreType.DMA((9,)),
        ],
        compiler_params=pltpu.CompilerParams(
            collective_id=1, has_side_effects=True, vmem_limit_bytes=60 << 20
        ),
        name="fetch_rows",
    )(owner, qrow, rem, quotient, remainder, edge_src, edge_dst, block_count)


def spread_kernel(
    devices, rem_scale, scale, grad_ref, qv_ref, rv_ref, slot_ref, node_rem_ref, asked_ref, sums_ref,
    quot_ref, total_ref, weight_ref, bias_ref, grads_ref, rem_ref, by_rv, grads_in, rem_in, sums_in, piece, whole, sems
):
    slot_cap = grads_ref.shape[0] // devices
    slots = grads_ref.shape[0]
    tall, wide = rem_in.shape[1:]
    across = rem_ref.shape[1] // wide
    peers = sums_in.shape[0]
    high = sums_ref.shape[0] - 8
    size = 256
    me = ring_place()
    dom = lax.axis_index("dom")
    blk = lax.axis_index("blk")
    greet_all(devices)

    def cut(r):
        return pl.ds(pl.multiple_of(r * size, size), size)

    by_rv[...] = (grad_ref[...] * qv_ref[...].astype(jnp.float32)).astype(jnp.bfloat16)

    def remain(r, carry):
        rem_ref[cut(r), :] = dot(pick_rows(node_rem_ref[...], r * size, size), by_rv[...]).astype(jnp.bfloat16)
        return carry

    lax.fori_loop(0, rem_ref.shape[0] // size, remain, 0)
    by_rv[...] = (grad_ref[...] * rv_ref[...].astype(jnp.float32)).astype(jnp.bfloat16)
    meet_all(devices)

    def tile(device):
        top = pl.multiple_of(device // across * tall, tall)
        return (pl.ds(top, tall), pl.ds(pl.multiple_of(lax.rem(device, across) * wide, wide), wide))

    def slot(device):
        return pl.ds(pl.multiple_of(device * slot_cap, slot_cap), slot_cap)

    def share(peer):
        top = pl.multiple_of(peer // across * 8, 8)
        return (pl.ds(top, 8), pl.ds(pl.multiple_of(lax.rem(peer, across) * wide, wide), wide))

    def send_rem(k, carry):
        other = lax.rem(me + k, devices)
        send(rem_ref.at[tile(other)], rem_in.at[me], other, sems.at[0], sems.at[1])
        return carry

    def send_sums(k, carry):
        other = lax.rem(blk + k, peers)
        to = dom * peers + other
        send(sums_ref.at[share(other)], sums_in.at[blk, pl.ds(0, 8), :], to, sems.at[7], sems.at[8])
        send(sums_ref.at[pl.ds(high, 8), pl.ds(0, wide)], sums_in.at[blk, pl.ds(8, 8), :], to, sems.at[7], sems.at[8])
        return carry

    step = size // slot_cap

    def send_grads(c, carry):
        turn = lax.rem(c + me // step, devices // step)
        grads_ref[cut(turn), :] = dot(pick_rows(slot_ref[...], turn * size, size), by_rv[...]).astype(jnp.bfloat16)

        def one(i, inner):
            other = turn * step + lax.rem(me + i, step)

            @pl.when(other != me)
            def _():
                send(grads_ref.at[slot(other)], grads_in.at[slot(me)], other, sems.at[2], sems.at[3])

            return inner

        lax.fori_loop(0, step, one, 0)
        return carry

    def send_total(k, carry):
        other = lax.rem(me + k, devices)
        send(piece, whole.at[me], other, sems.at[4], sems.at[5])
        return carry

    def keep(src, dst):
        copy = pltpu.make_async_copy(src, dst, sems.at[6])
        copy.start()
        copy.wait()

    lax.fori_loop(1, peers, send_sums, 0)
    lax.fori_loop(1, devices, send_rem, 0)
    lax.fori_loop(0, devices // step, send_grads, 0)
    keep(rem_ref.at[tile(me)], rem_in.at[me])
    keep(grads_ref.at[slot(me)], grads_in.at[slot(me)])
    keep(sums_ref.at[share(blk)], sums_in.at[blk, pl.ds(0, 8), :])
    keep(sums_ref.at[pl.ds(high, 8), pl.ds(0, wide)], sums_in.at[blk, pl.ds(8, 8), :])
    drain(sums_in.at[pl.ds(0, peers - 1)], sems.at[8])
    drain(rem_in.at[pl.ds(0, devices - 1)], sems.at[1])
    piece[:tall] = (jnp.sum(rem_in[...].astype(jnp.float32), axis=0) * rem_scale).astype(jnp.bfloat16)
    piece[tall:] = (jnp.sum(sums_in[...], axis=0) * scale).astype(jnp.bfloat16)
    lax.fori_loop(1, devices, send_total, 0)
    keep(piece, whole.at[me])
    drain(grads_in.at[pl.ds(0, slots - slot_cap)], sems.at[3])

    def collect(r, carry):
        quot_ref[cut(r), :] = dot(pick_rows(asked_ref[...], r * size, size), grads_in[...])
        return carry

    lax.fori_loop(0, quot_ref.shape[0] // size, collect, 0)
    drain(whole.at[pl.ds(0, devices - 1)], sems.at[5])

    def lay(k, carry):
        for part in range(across):
            got = whole[k * across + part].astype(jnp.float32)
            lanes = slice(part * wide, (part + 1) * wide)
            total_ref[pl.ds(pl.multiple_of(k * tall, tall), tall), lanes] = got[:tall]
            weight_ref[pl.ds(pl.multiple_of(k * 8, 8), 8), lanes] = got[tall : tall + 8]
        return carry

    lax.fori_loop(0, devices // across, lay, 0)
    for d in range(devices // peers):
        bias_ref[d : d + 1, :] = whole[d * peers, tall + 8 : tall + 16, :].astype(jnp.float32)[0:1]
    drain(rem_in.at[pl.ds(0, devices - 1)], sems.at[0])
    drain(grads_in.at[pl.ds(0, slots - slot_cap)], sems.at[2])
    drain(whole.at[pl.ds(0, devices - 1)], sems.at[4])
    drain(sums_in.at[pl.ds(0, peers - 1)], sems.at[7])


def spread_grads(grad, qv, rv, slot_row, rem_row, asked_row, sums, table_rows, rem_rows, peers, rem_scale, scale):
    nodes, width = grad.shape
    slots = asked_row.shape[1]
    doms = lax.axis_size("dom")
    devices = doms * peers
    wide = LANES
    tall = rem_rows * width // devices // wide
    kind = jnp.bfloat16
    vmem = pl.BlockSpec(memory_space=pltpu.VMEM)
    return pl.pallas_call(
        functools.partial(spread_kernel, devices, rem_scale, scale),
        out_shape=(
            jax.ShapeDtypeStruct((table_rows, width), jnp.float32),
            jax.ShapeDtypeStruct((rem_rows, width), jnp.float32),
            jax.ShapeDtypeStruct((doms * (sums.shape[0] - 8), width), jnp.float32),
            jax.ShapeDtypeStruct((doms, wide), jnp.float32),
        ),
        in_specs=[vmem] * 7,
        out_specs=(vmem, vmem, vmem, vmem),
        scratch_shapes=[
            pltpu.VMEM((slots, width), kind),
            pltpu.VMEM((rem_rows, width), kind),
            pltpu.VMEM((nodes, width), kind),
            pltpu.VMEM((slots, width), kind),
            pltpu.VMEM((devices, tall, wide), kind),
            pltpu.VMEM((peers, 16, wide), jnp.float32),
            pltpu.VMEM((tall + 16, wide), kind),
            pltpu.VMEM((devices, tall + 16, wide), kind),
            pltpu.SemaphoreType.DMA((9,)),
        ],
        compiler_params=pltpu.CompilerParams(
            collective_id=2, has_side_effects=True, vmem_limit_bytes=60 << 20
        ),
        name="spread_grads",
    )(grad, qv, rv, slot_row, rem_row, asked_row, sums)


def forward_kernel(
    counts_ref, rows_ref, halo_counts_ref, halo_rows_ref, deg_ref, x_ref, w_self_ref, w_neigh_ref, bias_ref, cot_ref,
    out_ref, grad_ref, halo_ref, dx_ref, weights_ref, total, acc_self, acc_neigh
):
    k = pl.program_id(0)
    nodes, feats = total.shape
    tile = 256

    def cut(r):
        return pl.ds(pl.multiple_of(r * tile, tile), tile)

    @pl.when(k == 0)
    def _():
        def start(r, carry):
            total[cut(r), :] = dot(halo_counts_ref[cut(r), :], halo_rows_ref[...])
            return carry

        lax.fori_loop(0, nodes // tile, start, 0)

    total[...] += dot(counts_ref[...], rows_ref[...])

    @pl.when(k == pl.num_programs(0) - 1)
    def _():
        acc_self[...] = jnp.zeros_like(acc_self)
        acc_neigh[...] = jnp.zeros_like(acc_neigh)

        def layer(r, bias_sum):
            rows = cut(r)
            divisor = jnp.maximum(deg_ref[rows, :], 1.0)
            x = x_ref[rows, :]
            neighbour = (total[rows, :] / divisor).astype(jnp.bfloat16)
            preact = dot(x, w_self_ref[...]) + dot(neighbour, w_neigh_ref[...]) + bias_ref[...]
            sigma = jax.nn.sigmoid(preact)
            out_ref[rows, :] = (preact * sigma).astype(jnp.bfloat16)
            slope = sigma * (1.0 + preact * (1.0 - sigma))
            dpre = (cot_ref[rows, :].astype(jnp.float32) * slope).astype(jnp.bfloat16)
            scaled = dot(dpre, w_neigh_ref[...], COLS) / divisor
            grad_ref[:, rows] = scaled.T.astype(jnp.bfloat16)
            dx_ref[rows, :] = dot(dpre, w_self_ref[...], COLS)
            acc_self[...] += dot(x, dpre, ROWS)
            acc_neigh[...] += dot(neighbour, dpre, ROWS)
            return bias_sum + jnp.sum(dpre.astype(jnp.float32), axis=0, keepdims=True)

        bias_sum = lax.fori_loop(0, nodes // tile, layer, jnp.zeros((1, feats), jnp.float32))
        halo_ref[...] = dot(grad_ref[...], halo_counts_ref[...]).T.astype(jnp.bfloat16)
        doms = weights_ref.shape[0]
        each = 2 * feats // doms
        wide = feats // doms
        spread = jnp.broadcast_to(bias_sum, (8, feats))
        for c in range(doms):
            source, at = (acc_self, c * each) if c * each < feats else (acc_neigh, c * each - feats)
            weights_ref[c, :each, :] = source[at : at + each, :]
            shift = (feats - c * wide) % feats
            weights_ref[c, each:, :] = pltpu.roll(spread, shift, 1) if shift else spread


def forward(counts, gathered, halo_counts, halo_rows, degree, features, w_self, w_neigh, bias, cotangent, doms):
    nodes, feats = features.shape
    wide = 4 * nodes
    steps = counts.shape[1] // wide

    def whole(array):
        return pl.BlockSpec(array.shape, lambda k: (0,) * len(array.shape))

    out_shape = (
        jax.ShapeDtypeStruct((nodes, feats), jnp.bfloat16),
        jax.ShapeDtypeStruct((feats, nodes), jnp.bfloat16),
        jax.ShapeDtypeStruct(halo_rows.shape, jnp.bfloat16),
        jax.ShapeDtypeStruct((nodes, feats), jnp.float32),
        jax.ShapeDtypeStruct((doms, 2 * feats // doms + 8, feats), jnp.float32),
    )
    kept = (halo_counts, halo_rows, degree, features, w_self, w_neigh, bias, cotangent)
    return pl.pallas_call(
        forward_kernel,
        grid=(steps,),
        out_shape=out_shape,
        in_specs=[
            pl.BlockSpec((nodes, wide), lambda k: (0, k)),
            pl.BlockSpec((wide, feats), lambda k: (k, 0)),
        ]
        + [whole(array) for array in kept],
        out_specs=tuple(whole(array) for array in out_shape),
        scratch_shapes=[
            pltpu.VMEM((nodes, feats), jnp.float32),
            pltpu.VMEM((feats, feats), jnp.float32),
            pltpu.VMEM((feats, feats), jnp.float32),
        ],
        compiler_params=pltpu.CompilerParams(vmem_limit_bytes=60 << 20),
        name="forward_layer",
    )(counts, gathered, *kept)


def reduce_kernel(
    counts_ref, grad_ref, weights_ref, halo_ref, dx_ref, out_ref, sums_ref, load, part, mid, fin, half_sum, mid2, fin2, sems_load, s_out, s_mid, s_fin, t_out, t_mid, t_fin, weights_in, w_out, w_in, halo_in, own, h_out, h_in, dx_in, mine_in, s_own
):
    side = 4
    nodes = grad_ref.shape[1]
    feats = grad_ref.shape[0] // 2
    span = nodes // 2
    dom = lax.axis_index("dom")
    blk = lax.axis_index("blk")
    x, y = blk // side, lax.rem(blk, side)

    def at(dx, dy):
        return lax.rem(x + dx, side) * side + lax.rem(y + dy, side)

    def device(half, first, second):
        dx, dy = (first, second) if half == 0 else (second, first)
        return (dom, at(dx, dy))

    barrier = pltpu.get_barrier_semaphore()
    for dx, dy in ((1, 0), (3, 0), (0, 1), (0, 3)):
        pl.semaphore_signal(barrier, inc=1, device_id=(dom, at(dx, dy)), device_id_type=MESH)
    doms = weights_ref.shape[0]
    for k in range(1, doms):
        pl.semaphore_signal(barrier, inc=1, device_id=(lax.rem(dom + k, doms), blk), device_id_type=MESH)

    order = [(2, 2), (2, 1), (1, 2), (2, 3), (3, 2), (2, 0), (0, 2), (1, 1), (3, 3), (1, 3), (3, 1)]
    order += [(1, 0), (0, 1), (3, 0), (0, 3), (0, 0)]
    depth = load.shape[0]

    def fetch(i):
        dx, dy = order[i]
        columns = pl.ds(pl.multiple_of(at(dx, dy) * nodes, nodes), nodes)
        return pltpu.make_async_copy(counts_ref.at[:, columns], load.at[i % depth], sems_load.at[i % depth])

    for i in range(depth - 1):
        fetch(i).start()
    own_dx = pltpu.make_async_copy(dx_ref, dx_in, s_own.at[0])
    own_dx.start()
    own_weights = pltpu.make_async_copy(weights_ref.at[dom], mine_in, s_own.at[1])
    own_weights.start()
    pl.semaphore_wait(barrier, 4 + doms - 1)

    def to_dom(k):
        other = lax.rem(dom + k, doms)
        return pltpu.make_async_remote_copy(
            src_ref=weights_ref.at[other],
            dst_ref=weights_in.at[k],
            send_sem=w_out.at[k],
            recv_sem=w_in.at[k],
            device_id=(other, blk),
            device_id_type=MESH,
        )

    halo = halo_in.shape[1]

    def to_side(side_index):
        return pltpu.make_async_remote_copy(
            src_ref=halo_ref.at[pl.ds(side_index * halo, halo)],
            dst_ref=halo_in.at[side_index],
            send_sem=h_out.at[side_index],
            recv_sem=h_in.at[side_index],
            device_id=(lax.rem(dom + (doms - 1 if side_index == 0 else 1), doms), blk),
            device_id_type=MESH,
        )

    for k in range(1, doms):
        to_dom(k).start()
    to_side(0).start()
    to_side(1).start()

    def remote(src, dst, half, first, second, send_sem, recv_sem):
        return pltpu.make_async_remote_copy(
            src_ref=src,
            dst_ref=dst,
            send_sem=send_sem,
            recv_sem=recv_sem,
            device_id=device(half, first, second),
            device_id_type=MESH,
        )

    def along(unit):
        return unit % 2 == 0

    def to_mid(half, unit):
        return remote(
            part.at[half, 2, unit], mid.at[half, unit], half, 1 if along(unit) else 3, 0,
            s_out.at[half, 0, unit], s_mid.at[half, unit],
        )

    def to_fin(half, first, unit):
        way = 0 if first == 1 else 1
        return remote(
            part.at[half, first, unit], fin.at[half, way, unit], half, first, 0,
            s_out.at[half, 1 + way, unit], s_fin.at[half, way, unit],
        )

    def relays(first, unit):
        return along(unit) == (first == 1)

    tile = 256
    waiting = []
    for i, (dx, dy) in enumerate(order):
        if i + depth - 1 < len(order):
            fetch(i + depth - 1).start()
        fetch(i).wait()

        def columns(n, carry, slot=i % depth, dx=dx, dy=dy):
            cut = pl.ds(pl.multiple_of(n * tile, tile), tile)
            value = jnp.dot(grad_ref[...], load[slot, :, cut], preferred_element_type=jnp.float32)
            part[0, dx, dy, :, cut] = value[:feats].astype(jnp.bfloat16)
            part[1, dy, dx, :, cut] = value[feats:].astype(jnp.bfloat16)
            return carry

        lax.fori_loop(0, nodes // tile, columns, 0)
        for half, first, unit in ((0, dx, dy), (1, dy, dx)):
            if first == 2:
                to_mid(half, unit).start()
            elif first != 0:
                if relays(first, unit):
                    waiting.append((half, first, unit))
                else:
                    to_fin(half, first, unit).start()
    waiting.sort(key=lambda item: (2, 1, 3, 0).index(item[2]))
    for half, first, unit in waiting:
        to_mid(half, unit).wait_recv()
        mine = part[half, first, unit].astype(jnp.float32)
        part[half, first, unit] = (mine + mid[half, unit].astype(jnp.float32)).astype(jnp.bfloat16)
        to_fin(half, first, unit).start()

    def cut(piece):
        return pl.ds(piece * span, span)

    def to_mid2(half, piece):
        return remote(
            half_sum.at[half, 1, :, cut(piece)], mid2.at[half, piece], half, 0, 1 if piece == 0 else 3,
            t_out.at[half, 0, piece], t_mid.at[half, piece],
        )

    def to_fin2(half, second, piece):
        way = 0 if second == 1 else 1
        return remote(
            half_sum.at[half, 0 if second == 1 else 2, :, cut(piece)], fin2.at[half, way, piece], half, 0, second,
            t_out.at[half, 1 + way, piece], t_fin.at[half, way, piece],
        )

    def summed(half, unit):
        to_fin(half, 1, unit).wait_recv()
        to_fin(half, 3, unit).wait_recv()
        total = part[half, 0, unit].astype(jnp.float32) + fin[half, 0, unit].astype(jnp.float32)
        return total + fin[half, 1, unit].astype(jnp.float32)

    for half in range(2):
        half_sum[half, 1] = summed(half, 2).astype(jnp.bfloat16)
        to_mid2(half, 0).start()
        to_mid2(half, 1).start()
    for second in (1, 3):
        direct, relayed = (1, 0) if second == 1 else (0, 1)
        for half in range(2):
            half_sum[half, second - 1] = summed(half, second).astype(jnp.bfloat16)
            to_fin2(half, second, direct).start()
    for second in (1, 3):
        direct, relayed = (1, 0) if second == 1 else (0, 1)
        for half in range(2):
            to_mid2(half, relayed).wait_recv()
            mine = half_sum[half, second - 1, :, cut(relayed)].astype(jnp.float32)
            both = mine + mid2[half, relayed].astype(jnp.float32)
            half_sum[half, second - 1, :, cut(relayed)] = both.astype(jnp.bfloat16)
            to_fin2(half, second, relayed).start()
    for half in range(2):
        own[half * feats : (half + 1) * feats, :] = summed(half, 0)
    to_side(0).wait_recv()
    to_side(1).wait_recv()
    own_dx.wait()
    for half in range(2):
        rows = slice(half * feats, (half + 1) * feats)
        for piece in range(2):
            to_fin2(half, 1, piece).wait_recv()
            to_fin2(half, 3, piece).wait_recv()
            total = own[rows, piece * span : (piece + 1) * span] + fin2[half, 0, piece].astype(jnp.float32)
            total = (total + fin2[half, 1, piece].astype(jnp.float32)).T
            near = slice(piece * span, (piece + 1) * span)
            out_ref[near, rows] = dx_in[near, rows] + total
            edge = slice(0, halo) if piece == 0 else slice(nodes - halo, nodes)
            out_ref[edge, rows] += halo_in[1 - piece, :, rows].astype(jnp.float32)
    to_side(0).wait_send()
    to_side(1).wait_send()
    own_weights.wait()
    sums = mine_in[...]
    for k in range(1, doms):
        to_dom(k).wait_recv()
        sums = sums + weights_in[k]
    sums_ref[...] = sums
    for k in range(1, doms):
        to_dom(k).wait_send()
    for half in range(2):
        for unit in range(side):
            to_mid(half, unit).wait_send()
            to_fin(half, 1, unit).wait_send()
            to_fin(half, 3, unit).wait_send()
        for piece in range(2):
            to_mid2(half, piece).wait_send()
            to_fin2(half, 1, piece).wait_send()
            to_fin2(half, 3, piece).wait_send()


def reduce_sources(counts, grad, weights, halo, dx):
    feats, nodes = grad.shape
    half = feats // 2
    kind = jnp.bfloat16
    dma = pltpu.SemaphoreType.DMA
    vmem = pl.BlockSpec(memory_space=pltpu.VMEM)
    anywhere = pl.BlockSpec(memory_space=pl.ANY)
    return pl.pallas_call(
        reduce_kernel,
        out_shape=(
            jax.ShapeDtypeStruct((nodes, feats), jnp.float32),
            jax.ShapeDtypeStruct(weights.shape[1:], jnp.float32),
        ),
        in_specs=[anywhere, vmem, anywhere, anywhere, anywhere],
        out_specs=(vmem, vmem),
        scratch_shapes=[
            pltpu.VMEM((3, nodes, nodes), kind),
            pltpu.VMEM((2, 4, 4, half, nodes), kind),
            pltpu.VMEM((2, 4, half, nodes), kind),
            pltpu.VMEM((2, 2, 4, half, nodes), kind),
            pltpu.VMEM((2, 3, half, nodes), kind),
            pltpu.VMEM((2, 2, half, nodes // 2), kind),
            pltpu.VMEM((2, 2, 2, half, nodes // 2), kind),
            dma((3,)),
            dma((2, 3, 4)),
            dma((2, 4)),
            dma((2, 2, 4)),
            dma((2, 3, 2)),
            dma((2, 2)),
            dma((2, 2, 2)),
            pltpu.VMEM(weights.shape, jnp.float32),
            dma((weights.shape[0],)),
            dma((weights.shape[0],)),
            pltpu.VMEM((2, halo.shape[0] // 2, feats), kind),
            pltpu.VMEM((feats, nodes), jnp.float32),
            dma((2,)),
            dma((2,)),
            pltpu.VMEM((nodes, feats), jnp.float32),
            pltpu.VMEM(weights.shape[1:], jnp.float32),
            dma((2,)),
        ],
        compiler_params=pltpu.CompilerParams(
            collective_id=3, has_side_effects=True, vmem_limit_bytes=60 << 20
        ),
        name="reduce_sources",
    )(counts, grad, weights, halo, dx)


def shifted(block, axis, distance):
    devices = range(lax.axis_size(axis))
    route = [((i - distance) % len(devices), i) for i in devices]
    return lax.ppermute(block, axis, route)


def dot(a, b, dims=(((1,), (0,)), ((), ()))):
    return lax.dot_general(a, b, dims, preferred_element_type=jnp.float32)


def per_device(
    node_owner,
    node_qrow,
    node_rem,
    quotient,
    remainder,
    edge_src,
    edge_dst,
    block_count,
    w_self,
    w_neigh,
    bias,
    cotangent,
):
    nodes_dev = node_qrow.shape[0]
    feature_dim = quotient.shape[1]
    devices = lax.axis_size("dom") * lax.axis_size("blk")
    part_nodes = nodes_dev * lax.axis_size("blk")
    doms = lax.axis_size("dom")
    features, quot_rows, remain_rows, asked_row, slot_row, fast, slow, flags = fetch_rows(
        node_owner.reshape(1, -1),
        node_qrow[None],
        node_rem[None],
        quotient,
        remainder,
        edge_src,
        edge_dst,
        block_count,
        devices,
        part_nodes,
    )
    part_gathered = lax.all_gather(features, "blk", axis=0, tiled=True)
    low_rows = shifted(features[nodes_dev - HALO :], "dom", 1)
    high_rows = shifted(features[:HALO], "dom", -1)
    halo_rows = jnp.concatenate([low_rows, high_rows], axis=0)

    counts, halo_counts, degree = build_counts(fast, slow, flags, block_count, part_nodes)
    out, grad_t, halo_grads, dx_self, weights = forward(
        counts, part_gathered, halo_counts, halo_rows, degree, features, w_self, w_neigh, bias[None], cotangent, doms
    )
    grad_x, weight_sums = reduce_sources(counts, grad_t, weights, halo_grads, dx_self)
    nodes_total = nodes_dev * devices
    weight_scale = 1.0 / math.sqrt(nodes_total)
    remain_scale = math.sqrt(remainder.shape[0] / nodes_total)
    d_quotient, d_remainder, d_weights, d_bias = spread_grads(
        grad_x,
        quot_rows,
        remain_rows,
        slot_row,
        node_rem[None],
        asked_row,
        weight_sums,
        quotient.shape[0],
        remainder.shape[0],
        lax.axis_size("blk"),
        remain_scale,
        weight_scale,
    )
    d_self, d_neigh = d_weights[:feature_dim], d_weights[feature_dim:]
    d_bias = d_bias[:, : feature_dim // doms].reshape(-1)
    return (out, d_quotient, d_remainder, d_self, d_neigh, d_bias)


def solution(mesh):
    both = P(AXES)
    rows = P(AXES, None)
    return jax.shard_map(
        per_device,
        mesh=mesh,
        in_specs=(rows, both, both, rows, P(), rows, rows, both, P(), P(), P(), rows),
        out_specs=(rows, rows, P(), P(), P(), P()),
        check_vma=False,
    )
```

```python
import functools
import math

import jax
import jax.numpy as jnp
from jax import lax
from jax.experimental import pallas as pl
from jax.experimental.pallas import tpu as pltpu
from jax.sharding import PartitionSpec as P

ROWS_BLK = 128
HALO = 256
LANES = 128
BATCH = 8
AXES = ("dom", "blk")
MESH = pl.DeviceIdType.MESH
ROWS = (((0,), (0,)), ((), ()))
COLS = (((1,), (1,)), ((), ()))


def place_edges(dump, src_ref, dst_ref, counts, fast_ref, slow_ref, flag_ref):
    blocks, slots = src_ref.shape
    src = src_ref[...]
    lane = lax.broadcasted_iota(jnp.int32, (blocks, slots), 1)
    cell = ((src >> 7) * ROWS_BLK + dst_ref[...]) * LANES + (src & 127)
    live = lane < counts
    spare = dump * LANES
    cell = jnp.where(live, cell, spare)
    row = cell >> 7
    clash = jnp.zeros((blocks, slots), jnp.bool_)
    place = lane & (BATCH - 1)
    for s in range(1, BATCH):
        clash = clash | ((pltpu.roll(row, s, 1) == row) & (place >= s))
    clash = clash & live
    fast_ref[:, 0, :] = jnp.where(clash, spare, cell)
    slow_ref[:, 0, :] = jnp.where(clash, cell, spare)
    ones = jnp.where(clash, 1.0, 0.0).astype(jnp.bfloat16)
    chunks = slots // LANES
    col = lax.broadcasted_iota(jnp.int32, (blocks, LANES), 1)
    into = lax.broadcasted_iota(jnp.int32, (LANES, LANES), 0) // BATCH
    group = (into == lax.broadcasted_iota(jnp.int32, (LANES, LANES), 1)).astype(jnp.bfloat16)
    found = jnp.zeros((blocks, LANES), jnp.int32)
    number = jnp.zeros((blocks, 1), jnp.int32)
    for c in range(chunks):
        hits = jnp.dot(ones[:, c * LANES : (c + 1) * LANES], group, preferred_element_type=jnp.float32)
        bits = jnp.sum(jnp.where(hits > 0.5, (1 << (col & (LANES // BATCH - 1))).astype(jnp.float32), 0.0), axis=1, keepdims=True)
        bits = bits.astype(jnp.int32)
        some = bits > 0
        found = found + jnp.where((col == number) & some, c * 65536 + bits, 0)
        number = number + some.astype(jnp.int32)
    flag_ref[:, 0, :] = jnp.where(col == LANES - 1, number, found)


def count_kernel(dump, count_ref, fast_ref, slow_ref, flag_ref, main_ref, halo_ref, deg_ref, *cells):
    j = pl.program_id(0)
    blocks = pl.num_programs(0) - 1
    his = dump // ROWS_BLK
    his_main = main_ref.shape[1] // LANES
    zero = jnp.zeros((ROWS_BLK, LANES), jnp.float32)
    lanes = lax.broadcasted_iota(jnp.int32, (1, LANES), 1)

    @pl.when(j == 0)
    def _():
        def clear(i, carry):
            for ref in cells[:2]:
                ref[pl.ds(pl.multiple_of(i * ROWS_BLK, ROWS_BLK), ROWS_BLK), :] = zero
            return carry

        lax.fori_loop(0, his, clear, 0)
        for ref in cells:
            ref[pl.ds(dump, 8), :] = jnp.zeros((8, LANES), jnp.float32)

    count = jnp.where(j < blocks, count_ref[jnp.minimum(j, blocks - 1)], 0)
    pairs = (count + 4 * BATCH - 1) // (4 * BATCH)

    def add_batch(ref, first):
        keys = [fast_ref[0, 0, first + i] for i in range(BATCH)]
        rows = [k >> 7 for k in keys]
        olds = [ref[pl.ds(r, 1), :] for r in rows]
        news = [old + jnp.where(lanes == (k & 127), 1.0, 0.0) for old, k in zip(olds, keys)]
        for r, new in zip(rows, news):
            ref[pl.ds(r, 1), :] = new

    def turn(fill, leave):
        def add_pair(t, carry):
            for i in range(4):
                add_batch(fill[i % 2], (t * 4 + i) * BATCH)
            return carry

        def flush(ref, first):
            def step(h, total):
                at = pl.multiple_of((first + h) * ROWS_BLK, ROWS_BLK)
                rows = pl.ds(at, ROWS_BLK)
                value = leave[0][rows, :] + leave[1][rows, :]
                ref[:, pl.ds(pl.multiple_of(h * LANES, LANES), LANES)] = value.astype(jnp.bfloat16)
                leave[0][rows, :] = zero
                leave[1][rows, :] = zero
                return total + value

            return step

        def both(t, total):
            add_pair(t, 0)
            for i in range(2):
                total = flush(main_ref, 0)(t * 2 + i, total)
            return total

        steps = his_main
        joint = jnp.minimum(pairs, steps // 2)
        total = lax.fori_loop(0, joint, both, zero)
        lax.fori_loop(joint, pairs, add_pair, 0)
        total = lax.fori_loop(joint * 2, steps, flush(main_ref, 0), total)

        total = lax.fori_loop(0, his - his_main, flush(halo_ref, his_main), total)
        deg_ref[...] = jnp.sum(total, axis=1, keepdims=True)

        def chunk(c, carry):
            entry = flag_ref[0, 0, c]
            first = (entry >> 16) * LANES

            def some(g, inner):
                @pl.when(((entry >> g) & 1) != 0)
                def _():
                    for i in range(BATCH):
                        k = slow_ref[0, 0, first + g * BATCH + i]
                        r = k >> 7
                        old = fill[0][pl.ds(r, 1), :]
                        fill[0][pl.ds(r, 1), :] = old + jnp.where(lanes == (k & 127), 1.0, 0.0)

                return inner

            lax.fori_loop(0, LANES // BATCH, some, 0)
            return carry

        lax.fori_loop(0, jnp.where(j < blocks, flag_ref[0, 0, LANES - 1], 0), chunk, 0)

    @pl.when(lax.rem(j, 2) == 0)
    def _():
        turn(cells[:2], cells[2:])

    @pl.when(lax.rem(j, 2) == 1)
    def _():
        turn(cells[2:], cells[:2])


def build_counts(fast, slow, flags, block_count, part_nodes):
    blocks, _, slots = fast.shape
    width = part_nodes + 2 * HALO
    dump = width // LANES * ROWS_BLK
    nodes = blocks * ROWS_BLK

    def filled(j):
        return (jnp.minimum(j, blocks - 1), 0, 0)

    def left(j):
        return (jnp.maximum(j - 1, 0), 0)

    return pl.pallas_call(
        functools.partial(count_kernel, dump),
        grid=(blocks + 1,),
        out_shape=(
            jax.ShapeDtypeStruct((nodes, part_nodes), jnp.bfloat16),
            jax.ShapeDtypeStruct((nodes, 2 * HALO), jnp.bfloat16),
            jax.ShapeDtypeStruct((nodes, 1), jnp.float32),
        ),
        in_specs=[
            pl.BlockSpec(memory_space=pltpu.SMEM),
            pl.BlockSpec((1, 1, slots), filled, memory_space=pltpu.SMEM),
            pl.BlockSpec((1, 1, slots), filled, memory_space=pltpu.SMEM),
            pl.BlockSpec((1, 1, LANES), filled, memory_space=pltpu.SMEM),
        ],
        out_specs=(
            pl.BlockSpec((ROWS_BLK, part_nodes), left),
            pl.BlockSpec((ROWS_BLK, 2 * HALO), left),
            pl.BlockSpec((ROWS_BLK, 1), left),
        ),
        scratch_shapes=[pltpu.VMEM((dump + 8, LANES), jnp.float32)] * 4,
        compiler_params=pltpu.CompilerParams(vmem_limit_bytes=60 << 20),
        cost_estimate=pl.CostEstimate(flops=80_000_000_000, bytes_accessed=40_000_000, transcendentals=0),
        name="edge_counts",
    )(block_count, fast, slow, flags)


def ring_place():
    blk = lax.axis_size("blk")
    return lax.axis_index("dom") * blk + lax.axis_index("blk")


def greet_all(devices):
    me = ring_place()

    def greet(k, carry):
        other = lax.rem(me + k, devices)
        barrier = pltpu.get_barrier_semaphore()
        pl.semaphore_signal(barrier, inc=1, device_id=coords(other), device_id_type=MESH)
        return carry

    lax.fori_loop(1, devices, greet, 0)


def meet_all(devices):
    pl.semaphore_wait(pltpu.get_barrier_semaphore(), devices - 1)


def as_row(column):
    wide = jnp.broadcast_to(column.astype(jnp.float32), (column.shape[0], LANES))
    return wide.T[0:1].astype(jnp.int32)


def as_column(row):
    tall = jnp.broadcast_to(row.astype(jnp.float32), (LANES, row.shape[1]))
    return tall.T[:, 0:1].astype(jnp.int32)


def pick(column, first, size):
    lane = lax.broadcasted_iota(jnp.int32, (column.shape[0], size), 1) + first
    return (lane == column).astype(jnp.bfloat16)


def pick_rows(row, first, size):
    line = lax.broadcasted_iota(jnp.int32, (size, row.shape[1]), 0) + first
    return (line == row).astype(jnp.bfloat16)


def coords(device):
    blk = lax.axis_size("blk")
    return (device // blk, lax.rem(device, blk))


def send(src, dst, device, send_sem, recv_sem):
    pltpu.make_async_remote_copy(
        src_ref=src,
        dst_ref=dst,
        send_sem=send_sem,
        recv_sem=recv_sem,
        device_id=coords(device),
        device_id_type=MESH,
    ).start()


def drain(ref, sem):
    pltpu.make_async_copy(ref, ref, sem).wait()


def fetch_kernel(
    devices, dump, owner_row, qrow_row, rem_row, table_hbm, remainder_hbm, src_hbm, dst_hbm, count_ref,
    x_ref, qv_ref, rv_ref, asked_ref, slot_ref, fast_ref, slow_ref, flag_ref, first_ref, last_ref,
    ids_out, ids_in, served, rows_in, slot_col, slot_hot, owner_ref, qrow_ref, rem_ref, table_ref, remainder_ref,
    src_ref, dst_ref, sems
):
    slots, width = served.shape
    slot_cap = slots // devices
    nodes = owner_ref.shape[0]
    me = ring_place()
    tile = 256
    greet_all(devices)
    loads = [
        pltpu.make_async_copy(table_hbm, table_ref, sems.at[5]),
        pltpu.make_async_copy(remainder_hbm, remainder_ref, sems.at[6]),
        pltpu.make_async_copy(src_hbm, src_ref, sems.at[7]),
        pltpu.make_async_copy(dst_hbm, dst_ref, sems.at[8]),
    ]
    for load in loads:
        load.start()

    def cut(r):
        return pl.ds(pl.multiple_of(r * tile, tile), tile)

    owner_ref[...] = as_column(owner_row[...])
    qrow_ref[...] = as_column(qrow_row[...])
    rem_ref[...] = as_column(rem_row[...])

    owner_hot = pick(owner_ref[...], 0, devices)
    lane = lax.broadcasted_iota(jnp.int32, (tile, devices), 1)
    wish = jnp.zeros((devices, devices), jnp.float32)
    for r in range(nodes // tile):
        rows = slice(r * tile, (r + 1) * tile)
        line = lax.broadcasted_iota(jnp.int32, (tile, nodes), 0) + r * tile
        before = (line > lax.broadcasted_iota(jnp.int32, (tile, nodes), 1)).astype(jnp.bfloat16)
        mine = owner_hot[rows]
        rank = jnp.sum(dot(before, owner_hot) * mine.astype(jnp.float32), axis=1, keepdims=True).astype(jnp.int32)
        slot_col[rows, :] = owner_ref[rows, :] * slot_cap + rank
        qrow = qrow_ref[rows, :]
        parts = jnp.where(lane == rank, qrow >> 5, 0) + jnp.where(lane == rank + slot_cap, qrow & 31, 0)
        wish = wish + dot(mine, parts.astype(jnp.float32).astype(jnp.bfloat16), ROWS)
    ids_out[:, 0, :] = wish
    meet_all(devices)

    def ask(k, carry):
        other = lax.rem(me + k, devices)
        send(ids_out.at[other], ids_in.at[me], other, sems.at[0], sems.at[1])
        return carry

    lax.fori_loop(1, devices, ask, 0)
    loads[1].wait()

    def remain(r, carry):
        rows = cut(r)
        rv_ref[rows, :] = dot(pick(rem_ref[rows, :], 0, remainder_ref.shape[0]), remainder_ref[...]).astype(jnp.bfloat16)
        return carry

    lax.fori_loop(0, nodes // tile, remain, 0)
    slot_ref[...] = as_row(slot_col[...])
    own = pltpu.make_async_copy(ids_out.at[me], ids_in.at[me], sems.at[2])
    own.start()
    own.wait()
    loads[0].wait()
    drain(ids_in.at[pl.ds(0, devices - 1)], sems.at[1])
    ids = ids_in[:, 0, :].astype(jnp.bfloat16)
    step = 16
    part = step * slot_cap
    slot = lax.broadcasted_iota(jnp.int32, (part, devices), 0)
    place = lax.broadcasted_iota(jnp.int32, (part, devices), 1)
    rank_of = lax.rem(slot, slot_cap)
    weight = jnp.where(place == rank_of, 32.0, 0.0) + jnp.where(place == rank_of + slot_cap, 1.0, 0.0)

    def serve(c, carry):
        turn = lax.rem(c + me // step, devices // step)
        whose = (place - turn * step == slot // slot_cap).astype(jnp.bfloat16)
        asked = jnp.sum(dot(whose, ids) * weight, axis=1, keepdims=True).astype(jnp.int32)
        at = pl.multiple_of(turn * part, part)
        asked_ref[:, pl.ds(at, part)] = as_row(asked)
        served[pl.ds(at, part), :] = dot(pick(asked, 0, table_ref.shape[0]), table_ref[...]).astype(jnp.bfloat16)

        def back(i, inner):
            other = turn * step + lax.rem(me + i, step)

            @pl.when(other != me)
            def _():
                send(
                    served.at[pl.ds(pl.multiple_of(other * slot_cap, slot_cap), slot_cap)],
                    rows_in.at[pl.ds(pl.multiple_of(me * slot_cap, slot_cap), slot_cap)],
                    other,
                    sems.at[3],
                    sems.at[4],
                )

            return inner

        lax.fori_loop(0, step, back, 0)
        return carry

    lax.fori_loop(0, devices // step, serve, 0)
    mine = pl.ds(pl.multiple_of(me * slot_cap, slot_cap), slot_cap)
    own_rows = pltpu.make_async_copy(served.at[mine], rows_in.at[mine], sems.at[2])
    own_rows.start()

    def prepare(r, carry):
        slot_hot[cut(r), :] = pick(slot_col[cut(r), :], 0, slots)
        return carry

    lax.fori_loop(0, nodes // tile, prepare, 0)
    loads[2].wait()
    loads[3].wait()
    blocks = src_ref.shape[0]
    which = lax.broadcasted_iota(jnp.int32, (blocks, 1), 0)
    counts = jnp.zeros((blocks, 1), jnp.int32)
    for j in range(blocks):
        counts = counts + jnp.where(which == j, count_ref[j], 0)
    place_edges(dump, src_ref, dst_ref, counts, fast_ref, slow_ref, flag_ref)
    own_rows.wait()
    drain(rows_in.at[pl.ds(0, slots - slot_cap)], sems.at[4])

    def finish(r, carry):
        rows = cut(r)
        qv = dot(slot_hot[rows, :], rows_in[...])
        qv_ref[rows, :] = qv.astype(jnp.bfloat16)
        x_ref[rows, :] = (qv * rv_ref[rows, :].astype(jnp.float32)).astype(jnp.bfloat16)
        return carry

    lax.fori_loop(0, nodes // tile, finish, 0)
    first_ref[...] = x_ref[:HALO, :]
    last_ref[...] = x_ref[nodes - HALO :, :]
    drain(ids_in.at[pl.ds(0, devices - 1)], sems.at[0])
    drain(rows_in.at[pl.ds(0, slots - slot_cap)], sems.at[3])


def fetch_rows(owner, qrow, rem, quotient, remainder, edge_src, edge_dst, block_count, devices, part_nodes):
    nodes = owner.shape[1]
    slots = 2 * nodes
    width = quotient.shape[1]
    vmem = pl.BlockSpec(memory_space=pltpu.VMEM)
    anywhere = pl.BlockSpec(memory_space=pl.ANY)
    rows = jax.ShapeDtypeStruct((nodes, width), jnp.bfloat16)
    blocks, edges = edge_src.shape
    edge = jax.ShapeDtypeStruct((blocks, 1, edges), jnp.int32)
    half = jax.ShapeDtypeStruct((HALO, width), jnp.bfloat16)
    dump = (part_nodes + 2 * HALO) // LANES * ROWS_BLK
    column = pltpu.VMEM((nodes, 1), jnp.int32)
    return pl.pallas_call(
        functools.partial(fetch_kernel, devices, dump),
        out_shape=(
            rows,
            rows,
            rows,
            jax.ShapeDtypeStruct((1, slots), jnp.int32),
            jax.ShapeDtypeStruct((1, nodes), jnp.int32),
            edge,
            edge,
            jax.ShapeDtypeStruct((blocks, 1, LANES), jnp.int32),
            half,
            half,
        ),
        in_specs=[vmem] * 3 + [anywhere] * 4 + [pl.BlockSpec(memory_space=pltpu.SMEM)],
        out_specs=(vmem,) * 10,
        scratch_shapes=[
            pltpu.VMEM((devices, 1, devices), jnp.float32),
            pltpu.VMEM((devices, 1, devices), jnp.float32),
            pltpu.VMEM((slots, width), jnp.bfloat16),
            pltpu.VMEM((slots, width), jnp.bfloat16),
            column,
            pltpu.VMEM((nodes, slots), jnp.bfloat16),
            column,
            column,
            column,
            pltpu.VMEM(quotient.shape, jnp.bfloat16),
            pltpu.VMEM(remainder.shape, jnp.bfloat16),
            pltpu.VMEM(edge_src.shape, jnp.int32),
            pltpu.VMEM(edge_src.shape, jnp.int32),
            pltpu.SemaphoreType.DMA((9,)),
        ],
        compiler_params=pltpu.CompilerParams(
            collective_id=1, has_side_effects=True, vmem_limit_bytes=60 << 20
        ),
        name="fetch_rows",
    )(owner, qrow, rem, quotient, remainder, edge_src, edge_dst, block_count)


def spread_kernel(
    devices, rem_scale, scale, grad_ref, qv_ref, rv_ref, slot_ref, node_rem_ref, asked_ref, sums_ref,
    quot_ref, total_ref, weight_ref, bias_ref, grads_ref, rem_ref, by_rv, grads_in, rem_in, sums_in, piece, whole, sems
):
    slot_cap = grads_ref.shape[0] // devices
    slots = grads_ref.shape[0]
    tall, wide = rem_in.shape[1:]
    across = rem_ref.shape[1] // wide
    peers = sums_in.shape[0]
    high = sums_ref.shape[0] - 8
    size = 256
    me = ring_place()
    dom = lax.axis_index("dom")
    blk = lax.axis_index("blk")
    greet_all(devices)

    def cut(r):
        return pl.ds(pl.multiple_of(r * size, size), size)

    by_rv[...] = (grad_ref[...] * qv_ref[...].astype(jnp.float32)).astype(jnp.bfloat16)

    def remain(r, carry):
        rem_ref[cut(r), :] = dot(pick_rows(node_rem_ref[...], r * size, size), by_rv[...]).astype(jnp.bfloat16)
        return carry

    lax.fori_loop(0, rem_ref.shape[0] // size, remain, 0)
    by_rv[...] = (grad_ref[...] * rv_ref[...].astype(jnp.float32)).astype(jnp.bfloat16)
    meet_all(devices)

    def tile(device):
        top = pl.multiple_of(device // across * tall, tall)
        return (pl.ds(top, tall), pl.ds(pl.multiple_of(lax.rem(device, across) * wide, wide), wide))

    def slot(device):
        return pl.ds(pl.multiple_of(device * slot_cap, slot_cap), slot_cap)

    def share(peer):
        top = pl.multiple_of(peer // across * 8, 8)
        return (pl.ds(top, 8), pl.ds(pl.multiple_of(lax.rem(peer, across) * wide, wide), wide))

    def send_rem(k, carry):
        other = lax.rem(me + k, devices)
        send(rem_ref.at[tile(other)], rem_in.at[me], other, sems.at[0], sems.at[1])
        return carry

    def send_sums(k, carry):
        other = lax.rem(blk + k, peers)
        to = dom * peers + other
        send(sums_ref.at[share(other)], sums_in.at[blk, pl.ds(0, 8), :], to, sems.at[7], sems.at[8])
        send(sums_ref.at[pl.ds(high, 8), pl.ds(0, wide)], sums_in.at[blk, pl.ds(8, 8), :], to, sems.at[7], sems.at[8])
        return carry

    step = size // slot_cap

    def send_grads(c, carry):
        turn = lax.rem(c + me // step, devices // step)
        grads_ref[cut(turn), :] = dot(pick_rows(slot_ref[...], turn * size, size), by_rv[...]).astype(jnp.bfloat16)

        def one(i, inner):
            other = turn * step + lax.rem(me + i, step)

            @pl.when(other != me)
            def _():
                send(grads_ref.at[slot(other)], grads_in.at[slot(me)], other, sems.at[2], sems.at[3])

            return inner

        lax.fori_loop(0, step, one, 0)
        return carry

    def send_total(k, carry):
        other = lax.rem(me + k, devices)
        send(piece, whole.at[me], other, sems.at[4], sems.at[5])
        return carry

    def keep(src, dst):
        copy = pltpu.make_async_copy(src, dst, sems.at[6])
        copy.start()
        copy.wait()

    lax.fori_loop(1, peers, send_sums, 0)
    lax.fori_loop(1, devices, send_rem, 0)
    lax.fori_loop(0, devices // step, send_grads, 0)
    keep(rem_ref.at[tile(me)], rem_in.at[me])
    keep(grads_ref.at[slot(me)], grads_in.at[slot(me)])
    keep(sums_ref.at[share(blk)], sums_in.at[blk, pl.ds(0, 8), :])
    keep(sums_ref.at[pl.ds(high, 8), pl.ds(0, wide)], sums_in.at[blk, pl.ds(8, 8), :])
    drain(sums_in.at[pl.ds(0, peers - 1)], sems.at[8])
    drain(rem_in.at[pl.ds(0, devices - 1)], sems.at[1])
    piece[:tall] = (jnp.sum(rem_in[...].astype(jnp.float32), axis=0) * rem_scale).astype(jnp.bfloat16)
    piece[tall:] = (jnp.sum(sums_in[...], axis=0) * scale).astype(jnp.bfloat16)
    lax.fori_loop(1, devices, send_total, 0)
    keep(piece, whole.at[me])
    drain(grads_in.at[pl.ds(0, slots - slot_cap)], sems.at[3])

    def collect(r, carry):
        quot_ref[cut(r), :] = dot(pick_rows(asked_ref[...], r * size, size), grads_in[...])
        return carry

    lax.fori_loop(0, quot_ref.shape[0] // size, collect, 0)
    drain(whole.at[pl.ds(0, devices - 1)], sems.at[5])

    def lay(k, carry):
        for part in range(across):
            got = whole[k * across + part].astype(jnp.float32)
            lanes = slice(part * wide, (part + 1) * wide)
            total_ref[pl.ds(pl.multiple_of(k * tall, tall), tall), lanes] = got[:tall]
            weight_ref[pl.ds(pl.multiple_of(k * 8, 8), 8), lanes] = got[tall : tall + 8]
        return carry

    lax.fori_loop(0, devices // across, lay, 0)
    for d in range(devices // peers):
        bias_ref[d : d + 1, :] = whole[d * peers, tall + 8 : tall + 16, :].astype(jnp.float32)[0:1]
    drain(rem_in.at[pl.ds(0, devices - 1)], sems.at[0])
    drain(grads_in.at[pl.ds(0, slots - slot_cap)], sems.at[2])
    drain(whole.at[pl.ds(0, devices - 1)], sems.at[4])
    drain(sums_in.at[pl.ds(0, peers - 1)], sems.at[7])


def spread_grads(grad, qv, rv, slot_row, rem_row, asked_row, sums, table_rows, rem_rows, peers, rem_scale, scale):
    nodes, width = grad.shape
    slots = asked_row.shape[1]
    doms = lax.axis_size("dom")
    devices = doms * peers
    wide = LANES
    tall = rem_rows * width // devices // wide
    kind = jnp.bfloat16
    vmem = pl.BlockSpec(memory_space=pltpu.VMEM)
    return pl.pallas_call(
        functools.partial(spread_kernel, devices, rem_scale, scale),
        out_shape=(
            jax.ShapeDtypeStruct((table_rows, width), jnp.float32),
            jax.ShapeDtypeStruct((rem_rows, width), jnp.float32),
            jax.ShapeDtypeStruct((doms * (sums.shape[0] - 8), width), jnp.float32),
            jax.ShapeDtypeStruct((doms, wide), jnp.float32),
        ),
        in_specs=[vmem] * 7,
        out_specs=(vmem, vmem, vmem, vmem),
        scratch_shapes=[
            pltpu.VMEM((slots, width), kind),
            pltpu.VMEM((rem_rows, width), kind),
            pltpu.VMEM((nodes, width), kind),
            pltpu.VMEM((slots, width), kind),
            pltpu.VMEM((devices, tall, wide), kind),
            pltpu.VMEM((peers, 16, wide), jnp.float32),
            pltpu.VMEM((tall + 16, wide), kind),
            pltpu.VMEM((devices, tall + 16, wide), kind),
            pltpu.SemaphoreType.DMA((9,)),
        ],
        compiler_params=pltpu.CompilerParams(
            collective_id=2, has_side_effects=True, vmem_limit_bytes=40 << 20
        ),
        name="spread_grads",
    )(grad, qv, rv, slot_row, rem_row, asked_row, sums)


def forward_kernel(
    counts_ref, rows_ref, halo_counts_ref, low_ref, high_ref, deg_ref, x_ref, w_self_ref, w_neigh_ref, bias_ref, cot_ref,
    out_ref, grad_ref, halo_ref, dx_ref, weights_ref, total, acc_self, acc_neigh
):
    k = pl.program_id(0)
    nodes, feats = total.shape
    tile = 256

    def cut(r):
        return pl.ds(pl.multiple_of(r * tile, tile), tile)

    @pl.when(k == 0)
    def _():
        def start(r, carry):
            low = dot(halo_counts_ref[cut(r), :HALO], low_ref[...])
            total[cut(r), :] = low + dot(halo_counts_ref[cut(r), HALO:], high_ref[...])
            return carry

        lax.fori_loop(0, nodes // tile, start, 0)

    total[...] += dot(counts_ref[...], rows_ref[...])

    @pl.when(k == pl.num_programs(0) - 1)
    def _():
        acc_self[...] = jnp.zeros_like(acc_self)
        acc_neigh[...] = jnp.zeros_like(acc_neigh)

        def layer(r, bias_sum):
            rows = cut(r)
            divisor = jnp.maximum(deg_ref[rows, :], 1.0)
            x = x_ref[rows, :]
            neighbour = (total[rows, :] / divisor).astype(jnp.bfloat16)
            preact = dot(x, w_self_ref[...]) + dot(neighbour, w_neigh_ref[...]) + bias_ref[...]
            sigma = jax.nn.sigmoid(preact)
            out_ref[rows, :] = (preact * sigma).astype(jnp.bfloat16)
            slope = sigma * (1.0 + preact * (1.0 - sigma))
            dpre = (cot_ref[rows, :].astype(jnp.float32) * slope).astype(jnp.bfloat16)
            scaled = dot(dpre, w_neigh_ref[...], COLS) / divisor
            grad_ref[:, rows] = scaled.T.astype(jnp.bfloat16)
            dx_ref[rows, :] = dot(dpre, w_self_ref[...], COLS)
            acc_self[...] += dot(x, dpre, ROWS)
            acc_neigh[...] += dot(neighbour, dpre, ROWS)
            return bias_sum + jnp.sum(dpre.astype(jnp.float32), axis=0, keepdims=True)

        bias_sum = lax.fori_loop(0, nodes // tile, layer, jnp.zeros((1, feats), jnp.float32))
        halo_ref[...] = dot(grad_ref[...], halo_counts_ref[...]).T.astype(jnp.bfloat16)
        doms = weights_ref.shape[0]
        each = 2 * feats // doms
        wide = feats // doms
        spread = jnp.broadcast_to(bias_sum, (8, feats))
        for c in range(doms):
            source, at = (acc_self, c * each) if c * each < feats else (acc_neigh, c * each - feats)
            weights_ref[c, :each, :] = source[at : at + each, :]
            shift = (feats - c * wide) % feats
            weights_ref[c, each:, :] = pltpu.roll(spread, shift, 1) if shift else spread


def forward(counts, gathered, halo_counts, low_rows, high_rows, degree, features, w_self, w_neigh, bias, cotangent, doms):
    nodes, feats = features.shape
    wide = 4 * nodes
    steps = counts.shape[1] // wide

    def whole(array):
        return pl.BlockSpec(array.shape, lambda k: (0,) * len(array.shape))

    out_shape = (
        jax.ShapeDtypeStruct((nodes, feats), jnp.bfloat16),
        jax.ShapeDtypeStruct((feats, nodes), jnp.bfloat16),
        jax.ShapeDtypeStruct((2 * HALO, feats), jnp.bfloat16),
        jax.ShapeDtypeStruct((nodes, feats), jnp.float32),
        jax.ShapeDtypeStruct((doms, 2 * feats // doms + 8, feats), jnp.float32),
    )
    kept = (halo_counts, low_rows, high_rows, degree, features, w_self, w_neigh, bias, cotangent)
    return pl.pallas_call(
        forward_kernel,
        grid=(steps,),
        out_shape=out_shape,
        in_specs=[
            pl.BlockSpec((nodes, wide), lambda k: (0, k)),
            pl.BlockSpec((wide, feats), lambda k: (k, 0)),
        ]
        + [whole(array) for array in kept],
        out_specs=tuple(whole(array) for array in out_shape),
        scratch_shapes=[
            pltpu.VMEM((nodes, feats), jnp.float32),
            pltpu.VMEM((feats, feats), jnp.float32),
            pltpu.VMEM((feats, feats), jnp.float32),
        ],
        compiler_params=pltpu.CompilerParams(vmem_limit_bytes=60 << 20),
        name="forward_layer",
    )(counts, gathered, *kept)


def reduce_kernel(
    counts_ref, grad_ref, weights_ref, halo_ref, dx_ref, out_ref, sums_ref, load, part, mid, fin, half_sum, mid2, fin2, sems_load, s_out, s_mid, s_fin, t_out, t_mid, t_fin, weights_in, w_out, w_in, halo_in, own, h_out, h_in, dx_in, mine_in, s_own
):
    side = 4
    nodes = grad_ref.shape[1]
    feats = grad_ref.shape[0] // 2
    span = nodes // 2
    dom = lax.axis_index("dom")
    blk = lax.axis_index("blk")
    x, y = blk // side, lax.rem(blk, side)

    def at(dx, dy):
        return lax.rem(x + dx, side) * side + lax.rem(y + dy, side)

    def device(half, first, second):
        dx, dy = (first, second) if half == 0 else (second, first)
        return (dom, at(dx, dy))

    barrier = pltpu.get_barrier_semaphore()
    for dx, dy in ((1, 0), (3, 0), (0, 1), (0, 3)):
        pl.semaphore_signal(barrier, inc=1, device_id=(dom, at(dx, dy)), device_id_type=MESH)
    doms = weights_ref.shape[0]
    for k in range(1, doms):
        pl.semaphore_signal(barrier, inc=1, device_id=(lax.rem(dom + k, doms), blk), device_id_type=MESH)

    order = [(2, 2), (2, 1), (1, 2), (2, 3), (3, 2), (2, 0), (0, 2), (1, 1), (3, 3), (1, 3), (3, 1)]
    order += [(1, 0), (0, 1), (3, 0), (0, 3), (0, 0)]
    depth = load.shape[0]

    def fetch(i):
        dx, dy = order[i]
        columns = pl.ds(pl.multiple_of(at(dx, dy) * nodes, nodes), nodes)
        return pltpu.make_async_copy(counts_ref.at[:, columns], load.at[i % depth], sems_load.at[i % depth])

    for i in range(depth - 1):
        fetch(i).start()
    own_dx = pltpu.make_async_copy(dx_ref, dx_in, s_own.at[0])
    own_dx.start()
    own_weights = pltpu.make_async_copy(weights_ref.at[dom], mine_in, s_own.at[1])
    own_weights.start()
    pl.semaphore_wait(barrier, 4 + doms - 1)

    def to_dom(k):
        other = lax.rem(dom + k, doms)
        return pltpu.make_async_remote_copy(
            src_ref=weights_ref.at[other],
            dst_ref=weights_in.at[k],
            send_sem=w_out.at[k],
            recv_sem=w_in.at[k],
            device_id=(other, blk),
            device_id_type=MESH,
        )

    halo = halo_in.shape[1]

    def to_side(side_index):
        return pltpu.make_async_remote_copy(
            src_ref=halo_ref.at[pl.ds(side_index * halo, halo)],
            dst_ref=halo_in.at[side_index],
            send_sem=h_out.at[side_index],
            recv_sem=h_in.at[side_index],
            device_id=(lax.rem(dom + (doms - 1 if side_index == 0 else 1), doms), blk),
            device_id_type=MESH,
        )

    for k in range(1, doms):
        to_dom(k).start()
    to_side(0).start()
    to_side(1).start()

    def remote(src, dst, half, first, second, send_sem, recv_sem):
        return pltpu.make_async_remote_copy(
            src_ref=src,
            dst_ref=dst,
            send_sem=send_sem,
            recv_sem=recv_sem,
            device_id=device(half, first, second),
            device_id_type=MESH,
        )

    def along(unit):
        return unit % 2 == 0

    def to_mid(half, unit):
        return remote(
            part.at[half, 2, unit], mid.at[half, unit], half, 1 if along(unit) else 3, 0,
            s_out.at[half, 0, unit], s_mid.at[half, unit],
        )

    def to_fin(half, first, unit):
        way = 0 if first == 1 else 1
        return remote(
            part.at[half, first, unit], fin.at[half, way, unit], half, first, 0,
            s_out.at[half, 1 + way, unit], s_fin.at[half, way, unit],
        )

    def relays(first, unit):
        return along(unit) == (first == 1)

    tile = 256
    waiting = []
    for i, (dx, dy) in enumerate(order):
        if i + depth - 1 < len(order):
            fetch(i + depth - 1).start()
        fetch(i).wait()

        def columns(n, carry, slot=i % depth, dx=dx, dy=dy):
            cut = pl.ds(pl.multiple_of(n * tile, tile), tile)
            value = jnp.dot(grad_ref[...], load[slot, :, cut], preferred_element_type=jnp.float32)
            part[0, dx, dy, :, cut] = value[:feats].astype(jnp.bfloat16)
            part[1, dy, dx, :, cut] = value[feats:].astype(jnp.bfloat16)
            return carry

        lax.fori_loop(0, nodes // tile, columns, 0)
        for half, first, unit in ((0, dx, dy), (1, dy, dx)):
            if first == 2:
                to_mid(half, unit).start()
            elif first != 0:
                if relays(first, unit):
                    waiting.append((half, first, unit))
                else:
                    to_fin(half, first, unit).start()
    waiting.sort(key=lambda item: (2, 1, 3, 0).index(item[2]))
    for half, first, unit in waiting:
        to_mid(half, unit).wait_recv()
        mine = part[half, first, unit].astype(jnp.float32)
        part[half, first, unit] = (mine + mid[half, unit].astype(jnp.float32)).astype(jnp.bfloat16)
        to_fin(half, first, unit).start()

    def cut(piece):
        return pl.ds(piece * span, span)

    def to_mid2(half, piece):
        return remote(
            half_sum.at[half, 1, :, cut(piece)], mid2.at[half, piece], half, 0, 1 if piece == 0 else 3,
            t_out.at[half, 0, piece], t_mid.at[half, piece],
        )

    def to_fin2(half, second, piece):
        way = 0 if second == 1 else 1
        return remote(
            half_sum.at[half, 0 if second == 1 else 2, :, cut(piece)], fin2.at[half, way, piece], half, 0, second,
            t_out.at[half, 1 + way, piece], t_fin.at[half, way, piece],
        )

    def summed(half, unit):
        to_fin(half, 1, unit).wait_recv()
        to_fin(half, 3, unit).wait_recv()
        total = part[half, 0, unit].astype(jnp.float32) + fin[half, 0, unit].astype(jnp.float32)
        return total + fin[half, 1, unit].astype(jnp.float32)

    for half in range(2):
        half_sum[half, 1] = summed(half, 2).astype(jnp.bfloat16)
        to_mid2(half, 0).start()
        to_mid2(half, 1).start()
    for second in (1, 3):
        direct, relayed = (1, 0) if second == 1 else (0, 1)
        for half in range(2):
            half_sum[half, second - 1] = summed(half, second).astype(jnp.bfloat16)
            to_fin2(half, second, direct).start()
    for second in (1, 3):
        direct, relayed = (1, 0) if second == 1 else (0, 1)
        for half in range(2):
            to_mid2(half, relayed).wait_recv()
            mine = half_sum[half, second - 1, :, cut(relayed)].astype(jnp.float32)
            both = mine + mid2[half, relayed].astype(jnp.float32)
            half_sum[half, second - 1, :, cut(relayed)] = both.astype(jnp.bfloat16)
            to_fin2(half, second, relayed).start()
    for half in range(2):
        own[half * feats : (half + 1) * feats, :] = summed(half, 0)
    to_side(0).wait_recv()
    to_side(1).wait_recv()
    own_dx.wait()
    for half in range(2):
        rows = slice(half * feats, (half + 1) * feats)
        for piece in range(2):
            to_fin2(half, 1, piece).wait_recv()
            to_fin2(half, 3, piece).wait_recv()
            total = own[rows, piece * span : (piece + 1) * span] + fin2[half, 0, piece].astype(jnp.float32)
            total = (total + fin2[half, 1, piece].astype(jnp.float32)).T
            near = slice(piece * span, (piece + 1) * span)
            out_ref[near, rows] = dx_in[near, rows] + total
            edge = slice(0, halo) if piece == 0 else slice(nodes - halo, nodes)
            out_ref[edge, rows] += halo_in[1 - piece, :, rows].astype(jnp.float32)
    to_side(0).wait_send()
    to_side(1).wait_send()
    own_weights.wait()
    sums = mine_in[...]
    for k in range(1, doms):
        to_dom(k).wait_recv()
        sums = sums + weights_in[k]
    sums_ref[...] = sums
    for k in range(1, doms):
        to_dom(k).wait_send()
    for half in range(2):
        for unit in range(side):
            to_mid(half, unit).wait_send()
            to_fin(half, 1, unit).wait_send()
            to_fin(half, 3, unit).wait_send()
        for piece in range(2):
            to_mid2(half, piece).wait_send()
            to_fin2(half, 1, piece).wait_send()
            to_fin2(half, 3, piece).wait_send()


def reduce_sources(counts, grad, weights, halo, dx):
    feats, nodes = grad.shape
    half = feats // 2
    kind = jnp.bfloat16
    dma = pltpu.SemaphoreType.DMA
    vmem = pl.BlockSpec(memory_space=pltpu.VMEM)
    anywhere = pl.BlockSpec(memory_space=pl.ANY)
    return pl.pallas_call(
        reduce_kernel,
        out_shape=(
            jax.ShapeDtypeStruct((nodes, feats), jnp.float32),
            jax.ShapeDtypeStruct(weights.shape[1:], jnp.float32),
        ),
        in_specs=[anywhere, vmem, anywhere, anywhere, anywhere],
        out_specs=(vmem, vmem),
        scratch_shapes=[
            pltpu.VMEM((3, nodes, nodes), kind),
            pltpu.VMEM((2, 4, 4, half, nodes), kind),
            pltpu.VMEM((2, 4, half, nodes), kind),
            pltpu.VMEM((2, 2, 4, half, nodes), kind),
            pltpu.VMEM((2, 3, half, nodes), kind),
            pltpu.VMEM((2, 2, half, nodes // 2), kind),
            pltpu.VMEM((2, 2, 2, half, nodes // 2), kind),
            dma((3,)),
            dma((2, 3, 4)),
            dma((2, 4)),
            dma((2, 2, 4)),
            dma((2, 3, 2)),
            dma((2, 2)),
            dma((2, 2, 2)),
            pltpu.VMEM(weights.shape, jnp.float32),
            dma((weights.shape[0],)),
            dma((weights.shape[0],)),
            pltpu.VMEM((2, halo.shape[0] // 2, feats), kind),
            pltpu.VMEM((feats, nodes), jnp.float32),
            dma((2,)),
            dma((2,)),
            pltpu.VMEM((nodes, feats), jnp.float32),
            pltpu.VMEM(weights.shape[1:], jnp.float32),
            dma((2,)),
        ],
        compiler_params=pltpu.CompilerParams(
            collective_id=3, has_side_effects=True, vmem_limit_bytes=60 << 20
        ),
        name="reduce_sources",
    )(counts, grad, weights, halo, dx)


def shifted(block, axis, distance):
    devices = range(lax.axis_size(axis))
    route = [((i - distance) % len(devices), i) for i in devices]
    return lax.ppermute(block, axis, route)


def dot(a, b, dims=(((1,), (0,)), ((), ()))):
    return lax.dot_general(a, b, dims, preferred_element_type=jnp.float32)


def per_device(
    node_owner,
    node_qrow,
    node_rem,
    quotient,
    remainder,
    edge_src,
    edge_dst,
    block_count,
    w_self,
    w_neigh,
    bias,
    cotangent,
):
    nodes_dev = node_qrow.shape[0]
    feature_dim = quotient.shape[1]
    devices = lax.axis_size("dom") * lax.axis_size("blk")
    part_nodes = nodes_dev * lax.axis_size("blk")
    doms = lax.axis_size("dom")
    features, quot_rows, remain_rows, asked_row, slot_row, fast, slow, flags, first, last = fetch_rows(
        node_owner.reshape(1, -1),
        node_qrow[None],
        node_rem[None],
        quotient,
        remainder,
        edge_src,
        edge_dst,
        block_count,
        devices,
        part_nodes,
    )
    part_gathered = lax.all_gather(features, "blk", axis=0, tiled=True)
    low_rows = shifted(last, "dom", 1)
    high_rows = shifted(first, "dom", -1)

    counts, halo_counts, degree = build_counts(fast, slow, flags, block_count, part_nodes)
    out, grad_t, halo_grads, dx_self, weights = forward(
        counts, part_gathered, halo_counts, low_rows, high_rows, degree, features, w_self, w_neigh, bias[None], cotangent, doms
    )
    grad_x, weight_sums = reduce_sources(counts, grad_t, weights, halo_grads, dx_self)
    nodes_total = nodes_dev * devices
    weight_scale = 1.0 / math.sqrt(nodes_total)
    remain_scale = math.sqrt(remainder.shape[0] / nodes_total)
    d_quotient, d_remainder, d_weights, d_bias = spread_grads(
        grad_x,
        quot_rows,
        remain_rows,
        slot_row,
        node_rem[None],
        asked_row,
        weight_sums,
        quotient.shape[0],
        remainder.shape[0],
        lax.axis_size("blk"),
        remain_scale,
        weight_scale,
    )
    d_self, d_neigh = d_weights[:feature_dim], d_weights[feature_dim:]
    d_bias = d_bias[:, : feature_dim // doms].reshape(-1)
    return (out, d_quotient, d_remainder, d_self, d_neigh, d_bias)


def solution(mesh):
    both = P(AXES)
    rows = P(AXES, None)
    return jax.shard_map(
        per_device,
        mesh=mesh,
        in_specs=(rows, both, both, rows, P(), rows, rows, both, P(), P(), P(), rows),
        out_specs=(rows, rows, P(), P(), P(), P()),
        check_vma=False,
    )
```

```python
import functools
import math

import jax
import jax.numpy as jnp
from jax import lax
from jax.experimental import pallas as pl
from jax.experimental.pallas import tpu as pltpu
from jax.sharding import PartitionSpec as P

ROWS_BLK = 128
HALO = 256
LANES = 128
BATCH = 8
AXES = ("dom", "blk")
MESH = pl.DeviceIdType.MESH
ROWS = (((0,), (0,)), ((), ()))
COLS = (((1,), (1,)), ((), ()))


def place_edges(dump, src_ref, dst_ref, counts, fast_ref, slow_ref, flag_ref):
    blocks, slots = src_ref.shape
    src = src_ref[...]
    lane = lax.broadcasted_iota(jnp.int32, (blocks, slots), 1)
    cell = ((src >> 7) * ROWS_BLK + dst_ref[...]) * LANES + (src & 127)
    live = lane < counts
    spare = dump * LANES
    cell = jnp.where(live, cell, spare)
    row = cell >> 7
    clash = jnp.zeros((blocks, slots), jnp.bool_)
    place = lane & (BATCH - 1)
    for s in range(1, BATCH):
        clash = clash | ((pltpu.roll(row, s, 1) == row) & (place >= s))
    clash = clash & live
    fast_ref[:, 0, :] = jnp.where(clash, spare, cell)
    slow_ref[:, 0, :] = jnp.where(clash, cell, spare)
    ones = jnp.where(clash, 1.0, 0.0).astype(jnp.bfloat16)
    chunks = slots // LANES
    col = lax.broadcasted_iota(jnp.int32, (blocks, LANES), 1)
    into = lax.broadcasted_iota(jnp.int32, (LANES, LANES), 0) // BATCH
    group = (into == lax.broadcasted_iota(jnp.int32, (LANES, LANES), 1)).astype(jnp.bfloat16)
    found = jnp.zeros((blocks, LANES), jnp.int32)
    number = jnp.zeros((blocks, 1), jnp.int32)
    for c in range(chunks):
        hits = jnp.dot(ones[:, c * LANES : (c + 1) * LANES], group, preferred_element_type=jnp.float32)
        bits = jnp.sum(jnp.where(hits > 0.5, (1 << (col & (LANES // BATCH - 1))).astype(jnp.float32), 0.0), axis=1, keepdims=True)
        bits = bits.astype(jnp.int32)
        some = bits > 0
        found = found + jnp.where((col == number) & some, c * 65536 + bits, 0)
        number = number + some.astype(jnp.int32)
    flag_ref[:, 0, :] = jnp.where(col == LANES - 1, number, found)


def count_kernel(dump, count_ref, fast_ref, slow_ref, flag_ref, main_ref, halo_ref, deg_ref, *cells):
    j = pl.program_id(0)
    blocks = pl.num_programs(0) - 1
    his = dump // ROWS_BLK
    his_main = main_ref.shape[1] // LANES
    zero = jnp.zeros((ROWS_BLK, LANES), jnp.float32)
    lanes = lax.broadcasted_iota(jnp.int32, (1, LANES), 1)

    @pl.when(j == 0)
    def _():
        def clear(i, carry):
            for ref in cells[:2]:
                ref[pl.ds(pl.multiple_of(i * ROWS_BLK, ROWS_BLK), ROWS_BLK), :] = zero
            return carry

        lax.fori_loop(0, his, clear, 0)
        for ref in cells:
            ref[pl.ds(dump, 8), :] = jnp.zeros((8, LANES), jnp.float32)

    count = jnp.where(j < blocks, count_ref[jnp.minimum(j, blocks - 1)], 0)
    pairs = (count + 4 * BATCH - 1) // (4 * BATCH)

    def add_batch(ref, first):
        keys = [fast_ref[0, 0, first + i] for i in range(BATCH)]
        rows = [k >> 7 for k in keys]
        olds = [ref[pl.ds(r, 1), :] for r in rows]
        news = [old + jnp.where(lanes == (k & 127), 1.0, 0.0) for old, k in zip(olds, keys)]
        for r, new in zip(rows, news):
            ref[pl.ds(r, 1), :] = new

    def turn(fill, leave):
        def add_pair(t, carry):
            for i in range(4):
                add_batch(fill[i % 2], (t * 4 + i) * BATCH)
            return carry

        def flush(ref, first):
            def step(h, total):
                at = pl.multiple_of((first + h) * ROWS_BLK, ROWS_BLK)
                rows = pl.ds(at, ROWS_BLK)
                value = leave[0][rows, :] + leave[1][rows, :]
                ref[:, pl.ds(pl.multiple_of(h * LANES, LANES), LANES)] = value.astype(jnp.bfloat16)
                leave[0][rows, :] = zero
                leave[1][rows, :] = zero
                return total + value

            return step

        def both(t, total):
            add_pair(t, 0)
            for i in range(2):
                total = flush(main_ref, 0)(t * 2 + i, total)
            return total

        steps = his_main
        joint = jnp.minimum(pairs, steps // 2)
        total = lax.fori_loop(0, joint, both, zero)
        lax.fori_loop(joint, pairs, add_pair, 0)
        total = lax.fori_loop(joint * 2, steps, flush(main_ref, 0), total)

        total = lax.fori_loop(0, his - his_main, flush(halo_ref, his_main), total)
        deg_ref[...] = jnp.sum(total, axis=1, keepdims=True)

        def chunk(c, carry):
            entry = flag_ref[0, 0, c]
            first = (entry >> 16) * LANES

            def some(g, inner):
                @pl.when(((entry >> g) & 1) != 0)
                def _():
                    for i in range(BATCH):
                        k = slow_ref[0, 0, first + g * BATCH + i]
                        r = k >> 7
                        old = fill[0][pl.ds(r, 1), :]
                        fill[0][pl.ds(r, 1), :] = old + jnp.where(lanes == (k & 127), 1.0, 0.0)

                return inner

            lax.fori_loop(0, LANES // BATCH, some, 0)
            return carry

        lax.fori_loop(0, jnp.where(j < blocks, flag_ref[0, 0, LANES - 1], 0), chunk, 0)

    @pl.when(lax.rem(j, 2) == 0)
    def _():
        turn(cells[:2], cells[2:])

    @pl.when(lax.rem(j, 2) == 1)
    def _():
        turn(cells[2:], cells[:2])


def build_counts(fast, slow, flags, block_count, part_nodes):
    blocks, _, slots = fast.shape
    width = part_nodes + 2 * HALO
    dump = width // LANES * ROWS_BLK
    nodes = blocks * ROWS_BLK

    def filled(j):
        return (jnp.minimum(j, blocks - 1), 0, 0)

    def left(j):
        return (jnp.maximum(j - 1, 0), 0)

    return pl.pallas_call(
        functools.partial(count_kernel, dump),
        grid=(blocks + 1,),
        out_shape=(
            jax.ShapeDtypeStruct((nodes, part_nodes), jnp.bfloat16),
            jax.ShapeDtypeStruct((nodes, 2 * HALO), jnp.bfloat16),
            jax.ShapeDtypeStruct((nodes, 1), jnp.float32),
        ),
        in_specs=[
            pl.BlockSpec(memory_space=pltpu.SMEM),
            pl.BlockSpec((1, 1, slots), filled, memory_space=pltpu.SMEM),
            pl.BlockSpec((1, 1, slots), filled, memory_space=pltpu.SMEM),
            pl.BlockSpec((1, 1, LANES), filled, memory_space=pltpu.SMEM),
        ],
        out_specs=(
            pl.BlockSpec((ROWS_BLK, part_nodes), left),
            pl.BlockSpec((ROWS_BLK, 2 * HALO), left),
            pl.BlockSpec((ROWS_BLK, 1), left),
        ),
        scratch_shapes=[pltpu.VMEM((dump + 8, LANES), jnp.float32)] * 4,
        compiler_params=pltpu.CompilerParams(vmem_limit_bytes=60 << 20),
        cost_estimate=pl.CostEstimate(flops=80_000_000_000, bytes_accessed=40_000_000, transcendentals=0),
        name="edge_counts",
    )(block_count, fast, slow, flags)


def ring_place():
    blk = lax.axis_size("blk")
    return lax.axis_index("dom") * blk + lax.axis_index("blk")


def greet_all(devices):
    me = ring_place()

    def greet(k, carry):
        other = lax.rem(me + k, devices)
        barrier = pltpu.get_barrier_semaphore()
        pl.semaphore_signal(barrier, inc=1, device_id=coords(other), device_id_type=MESH)
        return carry

    lax.fori_loop(1, devices, greet, 0)


def meet_all(devices):
    pl.semaphore_wait(pltpu.get_barrier_semaphore(), devices - 1)


def as_row(column):
    wide = jnp.broadcast_to(column.astype(jnp.float32), (column.shape[0], LANES))
    return wide.T[0:1].astype(jnp.int32)


def as_column(row):
    tall = jnp.broadcast_to(row.astype(jnp.float32), (LANES, row.shape[1]))
    return tall.T[:, 0:1].astype(jnp.int32)


def pick(column, first, size):
    lane = lax.broadcasted_iota(jnp.int32, (column.shape[0], size), 1) + first
    return (lane == column).astype(jnp.bfloat16)


def pick_rows(row, first, size):
    line = lax.broadcasted_iota(jnp.int32, (size, row.shape[1]), 0) + first
    return (line == row).astype(jnp.bfloat16)


def coords(device):
    blk = lax.axis_size("blk")
    return (device // blk, lax.rem(device, blk))


def send(src, dst, device, send_sem, recv_sem):
    pltpu.make_async_remote_copy(
        src_ref=src,
        dst_ref=dst,
        send_sem=send_sem,
        recv_sem=recv_sem,
        device_id=coords(device),
        device_id_type=MESH,
    ).start()


def drain(ref, sem):
    pltpu.make_async_copy(ref, ref, sem).wait()


def fetch_kernel(
    devices, dump, owner_row, qrow_row, rem_row, table_hbm, remainder_hbm, src_hbm, dst_hbm, count_ref,
    x_ref, qv_ref, rv_ref, asked_ref, slot_ref, fast_ref, slow_ref, flag_ref, first_ref, last_ref,
    ids_out, ids_in, served, rows_in, slot_col, slot_hot, owner_ref, qrow_ref, rem_ref, table_ref, remainder_ref,
    src_ref, dst_ref, sems
):
    slots, width = served.shape
    slot_cap = slots // devices
    nodes = owner_ref.shape[0]
    me = ring_place()
    tile = 256
    greet_all(devices)
    loads = [
        pltpu.make_async_copy(table_hbm, table_ref, sems.at[5]),
        pltpu.make_async_copy(remainder_hbm, remainder_ref, sems.at[6]),
        pltpu.make_async_copy(src_hbm, src_ref, sems.at[7]),
        pltpu.make_async_copy(dst_hbm, dst_ref, sems.at[8]),
    ]
    for load in loads:
        load.start()

    def cut(r):
        return pl.ds(pl.multiple_of(r * tile, tile), tile)

    owner_ref[...] = as_column(owner_row[...])
    qrow_ref[...] = as_column(qrow_row[...])
    rem_ref[...] = as_column(rem_row[...])

    owner_hot = pick(owner_ref[...], 0, devices)
    lane = lax.broadcasted_iota(jnp.int32, (tile, devices), 1)
    wish = jnp.zeros((devices, devices), jnp.float32)
    for r in range(nodes // tile):
        rows = slice(r * tile, (r + 1) * tile)
        line = lax.broadcasted_iota(jnp.int32, (tile, nodes), 0) + r * tile
        before = (line > lax.broadcasted_iota(jnp.int32, (tile, nodes), 1)).astype(jnp.bfloat16)
        mine = owner_hot[rows]
        rank = jnp.sum(dot(before, owner_hot) * mine.astype(jnp.float32), axis=1, keepdims=True).astype(jnp.int32)
        slot_col[rows, :] = owner_ref[rows, :] * slot_cap + rank
        qrow = qrow_ref[rows, :]
        parts = jnp.where(lane == rank, qrow >> 5, 0) + jnp.where(lane == rank + slot_cap, qrow & 31, 0)
        wish = wish + dot(mine, parts.astype(jnp.float32).astype(jnp.bfloat16), ROWS)
    ids_out[:, 0, :] = wish
    meet_all(devices)

    def ask(k, carry):
        other = lax.rem(me + k, devices)
        send(ids_out.at[other], ids_in.at[me], other, sems.at[0], sems.at[1])
        return carry

    lax.fori_loop(1, devices, ask, 0)
    loads[1].wait()

    def remain(r, carry):
        rows = cut(r)
        rv_ref[rows, :] = dot(pick(rem_ref[rows, :], 0, remainder_ref.shape[0]), remainder_ref[...]).astype(jnp.bfloat16)
        return carry

    lax.fori_loop(0, nodes // tile, remain, 0)
    slot_ref[...] = as_row(slot_col[...])
    own = pltpu.make_async_copy(ids_out.at[me], ids_in.at[me], sems.at[2])
    own.start()
    own.wait()
    loads[0].wait()
    drain(ids_in.at[pl.ds(0, devices - 1)], sems.at[1])
    ids = ids_in[:, 0, :].astype(jnp.bfloat16)
    step = 16
    part = step * slot_cap
    slot = lax.broadcasted_iota(jnp.int32, (part, devices), 0)
    place = lax.broadcasted_iota(jnp.int32, (part, devices), 1)
    rank_of = lax.rem(slot, slot_cap)
    weight = jnp.where(place == rank_of, 32.0, 0.0) + jnp.where(place == rank_of + slot_cap, 1.0, 0.0)

    def serve(c, carry):
        turn = lax.rem(c + me // step, devices // step)
        whose = (place - turn * step == slot // slot_cap).astype(jnp.bfloat16)
        asked = jnp.sum(dot(whose, ids) * weight, axis=1, keepdims=True).astype(jnp.int32)
        at = pl.multiple_of(turn * part, part)
        asked_ref[:, pl.ds(at, part)] = as_row(asked)
        served[pl.ds(at, part), :] = dot(pick(asked, 0, table_ref.shape[0]), table_ref[...]).astype(jnp.bfloat16)

        def back(i, inner):
            other = turn * step + lax.rem(me + i, step)

            @pl.when(other != me)
            def _():
                send(
                    served.at[pl.ds(pl.multiple_of(other * slot_cap, slot_cap), slot_cap)],
                    rows_in.at[pl.ds(pl.multiple_of(me * slot_cap, slot_cap), slot_cap)],
                    other,
                    sems.at[3],
                    sems.at[4],
                )

            return inner

        lax.fori_loop(0, step, back, 0)
        return carry

    lax.fori_loop(0, devices // step, serve, 0)
    mine = pl.ds(pl.multiple_of(me * slot_cap, slot_cap), slot_cap)
    own_rows = pltpu.make_async_copy(served.at[mine], rows_in.at[mine], sems.at[2])
    own_rows.start()

    def prepare(r, carry):
        slot_hot[cut(r), :] = pick(slot_col[cut(r), :], 0, slots)
        return carry

    lax.fori_loop(0, nodes // tile, prepare, 0)
    loads[2].wait()
    loads[3].wait()
    blocks = src_ref.shape[0]
    which = lax.broadcasted_iota(jnp.int32, (blocks, 1), 0)
    counts = jnp.zeros((blocks, 1), jnp.int32)
    for j in range(blocks):
        counts = counts + jnp.where(which == j, count_ref[j], 0)
    place_edges(dump, src_ref, dst_ref, counts, fast_ref, slow_ref, flag_ref)
    own_rows.wait()
    drain(rows_in.at[pl.ds(0, slots - slot_cap)], sems.at[4])

    def finish(r, carry):
        rows = cut(r)
        qv = dot(slot_hot[rows, :], rows_in[...])
        qv_ref[rows, :] = qv.astype(jnp.bfloat16)
        x_ref[rows, :] = (qv * rv_ref[rows, :].astype(jnp.float32)).astype(jnp.bfloat16)
        return carry

    lax.fori_loop(0, nodes // tile, finish, 0)
    first_ref[...] = x_ref[:HALO, :]
    last_ref[...] = x_ref[nodes - HALO :, :]
    drain(ids_in.at[pl.ds(0, devices - 1)], sems.at[0])
    drain(rows_in.at[pl.ds(0, slots - slot_cap)], sems.at[3])


def fetch_rows(owner, qrow, rem, quotient, remainder, edge_src, edge_dst, block_count, devices, part_nodes):
    nodes = owner.shape[1]
    slots = 2 * nodes
    width = quotient.shape[1]
    vmem = pl.BlockSpec(memory_space=pltpu.VMEM)
    anywhere = pl.BlockSpec(memory_space=pl.ANY)
    rows = jax.ShapeDtypeStruct((nodes, width), jnp.bfloat16)
    blocks, edges = edge_src.shape
    edge = jax.ShapeDtypeStruct((blocks, 1, edges), jnp.int32)
    half = jax.ShapeDtypeStruct((HALO, width), jnp.bfloat16)
    dump = (part_nodes + 2 * HALO) // LANES * ROWS_BLK
    column = pltpu.VMEM((nodes, 1), jnp.int32)
    return pl.pallas_call(
        functools.partial(fetch_kernel, devices, dump),
        out_shape=(
            rows,
            rows,
            rows,
            jax.ShapeDtypeStruct((1, slots), jnp.int32),
            jax.ShapeDtypeStruct((1, nodes), jnp.int32),
            edge,
            edge,
            jax.ShapeDtypeStruct((blocks, 1, LANES), jnp.int32),
            half,
            half,
        ),
        in_specs=[vmem] * 3 + [anywhere] * 4 + [pl.BlockSpec(memory_space=pltpu.SMEM)],
        out_specs=(vmem,) * 10,
        scratch_shapes=[
            pltpu.VMEM((devices, 1, devices), jnp.float32),
            pltpu.VMEM((devices, 1, devices), jnp.float32),
            pltpu.VMEM((slots, width), jnp.bfloat16),
            pltpu.VMEM((slots, width), jnp.bfloat16),
            column,
            pltpu.VMEM((nodes, slots), jnp.bfloat16),
            column,
            column,
            column,
            pltpu.VMEM(quotient.shape, jnp.bfloat16),
            pltpu.VMEM(remainder.shape, jnp.bfloat16),
            pltpu.VMEM(edge_src.shape, jnp.int32),
            pltpu.VMEM(edge_src.shape, jnp.int32),
            pltpu.SemaphoreType.DMA((9,)),
        ],
        compiler_params=pltpu.CompilerParams(
            collective_id=1, has_side_effects=True, vmem_limit_bytes=60 << 20
        ),
        name="fetch_rows",
    )(owner, qrow, rem, quotient, remainder, edge_src, edge_dst, block_count)


def spread_kernel(
    devices, rem_scale, scale, grad_ref, qv_ref, rv_ref, slot_ref, node_rem_ref, asked_ref, sums_ref,
    quot_ref, total_ref, weight_ref, bias_ref, grads_ref, rem_ref, by_rv, grads_in, rem_in, sums_in, piece, whole, sems
):
    slot_cap = grads_ref.shape[0] // devices
    slots = grads_ref.shape[0]
    tall, wide = rem_in.shape[1:]
    across = rem_ref.shape[1] // wide
    peers = sums_in.shape[0]
    high = sums_ref.shape[0] - 8
    size = 256
    me = ring_place()
    dom = lax.axis_index("dom")
    blk = lax.axis_index("blk")
    greet_all(devices)

    def cut(r):
        return pl.ds(pl.multiple_of(r * size, size), size)

    by_rv[...] = (grad_ref[...] * qv_ref[...].astype(jnp.float32)).astype(jnp.bfloat16)

    def remain(r, carry):
        rem_ref[cut(r), :] = dot(pick_rows(node_rem_ref[...], r * size, size), by_rv[...]).astype(jnp.bfloat16)
        return carry

    lax.fori_loop(0, rem_ref.shape[0] // size, remain, 0)
    by_rv[...] = (grad_ref[...] * rv_ref[...].astype(jnp.float32)).astype(jnp.bfloat16)
    meet_all(devices)

    def tile(device):
        top = pl.multiple_of(device // across * tall, tall)
        return (pl.ds(top, tall), pl.ds(pl.multiple_of(lax.rem(device, across) * wide, wide), wide))

    def slot(device):
        return pl.ds(pl.multiple_of(device * slot_cap, slot_cap), slot_cap)

    def share(peer):
        top = pl.multiple_of(peer // across * 8, 8)
        return (pl.ds(top, 8), pl.ds(pl.multiple_of(lax.rem(peer, across) * wide, wide), wide))

    def send_rem(k, carry):
        other = lax.rem(me + k, devices)
        send(rem_ref.at[tile(other)], rem_in.at[me], other, sems.at[0], sems.at[1])
        return carry

    def send_sums(k, carry):
        other = lax.rem(blk + k, peers)
        to = dom * peers + other
        send(sums_ref.at[share(other)], sums_in.at[blk, pl.ds(0, 8), :], to, sems.at[7], sems.at[8])
        send(sums_ref.at[pl.ds(high, 8), pl.ds(0, wide)], sums_in.at[blk, pl.ds(8, 8), :], to, sems.at[7], sems.at[8])
        return carry

    step = size // slot_cap

    def send_grads(c, carry):
        turn = lax.rem(c + me // step, devices // step)
        grads_ref[cut(turn), :] = dot(pick_rows(slot_ref[...], turn * size, size), by_rv[...]).astype(jnp.bfloat16)

        def one(i, inner):
            other = turn * step + lax.rem(me + i, step)

            @pl.when(other != me)
            def _():
                send(grads_ref.at[slot(other)], grads_in.at[slot(me)], other, sems.at[2], sems.at[3])

            return inner

        lax.fori_loop(0, step, one, 0)
        return carry

    half = devices // 2
    core = lax.rem(dom, 2)
    twin = (dom + 1 - 2 * core) * peers + blk

    def send_total(k, carry):
        turn = lax.rem(dom // 2 * peers + blk + k, half)
        other = (turn // peers * 2 + core) * peers + lax.rem(turn, peers)
        send(piece, whole.at[me], other, sems.at[4], sems.at[5])
        return carry

    def relay(z, carry):
        group = pl.ds((z * 2 + core) * peers, peers)
        send(whole.at[group], whole.at[group], twin, sems.at[9], sems.at[10])
        return carry

    def keep(src, dst):
        copy = pltpu.make_async_copy(src, dst, sems.at[6])
        copy.start()
        copy.wait()

    lax.fori_loop(1, peers, send_sums, 0)
    lax.fori_loop(1, devices, send_rem, 0)
    lax.fori_loop(0, devices // step, send_grads, 0)
    keep(rem_ref.at[tile(me)], rem_in.at[me])
    keep(grads_ref.at[slot(me)], grads_in.at[slot(me)])
    keep(sums_ref.at[share(blk)], sums_in.at[blk, pl.ds(0, 8), :])
    keep(sums_ref.at[pl.ds(high, 8), pl.ds(0, wide)], sums_in.at[blk, pl.ds(8, 8), :])
    drain(sums_in.at[pl.ds(0, peers - 1)], sems.at[8])
    drain(rem_in.at[pl.ds(0, devices - 1)], sems.at[1])
    piece[:tall] = (jnp.sum(rem_in[...].astype(jnp.float32), axis=0) * rem_scale).astype(jnp.bfloat16)
    piece[tall:] = (jnp.sum(sums_in[...], axis=0) * scale).astype(jnp.bfloat16)
    lax.fori_loop(1, half, send_total, 0)
    keep(piece, whole.at[me])
    drain(grads_in.at[pl.ds(0, slots - slot_cap)], sems.at[3])
    drain(whole.at[pl.ds(0, half - 1)], sems.at[5])
    lax.fori_loop(0, half // peers, relay, 0)

    def collect(r, carry):
        quot_ref[cut(r), :] = dot(pick_rows(asked_ref[...], r * size, size), grads_in[...])
        return carry

    lax.fori_loop(0, quot_ref.shape[0] // size, collect, 0)
    drain(whole.at[pl.ds(0, half)], sems.at[10])

    def lay(k, carry):
        for part in range(across):
            got = whole[k * across + part].astype(jnp.float32)
            lanes = slice(part * wide, (part + 1) * wide)
            total_ref[pl.ds(pl.multiple_of(k * tall, tall), tall), lanes] = got[:tall]
            weight_ref[pl.ds(pl.multiple_of(k * 8, 8), 8), lanes] = got[tall : tall + 8]
        return carry

    lax.fori_loop(0, devices // across, lay, 0)
    for d in range(devices // peers):
        bias_ref[d : d + 1, :] = whole[d * peers, tall + 8 : tall + 16, :].astype(jnp.float32)[0:1]
    drain(rem_in.at[pl.ds(0, devices - 1)], sems.at[0])
    drain(grads_in.at[pl.ds(0, slots - slot_cap)], sems.at[2])
    drain(whole.at[pl.ds(0, half - 1)], sems.at[4])
    drain(whole.at[pl.ds(0, half)], sems.at[9])
    drain(sums_in.at[pl.ds(0, peers - 1)], sems.at[7])


def spread_grads(grad, qv, rv, slot_row, rem_row, asked_row, sums, table_rows, rem_rows, peers, rem_scale, scale):
    nodes, width = grad.shape
    slots = asked_row.shape[1]
    doms = lax.axis_size("dom")
    devices = doms * peers
    wide = LANES
    tall = rem_rows * width // devices // wide
    kind = jnp.bfloat16
    vmem = pl.BlockSpec(memory_space=pltpu.VMEM)
    return pl.pallas_call(
        functools.partial(spread_kernel, devices, rem_scale, scale),
        out_shape=(
            jax.ShapeDtypeStruct((table_rows, width), jnp.float32),
            jax.ShapeDtypeStruct((rem_rows, width), jnp.float32),
            jax.ShapeDtypeStruct((doms * (sums.shape[0] - 8), width), jnp.float32),
            jax.ShapeDtypeStruct((doms, wide), jnp.float32),
        ),
        in_specs=[vmem] * 7,
        out_specs=(vmem, vmem, vmem, vmem),
        scratch_shapes=[
            pltpu.VMEM((slots, width), kind),
            pltpu.VMEM((rem_rows, width), kind),
            pltpu.VMEM((nodes, width), kind),
            pltpu.VMEM((slots, width), kind),
            pltpu.VMEM((devices, tall, wide), kind),
            pltpu.VMEM((peers, 16, wide), jnp.float32),
            pltpu.VMEM((tall + 16, wide), kind),
            pltpu.VMEM((devices, tall + 16, wide), kind),
            pltpu.SemaphoreType.DMA((11,)),
        ],
        compiler_params=pltpu.CompilerParams(
            collective_id=2, has_side_effects=True, vmem_limit_bytes=40 << 20
        ),
        name="spread_grads",
    )(grad, qv, rv, slot_row, rem_row, asked_row, sums)


def forward_kernel(
    counts_ref, rows_ref, halo_counts_ref, low_ref, high_ref, deg_ref, x_ref, w_self_ref, w_neigh_ref, bias_ref, cot_ref,
    out_ref, grad_ref, halo_ref, dx_ref, weights_ref, total, acc_self, acc_neigh
):
    k = pl.program_id(0)
    nodes, feats = total.shape
    tile = 256

    def cut(r):
        return pl.ds(pl.multiple_of(r * tile, tile), tile)

    @pl.when(k == 0)
    def _():
        def start(r, carry):
            low = dot(halo_counts_ref[cut(r), :HALO], low_ref[...])
            total[cut(r), :] = low + dot(halo_counts_ref[cut(r), HALO:], high_ref[...])
            return carry

        lax.fori_loop(0, nodes // tile, start, 0)

    total[...] += dot(counts_ref[...], rows_ref[...])

    @pl.when(k == pl.num_programs(0) - 1)
    def _():
        acc_self[...] = jnp.zeros_like(acc_self)
        acc_neigh[...] = jnp.zeros_like(acc_neigh)

        def layer(r, bias_sum):
            rows = cut(r)
            divisor = jnp.maximum(deg_ref[rows, :], 1.0)
            x = x_ref[rows, :]
            neighbour = (total[rows, :] / divisor).astype(jnp.bfloat16)
            preact = dot(x, w_self_ref[...]) + dot(neighbour, w_neigh_ref[...]) + bias_ref[...]
            sigma = jax.nn.sigmoid(preact)
            out_ref[rows, :] = (preact * sigma).astype(jnp.bfloat16)
            slope = sigma * (1.0 + preact * (1.0 - sigma))
            dpre = (cot_ref[rows, :].astype(jnp.float32) * slope).astype(jnp.bfloat16)
            scaled = dot(dpre, w_neigh_ref[...], COLS) / divisor
            grad_ref[:, rows] = scaled.T.astype(jnp.bfloat16)
            dx_ref[rows, :] = dot(dpre, w_self_ref[...], COLS)
            acc_self[...] += dot(x, dpre, ROWS)
            acc_neigh[...] += dot(neighbour, dpre, ROWS)
            return bias_sum + jnp.sum(dpre.astype(jnp.float32), axis=0, keepdims=True)

        bias_sum = lax.fori_loop(0, nodes // tile, layer, jnp.zeros((1, feats), jnp.float32))
        halo_ref[...] = dot(grad_ref[...], halo_counts_ref[...]).T.astype(jnp.bfloat16)
        doms = weights_ref.shape[0]
        each = 2 * feats // doms
        wide = feats // doms
        spread = jnp.broadcast_to(bias_sum, (8, feats))
        for c in range(doms):
            source, at = (acc_self, c * each) if c * each < feats else (acc_neigh, c * each - feats)
            weights_ref[c, :each, :] = source[at : at + each, :]
            shift = (feats - c * wide) % feats
            weights_ref[c, each:, :] = pltpu.roll(spread, shift, 1) if shift else spread


def forward(counts, gathered, halo_counts, low_rows, high_rows, degree, features, w_self, w_neigh, bias, cotangent, doms):
    nodes, feats = features.shape
    wide = 4 * nodes
    steps = counts.shape[1] // wide

    def whole(array):
        return pl.BlockSpec(array.shape, lambda k: (0,) * len(array.shape))

    out_shape = (
        jax.ShapeDtypeStruct((nodes, feats), jnp.bfloat16),
        jax.ShapeDtypeStruct((feats, nodes), jnp.bfloat16),
        jax.ShapeDtypeStruct((2 * HALO, feats), jnp.bfloat16),
        jax.ShapeDtypeStruct((nodes, feats), jnp.float32),
        jax.ShapeDtypeStruct((doms, 2 * feats // doms + 8, feats), jnp.float32),
    )
    kept = (halo_counts, low_rows, high_rows, degree, features, w_self, w_neigh, bias, cotangent)
    return pl.pallas_call(
        forward_kernel,
        grid=(steps,),
        out_shape=out_shape,
        in_specs=[
            pl.BlockSpec((nodes, wide), lambda k: (0, k)),
            pl.BlockSpec((wide, feats), lambda k: (k, 0)),
        ]
        + [whole(array) for array in kept],
        out_specs=tuple(whole(array) for array in out_shape),
        scratch_shapes=[
            pltpu.VMEM((nodes, feats), jnp.float32),
            pltpu.VMEM((feats, feats), jnp.float32),
            pltpu.VMEM((feats, feats), jnp.float32),
        ],
        compiler_params=pltpu.CompilerParams(vmem_limit_bytes=60 << 20),
        name="forward_layer",
    )(counts, gathered, *kept)


def reduce_kernel(
    counts_ref, grad_ref, weights_ref, halo_ref, dx_ref, out_ref, sums_ref, load, part, mid, fin, half_sum, mid2, fin2, sems_load, s_out, s_mid, s_fin, t_out, t_mid, t_fin, weights_in, w_out, w_in, halo_in, own, h_out, h_in, dx_in, mine_in, s_own
):
    side = 4
    nodes = grad_ref.shape[1]
    feats = grad_ref.shape[0] // 2
    span = nodes // 2
    dom = lax.axis_index("dom")
    blk = lax.axis_index("blk")
    x, y = blk // side, lax.rem(blk, side)

    def at(dx, dy):
        return lax.rem(x + dx, side) * side + lax.rem(y + dy, side)

    def device(half, first, second):
        dx, dy = (first, second) if half == 0 else (second, first)
        return (dom, at(dx, dy))

    barrier = pltpu.get_barrier_semaphore()
    for dx, dy in ((1, 0), (3, 0), (0, 1), (0, 3)):
        pl.semaphore_signal(barrier, inc=1, device_id=(dom, at(dx, dy)), device_id_type=MESH)
    doms = weights_ref.shape[0]
    for k in range(1, doms):
        pl.semaphore_signal(barrier, inc=1, device_id=(lax.rem(dom + k, doms), blk), device_id_type=MESH)

    order = [(2, 2), (2, 1), (1, 2), (2, 3), (3, 2), (2, 0), (0, 2), (1, 1), (3, 3), (1, 3), (3, 1)]
    order += [(1, 0), (0, 1), (3, 0), (0, 3), (0, 0)]
    depth = load.shape[0]

    def fetch(i):
        dx, dy = order[i]
        columns = pl.ds(pl.multiple_of(at(dx, dy) * nodes, nodes), nodes)
        return pltpu.make_async_copy(counts_ref.at[:, columns], load.at[i % depth], sems_load.at[i % depth])

    for i in range(depth - 1):
        fetch(i).start()
    own_dx = pltpu.make_async_copy(dx_ref, dx_in, s_own.at[0])
    own_dx.start()
    own_weights = pltpu.make_async_copy(weights_ref.at[dom], mine_in, s_own.at[1])
    own_weights.start()
    pl.semaphore_wait(barrier, 4 + doms - 1)

    def to_dom(k):
        other = lax.rem(dom + k, doms)
        return pltpu.make_async_remote_copy(
            src_ref=weights_ref.at[other],
            dst_ref=weights_in.at[k],
            send_sem=w_out.at[k],
            recv_sem=w_in.at[k],
            device_id=(other, blk),
            device_id_type=MESH,
        )

    halo = halo_in.shape[1]

    def to_side(side_index):
        return pltpu.make_async_remote_copy(
            src_ref=halo_ref.at[pl.ds(side_index * halo, halo)],
            dst_ref=halo_in.at[side_index],
            send_sem=h_out.at[side_index],
            recv_sem=h_in.at[side_index],
            device_id=(lax.rem(dom + (doms - 1 if side_index == 0 else 1), doms), blk),
            device_id_type=MESH,
        )

    for k in range(1, doms):
        to_dom(k).start()
    to_side(0).start()
    to_side(1).start()

    def remote(src, dst, half, first, second, send_sem, recv_sem):
        return pltpu.make_async_remote_copy(
            src_ref=src,
            dst_ref=dst,
            send_sem=send_sem,
            recv_sem=recv_sem,
            device_id=device(half, first, second),
            device_id_type=MESH,
        )

    def along(unit):
        return unit % 2 == 0

    def to_mid(half, unit):
        return remote(
            part.at[half, 2, unit], mid.at[half, unit], half, 1 if along(unit) else 3, 0,
            s_out.at[half, 0, unit], s_mid.at[half, unit],
        )

    def to_fin(half, first, unit):
        way = 0 if first == 1 else 1
        return remote(
            part.at[half, first, unit], fin.at[half, way, unit], half, first, 0,
            s_out.at[half, 1 + way, unit], s_fin.at[half, way, unit],
        )

    def relays(first, unit):
        return along(unit) == (first == 1)

    tile = 256
    waiting = []
    for i, (dx, dy) in enumerate(order):
        if i + depth - 1 < len(order):
            fetch(i + depth - 1).start()
        fetch(i).wait()

        def columns(n, carry, slot=i % depth, dx=dx, dy=dy):
            cut = pl.ds(pl.multiple_of(n * tile, tile), tile)
            value = jnp.dot(grad_ref[...], load[slot, :, cut], preferred_element_type=jnp.float32)
            part[0, dx, dy, :, cut] = value[:feats].astype(jnp.bfloat16)
            part[1, dy, dx, :, cut] = value[feats:].astype(jnp.bfloat16)
            return carry

        lax.fori_loop(0, nodes // tile, columns, 0)
        for half, first, unit in ((0, dx, dy), (1, dy, dx)):
            if first == 2:
                to_mid(half, unit).start()
            elif first != 0:
                if relays(first, unit):
                    waiting.append((half, first, unit))
                else:
                    to_fin(half, first, unit).start()
    waiting.sort(key=lambda item: (2, 1, 3, 0).index(item[2]))
    for half, first, unit in waiting:
        to_mid(half, unit).wait_recv()
        mine = part[half, first, unit].astype(jnp.float32)
        part[half, first, unit] = (mine + mid[half, unit].astype(jnp.float32)).astype(jnp.bfloat16)
        to_fin(half, first, unit).start()

    def cut(piece):
        return pl.ds(piece * span, span)

    def to_mid2(half, piece):
        return remote(
            half_sum.at[half, 1, :, cut(piece)], mid2.at[half, piece], half, 0, 1 if piece == 0 else 3,
            t_out.at[half, 0, piece], t_mid.at[half, piece],
        )

    def to_fin2(half, second, piece):
        way = 0 if second == 1 else 1
        return remote(
            half_sum.at[half, 0 if second == 1 else 2, :, cut(piece)], fin2.at[half, way, piece], half, 0, second,
            t_out.at[half, 1 + way, piece], t_fin.at[half, way, piece],
        )

    def summed(half, unit):
        to_fin(half, 1, unit).wait_recv()
        to_fin(half, 3, unit).wait_recv()
        total = part[half, 0, unit].astype(jnp.float32) + fin[half, 0, unit].astype(jnp.float32)
        return total + fin[half, 1, unit].astype(jnp.float32)

    for half in range(2):
        half_sum[half, 1] = summed(half, 2).astype(jnp.bfloat16)
        to_mid2(half, 0).start()
        to_mid2(half, 1).start()
    for second in (1, 3):
        direct, relayed = (1, 0) if second == 1 else (0, 1)
        for half in range(2):
            half_sum[half, second - 1] = summed(half, second).astype(jnp.bfloat16)
            to_fin2(half, second, direct).start()
    for second in (1, 3):
        direct, relayed = (1, 0) if second == 1 else (0, 1)
        for half in range(2):
            to_mid2(half, relayed).wait_recv()
            mine = half_sum[half, second - 1, :, cut(relayed)].astype(jnp.float32)
            both = mine + mid2[half, relayed].astype(jnp.float32)
            half_sum[half, second - 1, :, cut(relayed)] = both.astype(jnp.bfloat16)
            to_fin2(half, second, relayed).start()
    for half in range(2):
        own[half * feats : (half + 1) * feats, :] = summed(half, 0)
    to_side(0).wait_recv()
    to_side(1).wait_recv()
    own_dx.wait()
    for half in range(2):
        rows = slice(half * feats, (half + 1) * feats)
        for piece in range(2):
            to_fin2(half, 1, piece).wait_recv()
            to_fin2(half, 3, piece).wait_recv()
            total = own[rows, piece * span : (piece + 1) * span] + fin2[half, 0, piece].astype(jnp.float32)
            total = (total + fin2[half, 1, piece].astype(jnp.float32)).T
            near = slice(piece * span, (piece + 1) * span)
            out_ref[near, rows] = dx_in[near, rows] + total
            edge = slice(0, halo) if piece == 0 else slice(nodes - halo, nodes)
            out_ref[edge, rows] += halo_in[1 - piece, :, rows].astype(jnp.float32)
    to_side(0).wait_send()
    to_side(1).wait_send()
    own_weights.wait()
    sums = mine_in[...]
    for k in range(1, doms):
        to_dom(k).wait_recv()
        sums = sums + weights_in[k]
    sums_ref[...] = sums
    for k in range(1, doms):
        to_dom(k).wait_send()
    for half in range(2):
        for unit in range(side):
            to_mid(half, unit).wait_send()
            to_fin(half, 1, unit).wait_send()
            to_fin(half, 3, unit).wait_send()
        for piece in range(2):
            to_mid2(half, piece).wait_send()
            to_fin2(half, 1, piece).wait_send()
            to_fin2(half, 3, piece).wait_send()


def reduce_sources(counts, grad, weights, halo, dx):
    feats, nodes = grad.shape
    half = feats // 2
    kind = jnp.bfloat16
    dma = pltpu.SemaphoreType.DMA
    vmem = pl.BlockSpec(memory_space=pltpu.VMEM)
    anywhere = pl.BlockSpec(memory_space=pl.ANY)
    return pl.pallas_call(
        reduce_kernel,
        out_shape=(
            jax.ShapeDtypeStruct((nodes, feats), jnp.float32),
            jax.ShapeDtypeStruct(weights.shape[1:], jnp.float32),
        ),
        in_specs=[anywhere, vmem, anywhere, anywhere, anywhere],
        out_specs=(vmem, vmem),
        scratch_shapes=[
            pltpu.VMEM((3, nodes, nodes), kind),
            pltpu.VMEM((2, 4, 4, half, nodes), kind),
            pltpu.VMEM((2, 4, half, nodes), kind),
            pltpu.VMEM((2, 2, 4, half, nodes), kind),
            pltpu.VMEM((2, 3, half, nodes), kind),
            pltpu.VMEM((2, 2, half, nodes // 2), kind),
            pltpu.VMEM((2, 2, 2, half, nodes // 2), kind),
            dma((3,)),
            dma((2, 3, 4)),
            dma((2, 4)),
            dma((2, 2, 4)),
            dma((2, 3, 2)),
            dma((2, 2)),
            dma((2, 2, 2)),
            pltpu.VMEM(weights.shape, jnp.float32),
            dma((weights.shape[0],)),
            dma((weights.shape[0],)),
            pltpu.VMEM((2, halo.shape[0] // 2, feats), kind),
            pltpu.VMEM((feats, nodes), jnp.float32),
            dma((2,)),
            dma((2,)),
            pltpu.VMEM((nodes, feats), jnp.float32),
            pltpu.VMEM(weights.shape[1:], jnp.float32),
            dma((2,)),
        ],
        compiler_params=pltpu.CompilerParams(
            collective_id=3, has_side_effects=True, vmem_limit_bytes=60 << 20
        ),
        name="reduce_sources",
    )(counts, grad, weights, halo, dx)


def shifted(block, axis, distance):
    devices = range(lax.axis_size(axis))
    route = [((i - distance) % len(devices), i) for i in devices]
    return lax.ppermute(block, axis, route)


def dot(a, b, dims=(((1,), (0,)), ((), ()))):
    return lax.dot_general(a, b, dims, preferred_element_type=jnp.float32)


def per_device(
    node_owner,
    node_qrow,
    node_rem,
    quotient,
    remainder,
    edge_src,
    edge_dst,
    block_count,
    w_self,
    w_neigh,
    bias,
    cotangent,
):
    nodes_dev = node_qrow.shape[0]
    feature_dim = quotient.shape[1]
    devices = lax.axis_size("dom") * lax.axis_size("blk")
    part_nodes = nodes_dev * lax.axis_size("blk")
    doms = lax.axis_size("dom")
    features, quot_rows, remain_rows, asked_row, slot_row, fast, slow, flags, first, last = fetch_rows(
        node_owner.reshape(1, -1),
        node_qrow[None],
        node_rem[None],
        quotient,
        remainder,
        edge_src,
        edge_dst,
        block_count,
        devices,
        part_nodes,
    )
    part_gathered = lax.all_gather(features, "blk", axis=0, tiled=True)
    low_rows = shifted(last, "dom", 1)
    high_rows = shifted(first, "dom", -1)

    counts, halo_counts, degree = build_counts(fast, slow, flags, block_count, part_nodes)
    out, grad_t, halo_grads, dx_self, weights = forward(
        counts, part_gathered, halo_counts, low_rows, high_rows, degree, features, w_self, w_neigh, bias[None], cotangent, doms
    )
    grad_x, weight_sums = reduce_sources(counts, grad_t, weights, halo_grads, dx_self)
    nodes_total = nodes_dev * devices
    weight_scale = 1.0 / math.sqrt(nodes_total)
    remain_scale = math.sqrt(remainder.shape[0] / nodes_total)
    d_quotient, d_remainder, d_weights, d_bias = spread_grads(
        grad_x,
        quot_rows,
        remain_rows,
        slot_row,
        node_rem[None],
        asked_row,
        weight_sums,
        quotient.shape[0],
        remainder.shape[0],
        lax.axis_size("blk"),
        remain_scale,
        weight_scale,
    )
    d_self, d_neigh = d_weights[:feature_dim], d_weights[feature_dim:]
    d_bias = d_bias[:, : feature_dim // doms].reshape(-1)
    return (out, d_quotient, d_remainder, d_self, d_neigh, d_bias)


def solution(mesh):
    both = P(AXES)
    rows = P(AXES, None)
    return jax.shard_map(
        per_device,
        mesh=mesh,
        in_specs=(rows, both, both, rows, P(), rows, rows, both, P(), P(), P(), rows),
        out_specs=(rows, rows, P(), P(), P(), P()),
        check_vma=False,
    )
```

```python
import functools
import math

import jax
import jax.numpy as jnp
from jax import lax
from jax.experimental import pallas as pl
from jax.experimental.pallas import tpu as pltpu
from jax.sharding import PartitionSpec as P

ROWS_BLK = 128
HALO = 256
LANES = 128
BATCH = 8
AXES = ("dom", "blk")
MESH = pl.DeviceIdType.MESH
ROWS = (((0,), (0,)), ((), ()))
COLS = (((1,), (1,)), ((), ()))


def place_edges(dump, src_ref, dst_ref, counts, fast_ref, slow_ref, flag_ref):
    blocks, slots = src_ref.shape
    src = src_ref[...]
    lane = lax.broadcasted_iota(jnp.int32, (blocks, slots), 1)
    cell = ((src >> 7) * ROWS_BLK + dst_ref[...]) * LANES + (src & 127)
    live = lane < counts
    spare = dump * LANES
    cell = jnp.where(live, cell, spare)
    row = cell >> 7
    clash = jnp.zeros((blocks, slots), jnp.bool_)
    place = lane & (BATCH - 1)
    for s in range(1, BATCH):
        clash = clash | ((pltpu.roll(row, s, 1) == row) & (place >= s))
    clash = clash & live
    fast_ref[:, 0, :] = jnp.where(clash, spare, cell)
    slow_ref[:, 0, :] = jnp.where(clash, cell, spare)
    ones = jnp.where(clash, 1.0, 0.0).astype(jnp.bfloat16)
    chunks = slots // LANES
    col = lax.broadcasted_iota(jnp.int32, (blocks, LANES), 1)
    into = lax.broadcasted_iota(jnp.int32, (LANES, LANES), 0) // BATCH
    group = (into == lax.broadcasted_iota(jnp.int32, (LANES, LANES), 1)).astype(jnp.bfloat16)
    found = jnp.zeros((blocks, LANES), jnp.int32)
    number = jnp.zeros((blocks, 1), jnp.int32)
    for c in range(chunks):
        hits = jnp.dot(ones[:, c * LANES : (c + 1) * LANES], group, preferred_element_type=jnp.float32)
        bits = jnp.sum(jnp.where(hits > 0.5, (1 << (col & (LANES // BATCH - 1))).astype(jnp.float32), 0.0), axis=1, keepdims=True)
        bits = bits.astype(jnp.int32)
        some = bits > 0
        found = found + jnp.where((col == number) & some, c * 65536 + bits, 0)
        number = number + some.astype(jnp.int32)
    flag_ref[:, 0, :] = jnp.where(col == LANES - 1, number, found)


def count_kernel(dump, count_ref, fast_ref, slow_ref, flag_ref, main_ref, halo_ref, deg_ref, *cells):
    j = pl.program_id(0)
    blocks = pl.num_programs(0) - 1
    his = dump // ROWS_BLK
    his_main = main_ref.shape[1] // LANES
    zero = jnp.zeros((ROWS_BLK, LANES), jnp.float32)
    lanes = lax.broadcasted_iota(jnp.int32, (1, LANES), 1)

    @pl.when(j == 0)
    def _():
        def clear(i, carry):
            for ref in cells[:2]:
                ref[pl.ds(pl.multiple_of(i * ROWS_BLK, ROWS_BLK), ROWS_BLK), :] = zero
            return carry

        lax.fori_loop(0, his, clear, 0)
        for ref in cells:
            ref[pl.ds(dump, 8), :] = jnp.zeros((8, LANES), jnp.float32)

    count = jnp.where(j < blocks, count_ref[jnp.minimum(j, blocks - 1)], 0)
    pairs = (count + 4 * BATCH - 1) // (4 * BATCH)

    def add_batch(ref, first):
        keys = [fast_ref[0, 0, first + i] for i in range(BATCH)]
        rows = [k >> 7 for k in keys]
        olds = [ref[pl.ds(r, 1), :] for r in rows]
        news = [old + jnp.where(lanes == (k & 127), 1.0, 0.0) for old, k in zip(olds, keys)]
        for r, new in zip(rows, news):
            ref[pl.ds(r, 1), :] = new

    def turn(fill, leave):
        def add_pair(t, carry):
            for i in range(4):
                add_batch(fill[i % 2], (t * 4 + i) * BATCH)
            return carry

        def flush(ref, first):
            def step(h, total):
                at = pl.multiple_of((first + h) * ROWS_BLK, ROWS_BLK)
                rows = pl.ds(at, ROWS_BLK)
                value = leave[0][rows, :] + leave[1][rows, :]
                ref[:, pl.ds(pl.multiple_of(h * LANES, LANES), LANES)] = value.astype(jnp.bfloat16)
                leave[0][rows, :] = zero
                leave[1][rows, :] = zero
                return total + value

            return step

        def both(t, total):
            add_pair(t, 0)
            for i in range(2):
                total = flush(main_ref, 0)(t * 2 + i, total)
            return total

        steps = his_main
        joint = jnp.minimum(pairs, steps // 2)
        total = lax.fori_loop(0, joint, both, zero)
        lax.fori_loop(joint, pairs, add_pair, 0)
        total = lax.fori_loop(joint * 2, steps, flush(main_ref, 0), total)

        total = lax.fori_loop(0, his - his_main, flush(halo_ref, his_main), total)
        deg_ref[...] = jnp.sum(total, axis=1, keepdims=True)

        def chunk(c, carry):
            entry = flag_ref[0, 0, c]
            first = (entry >> 16) * LANES

            def some(g, inner):
                @pl.when(((entry >> g) & 1) != 0)
                def _():
                    for i in range(BATCH):
                        k = slow_ref[0, 0, first + g * BATCH + i]
                        r = k >> 7
                        old = fill[0][pl.ds(r, 1), :]
                        fill[0][pl.ds(r, 1), :] = old + jnp.where(lanes == (k & 127), 1.0, 0.0)

                return inner

            lax.fori_loop(0, LANES // BATCH, some, 0)
            return carry

        lax.fori_loop(0, jnp.where(j < blocks, flag_ref[0, 0, LANES - 1], 0), chunk, 0)

    @pl.when(lax.rem(j, 2) == 0)
    def _():
        turn(cells[:2], cells[2:])

    @pl.when(lax.rem(j, 2) == 1)
    def _():
        turn(cells[2:], cells[:2])


def build_counts(fast, slow, flags, block_count, part_nodes):
    blocks, _, slots = fast.shape
    width = part_nodes + 2 * HALO
    dump = width // LANES * ROWS_BLK
    nodes = blocks * ROWS_BLK

    def filled(j):
        return (jnp.minimum(j, blocks - 1), 0, 0)

    def left(j):
        return (jnp.maximum(j - 1, 0), 0)

    return pl.pallas_call(
        functools.partial(count_kernel, dump),
        grid=(blocks + 1,),
        out_shape=(
            jax.ShapeDtypeStruct((nodes, part_nodes), jnp.bfloat16),
            jax.ShapeDtypeStruct((nodes, 2 * HALO), jnp.bfloat16),
            jax.ShapeDtypeStruct((nodes, 1), jnp.float32),
        ),
        in_specs=[
            pl.BlockSpec(memory_space=pltpu.SMEM),
            pl.BlockSpec((1, 1, slots), filled, memory_space=pltpu.SMEM),
            pl.BlockSpec((1, 1, slots), filled, memory_space=pltpu.SMEM),
            pl.BlockSpec((1, 1, LANES), filled, memory_space=pltpu.SMEM),
        ],
        out_specs=(
            pl.BlockSpec((ROWS_BLK, part_nodes), left),
            pl.BlockSpec((ROWS_BLK, 2 * HALO), left),
            pl.BlockSpec((ROWS_BLK, 1), left),
        ),
        scratch_shapes=[pltpu.VMEM((dump + 8, LANES), jnp.float32)] * 4,
        compiler_params=pltpu.CompilerParams(vmem_limit_bytes=60 << 20),
        cost_estimate=pl.CostEstimate(flops=80_000_000_000, bytes_accessed=40_000_000, transcendentals=0),
        name="edge_counts",
    )(block_count, fast, slow, flags)


def ring_place():
    blk = lax.axis_size("blk")
    return lax.axis_index("dom") * blk + lax.axis_index("blk")


def greet_all(devices):
    me = ring_place()

    def greet(k, carry):
        other = lax.rem(me + k, devices)
        barrier = pltpu.get_barrier_semaphore()
        pl.semaphore_signal(barrier, inc=1, device_id=coords(other), device_id_type=MESH)
        return carry

    lax.fori_loop(1, devices, greet, 0)


def meet_all(devices):
    pl.semaphore_wait(pltpu.get_barrier_semaphore(), devices - 1)


def as_row(column):
    wide = jnp.broadcast_to(column.astype(jnp.float32), (column.shape[0], LANES))
    return wide.T[0:1].astype(jnp.int32)


def as_column(row):
    tall = jnp.broadcast_to(row.astype(jnp.float32), (LANES, row.shape[1]))
    return tall.T[:, 0:1].astype(jnp.int32)


def pick(column, first, size):
    lane = lax.broadcasted_iota(jnp.int32, (column.shape[0], size), 1) + first
    return (lane == column).astype(jnp.bfloat16)


def pick_rows(row, first, size):
    line = lax.broadcasted_iota(jnp.int32, (size, row.shape[1]), 0) + first
    return (line == row).astype(jnp.bfloat16)


def coords(device):
    blk = lax.axis_size("blk")
    return (device // blk, lax.rem(device, blk))


def send(src, dst, device, send_sem, recv_sem):
    pltpu.make_async_remote_copy(
        src_ref=src,
        dst_ref=dst,
        send_sem=send_sem,
        recv_sem=recv_sem,
        device_id=coords(device),
        device_id_type=MESH,
    ).start()


def drain(ref, sem):
    pltpu.make_async_copy(ref, ref, sem).wait()


def fetch_kernel(
    devices, dump, owner_row, qrow_row, rem_row, table_hbm, remainder_hbm, src_hbm, dst_hbm, count_ref,
    x_ref, qv_ref, rv_ref, asked_ref, slot_ref, fast_ref, slow_ref, flag_ref, first_ref, last_ref,
    ids_out, ids_in, served, rows_in, slot_col, slot_hot, owner_ref, qrow_ref, rem_ref, table_ref, remainder_ref,
    src_ref, dst_ref, sems
):
    slots, width = served.shape
    slot_cap = slots // devices
    nodes = owner_ref.shape[0]
    me = ring_place()
    tile = 256
    greet_all(devices)
    loads = [
        pltpu.make_async_copy(table_hbm, table_ref, sems.at[5]),
        pltpu.make_async_copy(remainder_hbm, remainder_ref, sems.at[6]),
        pltpu.make_async_copy(src_hbm, src_ref, sems.at[7]),
        pltpu.make_async_copy(dst_hbm, dst_ref, sems.at[8]),
    ]
    for load in loads:
        load.start()

    def cut(r):
        return pl.ds(pl.multiple_of(r * tile, tile), tile)

    owner_ref[...] = as_column(owner_row[...])
    qrow_ref[...] = as_column(qrow_row[...])
    rem_ref[...] = as_column(rem_row[...])

    owner_hot = pick(owner_ref[...], 0, devices)
    lane = lax.broadcasted_iota(jnp.int32, (tile, devices), 1)
    wish = jnp.zeros((devices, devices), jnp.float32)
    for r in range(nodes // tile):
        rows = slice(r * tile, (r + 1) * tile)
        line = lax.broadcasted_iota(jnp.int32, (tile, nodes), 0) + r * tile
        before = (line > lax.broadcasted_iota(jnp.int32, (tile, nodes), 1)).astype(jnp.bfloat16)
        mine = owner_hot[rows]
        rank = jnp.sum(dot(before, owner_hot) * mine.astype(jnp.float32), axis=1, keepdims=True).astype(jnp.int32)
        slot_col[rows, :] = owner_ref[rows, :] * slot_cap + rank
        qrow = qrow_ref[rows, :]
        parts = jnp.where(lane == rank, qrow >> 5, 0) + jnp.where(lane == rank + slot_cap, qrow & 31, 0)
        wish = wish + dot(mine, parts.astype(jnp.float32).astype(jnp.bfloat16), ROWS)
    ids_out[:, 0, :] = wish
    meet_all(devices)

    def ask(k, carry):
        other = lax.rem(me + k, devices)
        send(ids_out.at[other], ids_in.at[me], other, sems.at[0], sems.at[1])
        return carry

    lax.fori_loop(1, devices, ask, 0)
    loads[1].wait()

    def remain(r, carry):
        rows = cut(r)
        rv_ref[rows, :] = dot(pick(rem_ref[rows, :], 0, remainder_ref.shape[0]), remainder_ref[...]).astype(jnp.bfloat16)
        return carry

    lax.fori_loop(0, nodes // tile, remain, 0)
    slot_ref[...] = as_row(slot_col[...])
    own = pltpu.make_async_copy(ids_out.at[me], ids_in.at[me], sems.at[2])
    own.start()
    own.wait()
    loads[0].wait()
    drain(ids_in.at[pl.ds(0, devices - 1)], sems.at[1])
    ids = ids_in[:, 0, :].astype(jnp.bfloat16)
    step = 16
    part = step * slot_cap
    slot = lax.broadcasted_iota(jnp.int32, (part, devices), 0)
    place = lax.broadcasted_iota(jnp.int32, (part, devices), 1)
    rank_of = lax.rem(slot, slot_cap)
    weight = jnp.where(place == rank_of, 32.0, 0.0) + jnp.where(place == rank_of + slot_cap, 1.0, 0.0)

    def serve(c, carry):
        turn = lax.rem(c + me // step, devices // step)
        whose = (place - turn * step == slot // slot_cap).astype(jnp.bfloat16)
        asked = jnp.sum(dot(whose, ids) * weight, axis=1, keepdims=True).astype(jnp.int32)
        at = pl.multiple_of(turn * part, part)
        asked_ref[:, pl.ds(at, part)] = as_row(asked)
        served[pl.ds(at, part), :] = dot(pick(asked, 0, table_ref.shape[0]), table_ref[...]).astype(jnp.bfloat16)

        def back(i, inner):
            other = turn * step + lax.rem(me + i, step)

            @pl.when(other != me)
            def _():
                send(
                    served.at[pl.ds(pl.multiple_of(other * slot_cap, slot_cap), slot_cap)],
                    rows_in.at[pl.ds(pl.multiple_of(me * slot_cap, slot_cap), slot_cap)],
                    other,
                    sems.at[3],
                    sems.at[4],
                )

            return inner

        lax.fori_loop(0, step, back, 0)
        return carry

    lax.fori_loop(0, devices // step, serve, 0)
    mine = pl.ds(pl.multiple_of(me * slot_cap, slot_cap), slot_cap)
    own_rows = pltpu.make_async_copy(served.at[mine], rows_in.at[mine], sems.at[2])
    own_rows.start()

    def prepare(r, carry):
        slot_hot[cut(r), :] = pick(slot_col[cut(r), :], 0, slots)
        return carry

    lax.fori_loop(0, nodes // tile, prepare, 0)
    loads[2].wait()
    loads[3].wait()
    blocks = src_ref.shape[0]
    which = lax.broadcasted_iota(jnp.int32, (blocks, 1), 0)
    counts = jnp.zeros((blocks, 1), jnp.int32)
    for j in range(blocks):
        counts = counts + jnp.where(which == j, count_ref[j], 0)
    place_edges(dump, src_ref, dst_ref, counts, fast_ref, slow_ref, flag_ref)
    own_rows.wait()
    drain(rows_in.at[pl.ds(0, slots - slot_cap)], sems.at[4])

    def finish(r, carry):
        rows = cut(r)
        qv = dot(slot_hot[rows, :], rows_in[...])
        qv_ref[rows, :] = qv.astype(jnp.bfloat16)
        x_ref[rows, :] = (qv * rv_ref[rows, :].astype(jnp.float32)).astype(jnp.bfloat16)
        return carry

    lax.fori_loop(0, nodes // tile, finish, 0)
    first_ref[...] = x_ref[:HALO, :]
    last_ref[...] = x_ref[nodes - HALO :, :]
    drain(ids_in.at[pl.ds(0, devices - 1)], sems.at[0])
    drain(rows_in.at[pl.ds(0, slots - slot_cap)], sems.at[3])


def fetch_rows(owner, qrow, rem, quotient, remainder, edge_src, edge_dst, block_count, devices, part_nodes):
    nodes = owner.shape[1]
    slots = 2 * nodes
    width = quotient.shape[1]
    vmem = pl.BlockSpec(memory_space=pltpu.VMEM)
    anywhere = pl.BlockSpec(memory_space=pl.ANY)
    rows = jax.ShapeDtypeStruct((nodes, width), jnp.bfloat16)
    blocks, edges = edge_src.shape
    edge = jax.ShapeDtypeStruct((blocks, 1, edges), jnp.int32)
    half = jax.ShapeDtypeStruct((HALO, width), jnp.bfloat16)
    dump = (part_nodes + 2 * HALO) // LANES * ROWS_BLK
    column = pltpu.VMEM((nodes, 1), jnp.int32)
    return pl.pallas_call(
        functools.partial(fetch_kernel, devices, dump),
        out_shape=(
            rows,
            rows,
            rows,
            jax.ShapeDtypeStruct((1, slots), jnp.int32),
            jax.ShapeDtypeStruct((1, nodes), jnp.int32),
            edge,
            edge,
            jax.ShapeDtypeStruct((blocks, 1, LANES), jnp.int32),
            half,
            half,
        ),
        in_specs=[vmem] * 3 + [anywhere] * 4 + [pl.BlockSpec(memory_space=pltpu.SMEM)],
        out_specs=(vmem,) * 10,
        scratch_shapes=[
            pltpu.VMEM((devices, 1, devices), jnp.float32),
            pltpu.VMEM((devices, 1, devices), jnp.float32),
            pltpu.VMEM((slots, width), jnp.bfloat16),
            pltpu.VMEM((slots, width), jnp.bfloat16),
            column,
            pltpu.VMEM((nodes, slots), jnp.bfloat16),
            column,
            column,
            column,
            pltpu.VMEM(quotient.shape, jnp.bfloat16),
            pltpu.VMEM(remainder.shape, jnp.bfloat16),
            pltpu.VMEM(edge_src.shape, jnp.int32),
            pltpu.VMEM(edge_src.shape, jnp.int32),
            pltpu.SemaphoreType.DMA((9,)),
        ],
        compiler_params=pltpu.CompilerParams(
            collective_id=1, has_side_effects=True, vmem_limit_bytes=60 << 20
        ),
        name="fetch_rows",
    )(owner, qrow, rem, quotient, remainder, edge_src, edge_dst, block_count)


def spread_kernel(
    devices, rem_scale, scale, grad_ref, qv_ref, rv_ref, slot_ref, node_rem_ref, asked_ref, sums_ref,
    quot_ref, total_ref, weight_ref, bias_ref, grads_ref, rem_ref, by_rv, grads_in, rem_in, sums_in, piece, whole, sems
):
    slot_cap = grads_ref.shape[0] // devices
    slots = grads_ref.shape[0]
    tall, wide = rem_in.shape[1:]
    across = rem_ref.shape[1] // wide
    peers = sums_in.shape[0]
    high = sums_ref.shape[0] - 8
    size = 256
    me = ring_place()
    dom = lax.axis_index("dom")
    blk = lax.axis_index("blk")
    greet_all(devices)

    def cut(r):
        return pl.ds(pl.multiple_of(r * size, size), size)

    by_rv[...] = (grad_ref[...] * qv_ref[...].astype(jnp.float32)).astype(jnp.bfloat16)

    def remain(r, carry):
        rem_ref[cut(r), :] = dot(pick_rows(node_rem_ref[...], r * size, size), by_rv[...]).astype(jnp.bfloat16)
        return carry

    lax.fori_loop(0, rem_ref.shape[0] // size, remain, 0)
    by_rv[...] = (grad_ref[...] * rv_ref[...].astype(jnp.float32)).astype(jnp.bfloat16)
    meet_all(devices)

    def tile(device):
        top = pl.multiple_of(device // across * tall, tall)
        return (pl.ds(top, tall), pl.ds(pl.multiple_of(lax.rem(device, across) * wide, wide), wide))

    def slot(device):
        return pl.ds(pl.multiple_of(device * slot_cap, slot_cap), slot_cap)

    def share(peer):
        top = pl.multiple_of(peer // across * 8, 8)
        return (pl.ds(top, 8), pl.ds(pl.multiple_of(lax.rem(peer, across) * wide, wide), wide))

    def send_rem(k, carry):
        other = lax.rem(me + k, devices)
        send(rem_ref.at[tile(other)], rem_in.at[me], other, sems.at[0], sems.at[1])
        return carry

    def send_sums(k, carry):
        other = lax.rem(blk + k, peers)
        to = dom * peers + other
        send(sums_ref.at[share(other)], sums_in.at[blk, pl.ds(0, 8), :], to, sems.at[7], sems.at[8])
        send(sums_ref.at[pl.ds(high, 8), pl.ds(0, wide)], sums_in.at[blk, pl.ds(8, 8), :], to, sems.at[7], sems.at[8])
        return carry

    step = size // slot_cap

    def send_grads(c, carry):
        turn = lax.rem(c + me // step, devices // step)
        grads_ref[cut(turn), :] = dot(pick_rows(slot_ref[...], turn * size, size), by_rv[...]).astype(jnp.bfloat16)

        def one(i, inner):
            other = turn * step + lax.rem(me + i, step)

            @pl.when(other != me)
            def _():
                send(grads_ref.at[slot(other)], grads_in.at[slot(me)], other, sems.at[2], sems.at[3])

            return inner

        lax.fori_loop(0, step, one, 0)
        return carry

    half = devices // 2
    core = lax.rem(dom, 2)
    twin = (dom + 1 - 2 * core) * peers + blk

    def send_total(k, carry):
        turn = lax.rem(dom // 2 * peers + blk + k, half)
        other = (turn // peers * 2 + core) * peers + lax.rem(turn, peers)
        send(piece, whole.at[me], other, sems.at[4], sems.at[5])
        return carry

    def relay(z, carry):
        group = pl.ds((z * 2 + core) * peers, peers)
        send(whole.at[group], whole.at[group], twin, sems.at[9], sems.at[10])
        return carry

    def keep(src, dst):
        copy = pltpu.make_async_copy(src, dst, sems.at[6])
        copy.start()
        copy.wait()

    lax.fori_loop(1, peers, send_sums, 0)
    lax.fori_loop(1, devices, send_rem, 0)
    lax.fori_loop(0, devices // step // 2, send_grads, 0)
    keep(rem_ref.at[tile(me)], rem_in.at[me])
    keep(sums_ref.at[share(blk)], sums_in.at[blk, pl.ds(0, 8), :])
    keep(sums_ref.at[pl.ds(high, 8), pl.ds(0, wide)], sums_in.at[blk, pl.ds(8, 8), :])
    drain(sums_in.at[pl.ds(0, peers - 1)], sems.at[8])
    drain(rem_in.at[pl.ds(0, devices - 1)], sems.at[1])
    piece[:tall] = (jnp.sum(rem_in[...].astype(jnp.float32), axis=0) * rem_scale).astype(jnp.bfloat16)
    piece[tall:] = (jnp.sum(sums_in[...], axis=0) * scale).astype(jnp.bfloat16)
    lax.fori_loop(1, half, send_total, 0)
    keep(piece, whole.at[me])
    lax.fori_loop(devices // step // 2, devices // step, send_grads, 0)
    keep(grads_ref.at[slot(me)], grads_in.at[slot(me)])
    drain(whole.at[pl.ds(0, half - 1)], sems.at[5])
    lax.fori_loop(0, half // peers, relay, 0)
    drain(grads_in.at[pl.ds(0, slots - slot_cap)], sems.at[3])

    def collect(r, carry):
        quot_ref[cut(r), :] = dot(pick_rows(asked_ref[...], r * size, size), grads_in[...])
        return carry

    lax.fori_loop(0, quot_ref.shape[0] // size, collect, 0)
    drain(whole.at[pl.ds(0, half)], sems.at[10])

    def lay(k, carry):
        for part in range(across):
            got = whole[k * across + part].astype(jnp.float32)
            lanes = slice(part * wide, (part + 1) * wide)
            total_ref[pl.ds(pl.multiple_of(k * tall, tall), tall), lanes] = got[:tall]
            weight_ref[pl.ds(pl.multiple_of(k * 8, 8), 8), lanes] = got[tall : tall + 8]
        return carry

    lax.fori_loop(0, devices // across, lay, 0)
    for d in range(devices // peers):
        bias_ref[d : d + 1, :] = whole[d * peers, tall + 8 : tall + 16, :].astype(jnp.float32)[0:1]
    drain(rem_in.at[pl.ds(0, devices - 1)], sems.at[0])
    drain(grads_in.at[pl.ds(0, slots - slot_cap)], sems.at[2])
    drain(whole.at[pl.ds(0, half - 1)], sems.at[4])
    drain(whole.at[pl.ds(0, half)], sems.at[9])
    drain(sums_in.at[pl.ds(0, peers - 1)], sems.at[7])


def spread_grads(grad, qv, rv, slot_row, rem_row, asked_row, sums, table_rows, rem_rows, peers, rem_scale, scale):
    nodes, width = grad.shape
    slots = asked_row.shape[1]
    doms = lax.axis_size("dom")
    devices = doms * peers
    wide = LANES
    tall = rem_rows * width // devices // wide
    kind = jnp.bfloat16
    vmem = pl.BlockSpec(memory_space=pltpu.VMEM)
    return pl.pallas_call(
        functools.partial(spread_kernel, devices, rem_scale, scale),
        out_shape=(
            jax.ShapeDtypeStruct((table_rows, width), jnp.float32),
            jax.ShapeDtypeStruct((rem_rows, width), jnp.float32),
            jax.ShapeDtypeStruct((doms * (sums.shape[0] - 8), width), jnp.float32),
            jax.ShapeDtypeStruct((doms, wide), jnp.float32),
        ),
        in_specs=[vmem] * 7,
        out_specs=(vmem, vmem, vmem, vmem),
        scratch_shapes=[
            pltpu.VMEM((slots, width), kind),
            pltpu.VMEM((rem_rows, width), kind),
            pltpu.VMEM((nodes, width), kind),
            pltpu.VMEM((slots, width), kind),
            pltpu.VMEM((devices, tall, wide), kind),
            pltpu.VMEM((peers, 16, wide), jnp.float32),
            pltpu.VMEM((tall + 16, wide), kind),
            pltpu.VMEM((devices, tall + 16, wide), kind),
            pltpu.SemaphoreType.DMA((11,)),
        ],
        compiler_params=pltpu.CompilerParams(
            collective_id=2, has_side_effects=True, vmem_limit_bytes=40 << 20
        ),
        name="spread_grads",
    )(grad, qv, rv, slot_row, rem_row, asked_row, sums)


def forward_kernel(
    counts_ref, rows_ref, halo_counts_ref, low_ref, high_ref, deg_ref, x_ref, w_self_ref, w_neigh_ref, bias_ref, cot_ref,
    out_ref, grad_ref, halo_ref, dx_ref, weights_ref, total, acc_self, acc_neigh
):
    k = pl.program_id(0)
    nodes, feats = total.shape
    tile = 256

    def cut(r):
        return pl.ds(pl.multiple_of(r * tile, tile), tile)

    @pl.when(k == 0)
    def _():
        def start(r, carry):
            low = dot(halo_counts_ref[cut(r), :HALO], low_ref[...])
            total[cut(r), :] = low + dot(halo_counts_ref[cut(r), HALO:], high_ref[...])
            return carry

        lax.fori_loop(0, nodes // tile, start, 0)

    total[...] += dot(counts_ref[...], rows_ref[...])

    @pl.when(k == pl.num_programs(0) - 1)
    def _():
        acc_self[...] = jnp.zeros_like(acc_self)
        acc_neigh[...] = jnp.zeros_like(acc_neigh)

        def layer(r, bias_sum):
            rows = cut(r)
            divisor = jnp.maximum(deg_ref[rows, :], 1.0)
            x = x_ref[rows, :]
            neighbour = (total[rows, :] / divisor).astype(jnp.bfloat16)
            preact = dot(x, w_self_ref[...]) + dot(neighbour, w_neigh_ref[...]) + bias_ref[...]
            sigma = jax.nn.sigmoid(preact)
            out_ref[rows, :] = (preact * sigma).astype(jnp.bfloat16)
            slope = sigma * (1.0 + preact * (1.0 - sigma))
            dpre = (cot_ref[rows, :].astype(jnp.float32) * slope).astype(jnp.bfloat16)
            scaled = dot(dpre, w_neigh_ref[...], COLS) / divisor
            grad_ref[:, rows] = scaled.T.astype(jnp.bfloat16)
            dx_ref[rows, :] = dot(dpre, w_self_ref[...], COLS)
            acc_self[...] += dot(x, dpre, ROWS)
            acc_neigh[...] += dot(neighbour, dpre, ROWS)
            return bias_sum + jnp.sum(dpre.astype(jnp.float32), axis=0, keepdims=True)

        bias_sum = lax.fori_loop(0, nodes // tile, layer, jnp.zeros((1, feats), jnp.float32))
        halo_ref[...] = dot(grad_ref[...], halo_counts_ref[...]).T.astype(jnp.bfloat16)
        doms = weights_ref.shape[0]
        each = 2 * feats // doms
        wide = feats // doms
        spread = jnp.broadcast_to(bias_sum, (8, feats))
        for c in range(doms):
            source, at = (acc_self, c * each) if c * each < feats else (acc_neigh, c * each - feats)
            weights_ref[c, :each, :] = source[at : at + each, :]
            shift = (feats - c * wide) % feats
            weights_ref[c, each:, :] = pltpu.roll(spread, shift, 1) if shift else spread


def forward(counts, gathered, halo_counts, low_rows, high_rows, degree, features, w_self, w_neigh, bias, cotangent, doms):
    nodes, feats = features.shape
    wide = 4 * nodes
    steps = counts.shape[1] // wide

    def whole(array):
        return pl.BlockSpec(array.shape, lambda k: (0,) * len(array.shape))

    out_shape = (
        jax.ShapeDtypeStruct((nodes, feats), jnp.bfloat16),
        jax.ShapeDtypeStruct((feats, nodes), jnp.bfloat16),
        jax.ShapeDtypeStruct((2 * HALO, feats), jnp.bfloat16),
        jax.ShapeDtypeStruct((nodes, feats), jnp.float32),
        jax.ShapeDtypeStruct((doms, 2 * feats // doms + 8, feats), jnp.float32),
    )
    kept = (halo_counts, low_rows, high_rows, degree, features, w_self, w_neigh, bias, cotangent)
    return pl.pallas_call(
        forward_kernel,
        grid=(steps,),
        out_shape=out_shape,
        in_specs=[
            pl.BlockSpec((nodes, wide), lambda k: (0, k)),
            pl.BlockSpec((wide, feats), lambda k: (k, 0)),
        ]
        + [whole(array) for array in kept],
        out_specs=tuple(whole(array) for array in out_shape),
        scratch_shapes=[
            pltpu.VMEM((nodes, feats), jnp.float32),
            pltpu.VMEM((feats, feats), jnp.float32),
            pltpu.VMEM((feats, feats), jnp.float32),
        ],
        compiler_params=pltpu.CompilerParams(vmem_limit_bytes=60 << 20),
        name="forward_layer",
    )(counts, gathered, *kept)


def reduce_kernel(
    counts_ref, grad_ref, weights_ref, halo_ref, dx_ref, out_ref, sums_ref, load, part, mid, fin, half_sum, mid2, fin2, sems_load, s_out, s_mid, s_fin, t_out, t_mid, t_fin, weights_in, w_out, w_in, halo_in, own, h_out, h_in, dx_in, mine_in, s_own
):
    side = 4
    nodes = grad_ref.shape[1]
    feats = grad_ref.shape[0] // 2
    span = nodes // 2
    dom = lax.axis_index("dom")
    blk = lax.axis_index("blk")
    x, y = blk // side, lax.rem(blk, side)

    def at(dx, dy):
        return lax.rem(x + dx, side) * side + lax.rem(y + dy, side)

    def device(half, first, second):
        dx, dy = (first, second) if half == 0 else (second, first)
        return (dom, at(dx, dy))

    barrier = pltpu.get_barrier_semaphore()
    for dx, dy in ((1, 0), (3, 0), (0, 1), (0, 3)):
        pl.semaphore_signal(barrier, inc=1, device_id=(dom, at(dx, dy)), device_id_type=MESH)
    doms = weights_ref.shape[0]
    for k in range(1, doms):
        pl.semaphore_signal(barrier, inc=1, device_id=(lax.rem(dom + k, doms), blk), device_id_type=MESH)

    order = [(2, 2), (2, 1), (1, 2), (2, 3), (3, 2), (2, 0), (0, 2), (1, 1), (3, 3), (1, 3), (3, 1)]
    order += [(1, 0), (0, 1), (3, 0), (0, 3), (0, 0)]
    depth = load.shape[0]

    def fetch(i):
        dx, dy = order[i]
        columns = pl.ds(pl.multiple_of(at(dx, dy) * nodes, nodes), nodes)
        return pltpu.make_async_copy(counts_ref.at[:, columns], load.at[i % depth], sems_load.at[i % depth])

    for i in range(depth - 1):
        fetch(i).start()
    own_dx = pltpu.make_async_copy(dx_ref, dx_in, s_own.at[0])
    own_dx.start()
    own_weights = pltpu.make_async_copy(weights_ref.at[dom], mine_in, s_own.at[1])
    own_weights.start()
    pl.semaphore_wait(barrier, 4 + doms - 1)

    def to_dom(k):
        other = lax.rem(dom + k, doms)
        return pltpu.make_async_remote_copy(
            src_ref=weights_ref.at[other],
            dst_ref=weights_in.at[k],
            send_sem=w_out.at[k],
            recv_sem=w_in.at[k],
            device_id=(other, blk),
            device_id_type=MESH,
        )

    halo = halo_in.shape[1]

    def to_side(side_index):
        return pltpu.make_async_remote_copy(
            src_ref=halo_ref.at[pl.ds(side_index * halo, halo)],
            dst_ref=halo_in.at[side_index],
            send_sem=h_out.at[side_index],
            recv_sem=h_in.at[side_index],
            device_id=(lax.rem(dom + (doms - 1 if side_index == 0 else 1), doms), blk),
            device_id_type=MESH,
        )

    for k in range(1, doms):
        to_dom(k).start()
    to_side(0).start()
    to_side(1).start()

    def remote(src, dst, half, first, second, send_sem, recv_sem):
        return pltpu.make_async_remote_copy(
            src_ref=src,
            dst_ref=dst,
            send_sem=send_sem,
            recv_sem=recv_sem,
            device_id=device(half, first, second),
            device_id_type=MESH,
        )

    def along(unit):
        return unit % 2 == 0

    def to_mid(half, unit):
        return remote(
            part.at[half, 2, unit], mid.at[half, unit], half, 1 if along(unit) else 3, 0,
            s_out.at[half, 0, unit], s_mid.at[half, unit],
        )

    def to_fin(half, first, unit):
        way = 0 if first == 1 else 1
        return remote(
            part.at[half, first, unit], fin.at[half, way, unit], half, first, 0,
            s_out.at[half, 1 + way, unit], s_fin.at[half, way, unit],
        )

    def relays(first, unit):
        return along(unit) == (first == 1)

    tile = 256
    waiting = []
    for i, (dx, dy) in enumerate(order):
        if i + depth - 1 < len(order):
            fetch(i + depth - 1).start()
        fetch(i).wait()

        def columns(n, carry, slot=i % depth, dx=dx, dy=dy):
            cut = pl.ds(pl.multiple_of(n * tile, tile), tile)
            value = jnp.dot(grad_ref[...], load[slot, :, cut], preferred_element_type=jnp.float32)
            part[0, dx, dy, :, cut] = value[:feats].astype(jnp.bfloat16)
            part[1, dy, dx, :, cut] = value[feats:].astype(jnp.bfloat16)
            return carry

        lax.fori_loop(0, nodes // tile, columns, 0)
        for half, first, unit in ((0, dx, dy), (1, dy, dx)):
            if first == 2:
                to_mid(half, unit).start()
            elif first != 0:
                if relays(first, unit):
                    waiting.append((half, first, unit))
                else:
                    to_fin(half, first, unit).start()
    waiting.sort(key=lambda item: (2, 1, 3, 0).index(item[2]))
    for half, first, unit in waiting:
        to_mid(half, unit).wait_recv()
        mine = part[half, first, unit].astype(jnp.float32)
        part[half, first, unit] = (mine + mid[half, unit].astype(jnp.float32)).astype(jnp.bfloat16)
        to_fin(half, first, unit).start()

    def cut(piece):
        return pl.ds(piece * span, span)

    def to_mid2(half, piece):
        return remote(
            half_sum.at[half, 1, :, cut(piece)], mid2.at[half, piece], half, 0, 1 if piece == 0 else 3,
            t_out.at[half, 0, piece], t_mid.at[half, piece],
        )

    def to_fin2(half, second, piece):
        way = 0 if second == 1 else 1
        return remote(
            half_sum.at[half, 0 if second == 1 else 2, :, cut(piece)], fin2.at[half, way, piece], half, 0, second,
            t_out.at[half, 1 + way, piece], t_fin.at[half, way, piece],
        )

    def summed(half, unit):
        to_fin(half, 1, unit).wait_recv()
        to_fin(half, 3, unit).wait_recv()
        total = part[half, 0, unit].astype(jnp.float32) + fin[half, 0, unit].astype(jnp.float32)
        return total + fin[half, 1, unit].astype(jnp.float32)

    for half in range(2):
        half_sum[half, 1] = summed(half, 2).astype(jnp.bfloat16)
        to_mid2(half, 0).start()
        to_mid2(half, 1).start()
    for second in (1, 3):
        direct, relayed = (1, 0) if second == 1 else (0, 1)
        for half in range(2):
            half_sum[half, second - 1] = summed(half, second).astype(jnp.bfloat16)
            to_fin2(half, second, direct).start()
    for second in (1, 3):
        direct, relayed = (1, 0) if second == 1 else (0, 1)
        for half in range(2):
            to_mid2(half, relayed).wait_recv()
            mine = half_sum[half, second - 1, :, cut(relayed)].astype(jnp.float32)
            both = mine + mid2[half, relayed].astype(jnp.float32)
            half_sum[half, second - 1, :, cut(relayed)] = both.astype(jnp.bfloat16)
            to_fin2(half, second, relayed).start()
    for half in range(2):
        own[half * feats : (half + 1) * feats, :] = summed(half, 0)
    to_side(0).wait_recv()
    to_side(1).wait_recv()
    own_dx.wait()
    for half in range(2):
        rows = slice(half * feats, (half + 1) * feats)
        for piece in range(2):
            to_fin2(half, 1, piece).wait_recv()
            to_fin2(half, 3, piece).wait_recv()
            total = own[rows, piece * span : (piece + 1) * span] + fin2[half, 0, piece].astype(jnp.float32)
            total = (total + fin2[half, 1, piece].astype(jnp.float32)).T
            near = slice(piece * span, (piece + 1) * span)
            out_ref[near, rows] = dx_in[near, rows] + total
            edge = slice(0, halo) if piece == 0 else slice(nodes - halo, nodes)
            out_ref[edge, rows] += halo_in[1 - piece, :, rows].astype(jnp.float32)
    to_side(0).wait_send()
    to_side(1).wait_send()
    own_weights.wait()
    sums = mine_in[...]
    for k in range(1, doms):
        to_dom(k).wait_recv()
        sums = sums + weights_in[k]
    sums_ref[...] = sums
    for k in range(1, doms):
        to_dom(k).wait_send()
    for half in range(2):
        for unit in range(side):
            to_mid(half, unit).wait_send()
            to_fin(half, 1, unit).wait_send()
            to_fin(half, 3, unit).wait_send()
        for piece in range(2):
            to_mid2(half, piece).wait_send()
            to_fin2(half, 1, piece).wait_send()
            to_fin2(half, 3, piece).wait_send()


def reduce_sources(counts, grad, weights, halo, dx):
    feats, nodes = grad.shape
    half = feats // 2
    kind = jnp.bfloat16
    dma = pltpu.SemaphoreType.DMA
    vmem = pl.BlockSpec(memory_space=pltpu.VMEM)
    anywhere = pl.BlockSpec(memory_space=pl.ANY)
    return pl.pallas_call(
        reduce_kernel,
        out_shape=(
            jax.ShapeDtypeStruct((nodes, feats), jnp.float32),
            jax.ShapeDtypeStruct(weights.shape[1:], jnp.float32),
        ),
        in_specs=[anywhere, vmem, anywhere, anywhere, anywhere],
        out_specs=(vmem, vmem),
        scratch_shapes=[
            pltpu.VMEM((3, nodes, nodes), kind),
            pltpu.VMEM((2, 4, 4, half, nodes), kind),
            pltpu.VMEM((2, 4, half, nodes), kind),
            pltpu.VMEM((2, 2, 4, half, nodes), kind),
            pltpu.VMEM((2, 3, half, nodes), kind),
            pltpu.VMEM((2, 2, half, nodes // 2), kind),
            pltpu.VMEM((2, 2, 2, half, nodes // 2), kind),
            dma((3,)),
            dma((2, 3, 4)),
            dma((2, 4)),
            dma((2, 2, 4)),
            dma((2, 3, 2)),
            dma((2, 2)),
            dma((2, 2, 2)),
            pltpu.VMEM(weights.shape, jnp.float32),
            dma((weights.shape[0],)),
            dma((weights.shape[0],)),
            pltpu.VMEM((2, halo.shape[0] // 2, feats), kind),
            pltpu.VMEM((feats, nodes), jnp.float32),
            dma((2,)),
            dma((2,)),
            pltpu.VMEM((nodes, feats), jnp.float32),
            pltpu.VMEM(weights.shape[1:], jnp.float32),
            dma((2,)),
        ],
        compiler_params=pltpu.CompilerParams(
            collective_id=3, has_side_effects=True, vmem_limit_bytes=60 << 20
        ),
        name="reduce_sources",
    )(counts, grad, weights, halo, dx)


def shifted(block, axis, distance):
    devices = range(lax.axis_size(axis))
    route = [((i - distance) % len(devices), i) for i in devices]
    return lax.ppermute(block, axis, route)


def dot(a, b, dims=(((1,), (0,)), ((), ()))):
    return lax.dot_general(a, b, dims, preferred_element_type=jnp.float32)


def per_device(
    node_owner,
    node_qrow,
    node_rem,
    quotient,
    remainder,
    edge_src,
    edge_dst,
    block_count,
    w_self,
    w_neigh,
    bias,
    cotangent,
):
    nodes_dev = node_qrow.shape[0]
    feature_dim = quotient.shape[1]
    devices = lax.axis_size("dom") * lax.axis_size("blk")
    part_nodes = nodes_dev * lax.axis_size("blk")
    doms = lax.axis_size("dom")
    features, quot_rows, remain_rows, asked_row, slot_row, fast, slow, flags, first, last = fetch_rows(
        node_owner.reshape(1, -1),
        node_qrow[None],
        node_rem[None],
        quotient,
        remainder,
        edge_src,
        edge_dst,
        block_count,
        devices,
        part_nodes,
    )
    part_gathered = lax.all_gather(features, "blk", axis=0, tiled=True)
    low_rows = shifted(last, "dom", 1)
    high_rows = shifted(first, "dom", -1)

    counts, halo_counts, degree = build_counts(fast, slow, flags, block_count, part_nodes)
    out, grad_t, halo_grads, dx_self, weights = forward(
        counts, part_gathered, halo_counts, low_rows, high_rows, degree, features, w_self, w_neigh, bias[None], cotangent, doms
    )
    grad_x, weight_sums = reduce_sources(counts, grad_t, weights, halo_grads, dx_self)
    nodes_total = nodes_dev * devices
    weight_scale = 1.0 / math.sqrt(nodes_total)
    remain_scale = math.sqrt(remainder.shape[0] / nodes_total)
    d_quotient, d_remainder, d_weights, d_bias = spread_grads(
        grad_x,
        quot_rows,
        remain_rows,
        slot_row,
        node_rem[None],
        asked_row,
        weight_sums,
        quotient.shape[0],
        remainder.shape[0],
        lax.axis_size("blk"),
        remain_scale,
        weight_scale,
    )
    d_self, d_neigh = d_weights[:feature_dim], d_weights[feature_dim:]
    d_bias = d_bias[:, : feature_dim // doms].reshape(-1)
    return (out, d_quotient, d_remainder, d_self, d_neigh, d_bias)


def solution(mesh):
    both = P(AXES)
    rows = P(AXES, None)
    return jax.shard_map(
        per_device,
        mesh=mesh,
        in_specs=(rows, both, both, rows, P(), rows, rows, both, P(), P(), P(), rows),
        out_specs=(rows, rows, P(), P(), P(), P()),
        check_vma=False,
    )
```
